32 devices in a mesh: rep: 4 (over z), ep: 8 (over y, x, core).
Axes of the slice: x: 2, y: 2, z: 4, core: 2. Of those that a mesh axis runs over, the one named last changes fastest.
Arguments:
- tokens: bfloat16 [32768, 1024], P(('rep', 'ep')), may hold values from -6 to 6
- cotangent: bfloat16 [32768, 1024], P(('rep', 'ep')), may hold values from -6 to 6
- lengths: int32 [32], P(('rep', 'ep')), may hold values from 64 to 1024, as said below
- expert_ids: int32 [32768, 1], P(('rep', 'ep')), may hold values from 0 to 7; in each aligned block of 1024 rows (0 to 1023, 1024 to 2047, ...) at most 160 rows name the same one
- norm1_gain: float32 [1024], replicated, may hold values from 0.5 to 1.5
- norm1_bias: float32 [1024], replicated, may hold values from -0.6 to 0.6
- w_query: bfloat16 [1024, 1024], replicated, may hold values from -0.25 to 0.25
- b_query: float32 [1024], replicated, may hold values from -0.6 to 0.6
- w_key: bfloat16 [1024, 1024], replicated, may hold values from -0.25 to 0.25
- w_value: bfloat16 [1024, 1024], replicated, may hold values from -0.1875 to 0.1875
- b_value: float32 [1024], replicated, may hold values from -0.6 to 0.6
- w_out: bfloat16 [1024, 1024], replicated, may hold values from -1 to 1
- b_out: float32 [1024], replicated, may hold values from -0.6 to 0.6
- norm2_gain: float32 [1024], replicated, may hold values from 0.5 to 1.5
- norm2_bias: float32 [1024], replicated, may hold values from -0.6 to 0.6
- w_in: bfloat16 [8, 1024, 4096], P('ep'), may hold values from -0.1875 to 0.1875
- b_in: float32 [8, 4096], P('ep'), may hold values from -0.6 to 0.6
- w_back: bfloat16 [8, 4096, 1024], P('ep'), may hold values from -0.125 to 0.125
- b_back: float32 [8, 1024], P('ep'), may hold values from -0.6 to 0.6
Outputs:
- block_out: bfloat16 [32768, 1024], P(('rep', 'ep'))
- grad_tokens: float32 [32768, 1024], P(('rep', 'ep'))
- grad_norm1_gain: float32 [1024], P(('rep', 'ep'))
- grad_norm1_bias: float32 [1024], P(('rep', 'ep'))
- grad_w_query: float32 [1024, 1024], P(('rep', 'ep'))
- grad_b_query: float32 [1024], P(('rep', 'ep'))
- grad_w_key: float32 [1024, 1024], P(('rep', 'ep'))
- grad_w_value: float32 [1024, 1024], P(('rep', 'ep'))
- grad_b_value: float32 [1024], P(('rep', 'ep'))
- grad_w_out: float32 [1024, 1024], P(('rep', 'ep'))
- grad_b_out: float32 [1024], P(('rep', 'ep'))
- grad_norm2_gain: float32 [1024], P(('rep', 'ep'))
- grad_norm2_bias: float32 [1024], P(('rep', 'ep'))
- grad_w_in: float32 [8, 1024, 4096], P('ep', 'rep')
- grad_b_in: float32 [8, 4096], P('ep', 'rep')
- grad_w_back: float32 [8, 4096, 1024], P('ep', 'rep')
- grad_b_back: float32 [8, 1024], P('ep', 'rep')
The draws below stay inside these ranges and needn't reach their ends.
Inputs may be any that keep to these rules, and one draw needn't show every extreme that they name: `lengths`: one sequence has exactly 1024 valid tokens. `expert_ids`: among the 1024 rows of one device no expert is named more than 160 times, a bound that some block reaches.
All inputs are finite; a program needn't handle non-finite values.
Results may differ from the reference program's by a relative error of at most 0.014.
Values may be sent and summed in bfloat16 or wider, within the bound.
A program may use at most 384 MiB of HBM per device.

```python
import math
import jax
import jax.numpy as jnp
import numpy as np
from jax import lax

D = 1024
HEADS = 16
FF = 4096
SEQ_LEN = 1024
TOK_DEV = 1024
SEQS = 32
TOKENS = 32768
EXPERTS = 8
CAP = 160


def draw_lengths(key, part):
    key_lens, key_pick = jax.random.split(key)
    drawn = jax.random.randint(key_lens, (SEQS,), SEQ_LEN // 16, SEQ_LEN + 1)
    chosen_seq = jax.random.randint(key_pick, (), 0, SEQS)
    return jnp.where(jnp.arange(SEQS) == chosen_seq, SEQ_LEN, drawn).astype(jnp.int32)


def levels(rng, dims, cuts, smallest, high):
    level, own = 1.0, jax.random.fold_in(rng, 6)
    for axis_at, blocks in cuts:
        draws = jnp.exp(jax.random.uniform(jax.random.fold_in(own, axis_at), (blocks,), jnp.float32, smallest / len(cuts), high / len(cuts)))
        level = level * jnp.repeat(draws, dims[axis_at] // blocks).reshape([-1 if axis == axis_at else 1 for axis in range(len(dims))])
    return level


def assign_block(own_key, own, number, rows, number_of, top, bound, skew):
    ranking = jax.random.permutation(own_key, number_of)
    crowded, common = shares(number_of, rows * top, bound, skew, True), shares(number_of, rows * top, bound, skew, False)
    places = jnp.arange(number_of)

    def named(tallies, offset_by):
        used = int((tallies > 0).sum())
        fixed = max(1, used // 4)
        moved = fixed + (places - fixed + offset_by * (used - fixed)) % max(1, number_of - fixed)
        return jnp.zeros((number_of,), jnp.int32).at[ranking[jnp.where(places < fixed, places, moved)]].set(jnp.asarray(tallies, jnp.int32))

    tallies = jnp.where(number % 4 == 0, named(crowded, number // 4), named(common, number - number // 4 - 1))
    mixed = jax.random.permutation(jax.random.fold_in(own, 3), number_of)
    giver, taker = mixed[0:number_of // 2 * 2:2], mixed[1:number_of // 2 * 2:2]
    margin = jnp.minimum(tallies[giver] - 1, bound - tallies[taker]) // 2
    margin = jnp.where((giver == ranking[0]) | (taker == ranking[0]) | (tallies[taker] == 0), 0, jnp.maximum(margin, 0))
    moved = jax.random.randint(jax.random.fold_in(own, 4), (number_of // 2,), 0, 1 << 20) % (margin + 1)
    tallies = tallies.at[giver].add(-moved).at[taker].add(moved)
    members = jnp.searchsorted(jnp.cumsum(tallies), jnp.arange(rows * top), side="right").astype(jnp.int32)
    grid = members.reshape(top, rows).T
    grid = grid[jax.random.permutation(jax.random.fold_in(own, 1), rows)]
    offset_by = jax.random.randint(jax.random.fold_in(own, 2), (rows, 1), 0, top)
    return jnp.take_along_axis(grid, (jnp.arange(top)[None, :] + offset_by) % top, axis=1)


def shares(count, total, limit, lean, full):
    weights = [(1 << 20) // math.isqrt(grade ** lean) + 1 for grade in range(1, count + 1)]
    largest = limit if full else min(limit, max(-(-total // count), total * weights[0] // sum(weights)))
    least = 1 if total - largest >= count - 1 else 0
    given, spare = [largest] + [least] * (count - 1), total - largest - least * (count - 1)
    while spare > 0:
        candidates = [i for i in range(1, count) if given[i] < largest] or [i for i in range(1, count) if given[i] < limit]
        whole, left = sum([weights[i] for i in candidates]), spare
        for i in candidates:
            more = min(limit - given[i], max(1, left * weights[i] // whole), spare)
            given[i] = given[i] + more
            spare = spare - more
    return np.array(given)


def gaussian(own_key, extent, spread, bound, pieces=(), held_as=jnp.bfloat16):
    gain = levels(own_key, extent, pieces, -0.22, 0.18) if pieces else 1.0
    array = jax.random.normal(own_key, extent, jnp.float32) * spread * gain
    return jnp.minimum(jnp.maximum(array, -bound), bound).astype(held_as)


def setup_inputs(seed: int = 0) -> dict:
    key_of = jax.random.split(jax.random.key(seed), 20)
    tokens = gaussian(key_of[0], (TOKENS, D), 1.0, 6.0, ((0, 32),))
    cotangent = gaussian(key_of[1], (TOKENS, D), 1.0, 6.0, ((0, 32),))
    lengths = draw_lengths(jax.random.fold_in(key_of[19], 71), 0)
    expert_ids_keys = jax.random.split(jax.random.fold_in(key_of[3], 1), TOKENS // TOK_DEV)
    expert_ids_turns = jax.random.permutation(jax.random.fold_in(key_of[3], 3), TOKENS // TOK_DEV)
    expert_ids = jax.vmap(lambda own, number: assign_block(jax.random.fold_in(key_of[3], 2), own, number, TOK_DEV, EXPERTS, 1, CAP, 1))(expert_ids_keys, expert_ids_turns).reshape((TOKENS, 1))
    norm1_gain = jnp.clip(1.0 + 0.1 * jax.random.normal(key_of[4], (D,), jnp.float32), 0.5, 1.5)
    norm1_bias = gaussian(key_of[5], (D,), 0.1, 0.6, (), jnp.float32)
    w_query = gaussian(key_of[6], (D, D), (D // 2) ** -0.5, 0.25)
    b_query = gaussian(key_of[7], (D,), 0.1, 0.6, (), jnp.float32)
    w_key = gaussian(key_of[8], (D, D), (D // 2) ** -0.5, 0.25)
    w_value = gaussian(key_of[9], (D, D), D ** -0.5, 0.1875)
    b_value = gaussian(key_of[10], (D,), 0.1, 0.6, (), jnp.float32)
    w_out = gaussian(key_of[11], (D, D), (D * 32 // SEQ_LEN) ** -0.5, 1.0)
    b_out = gaussian(key_of[12], (D,), 0.1, 0.6, (), jnp.float32)
    norm2_gain = jnp.clip(1.0 + 0.1 * jax.random.normal(key_of[13], (D,), jnp.float32), 0.5, 1.5)
    norm2_bias = gaussian(key_of[14], (D,), 0.1, 0.6, (), jnp.float32)
    w_in = gaussian(key_of[15], (EXPERTS, D, FF), D ** -0.5, 0.1875, ((0, 8),))
    b_in = gaussian(key_of[16], (EXPERTS, FF), 0.1, 0.6, ((0, 8),), jnp.float32)
    w_back = gaussian(key_of[17], (EXPERTS, FF, D), (FF // 2) ** -0.5, 0.125, ((0, 8),))
    b_back = gaussian(key_of[18], (EXPERTS, D), 0.1, 0.6, ((0, 8),), jnp.float32)
    return dict(tokens=tokens, cotangent=cotangent, lengths=lengths, expert_ids=expert_ids, norm1_gain=norm1_gain, norm1_bias=norm1_bias, w_query=w_query, b_query=b_query, w_key=w_key, w_value=w_value, b_value=b_value, w_out=w_out, b_out=b_out, norm2_gain=norm2_gain, norm2_bias=norm2_bias, w_in=w_in, b_in=b_in, w_back=w_back, b_back=b_back)


@jax.custom_vjp
def low(v):
    return lax.optimization_barrier(v.astype(jnp.bfloat16)).astype(jnp.float32)

@jax.custom_vjp
def low_back(v):
    return v

def low_keep(v):
    return (low(v), None)

def low_pass(kept, grad):
    return (grad,)

def back_keep(v):
    return (v, None)

def back_low(kept, grad):
    return (low(grad),)
low.defvjp(low_keep, low_pass)
low_back.defvjp(back_keep, back_low)

def project(left, right):
    return jnp.dot(left, right, precision=lax.Precision.HIGHEST, preferred_element_type=jnp.float32)

def normalize(hidden, norm_gain, norm_bias):
    row_mean = lax.optimization_barrier(jnp.mean(hidden, -1, keepdims=True))
    centred = hidden - row_mean
    inv_std = lax.rsqrt(lax.optimization_barrier(jnp.mean(centred * centred, -1, keepdims=True)) + 1e-05)
    return centred * inv_std * norm_gain + norm_bias

def attend(packed_in):
    queries, key_all, value_all, valid_length = packed_in
    seq_rows = queries.shape[0]
    raw_scores = jnp.einsum('qhd,khd->hqk', queries, key_all, precision=lax.Precision.HIGHEST) * queries.shape[2] ** (-0.5)
    raw_scores = low_back(raw_scores)
    positions = jnp.arange(seq_rows, dtype=jnp.int32)
    allowed = (positions[None, :] <= positions[:, None]) & (positions[None, :] < valid_length.astype(jnp.int32))
    masked = jnp.where(allowed[None], raw_scores, -1e+30)
    row_top = lax.optimization_barrier(jnp.max(masked, -1, keepdims=True))
    exponent = jnp.exp(masked - row_top)
    probability = low(exponent / lax.optimization_barrier(jnp.sum(exponent, -1, keepdims=True)))
    return jnp.einsum('hqk,khd->qhd', probability, value_all, precision=lax.Precision.HIGHEST).reshape(seq_rows, -1)

def expert(packed_in):
    buffer, first_w, bias_in, second_w, bias_out = packed_in
    pre_act = low_back(project(buffer, first_w) + bias_in)
    active = low(jax.nn.gelu(pre_act, approximate=True))
    return low_back(low(project(active, second_w) + bias_out))

def reference(tokens, cotangent, lengths, expert_ids, norm1_gain, norm1_bias, w_query, b_query, w_key, w_value, b_value, w_out, b_out, norm2_gain, norm2_bias, w_in, b_in, w_back, b_back):
    chosen = expert_ids[:, 0].astype(jnp.int32).reshape(SEQS, TOK_DEV)
    onehot = (chosen[:, :, None] == jnp.arange(EXPERTS, dtype=jnp.int32)[None, None, :]).astype(jnp.int32)
    before = (jnp.cumsum(onehot, 1, dtype=jnp.int32) - onehot).astype(jnp.int32)
    slot_index = lax.optimization_barrier(jnp.sum(before * onehot, -1, dtype=jnp.int32)).astype(jnp.int32)
    place_row = (jnp.arange(SEQS, dtype=jnp.int32)[:, None] * CAP + slot_index).reshape(-1).astype(jnp.int32)
    chosen_flat = chosen.reshape(-1).astype(jnp.int32)
    lengths_int = lengths.astype(jnp.int32)

    def forward(resid, gain_one, bias_one, wq_f, bq_f, wk_f, wv_f, bv_f, wo_f, bo_f, gain_two, bias_two, first_all, bin_all, second_all, bback_all):
        normed_a = low(normalize(resid, gain_one, bias_one))
        queries = low_back(low(project(normed_a, wq_f) + bq_f)).reshape(SEQS, TOK_DEV, HEADS, -1)
        key_all = low_back(low(project(normed_a, wk_f))).reshape(SEQS, TOK_DEV, HEADS, -1)
        value_all = low_back(low(project(normed_a, wv_f) + bv_f)).reshape(SEQS, TOK_DEV, HEADS, -1)
        mixed_heads = lax.map(jax.checkpoint(attend), (queries, key_all, value_all, lengths_int))
        mixed_heads = low_back(low(mixed_heads.reshape(TOKENS, -1)))
        attn_out = low_back(project(mixed_heads, wo_f) + bo_f)
        hidden_one = resid + attn_out
        normed_b = low_back(low(normalize(hidden_one, gain_two, bias_two)))
        buffer = jnp.zeros((EXPERTS, SEQS * CAP, normed_b.shape[1]), normed_b.dtype).at[chosen_flat, place_row].set(normed_b)
        outputs = lax.map(jax.checkpoint(expert), (buffer, first_all, bin_all, second_all, bback_all))
        return hidden_one + outputs[chosen_flat, place_row]
    floats = tuple((item.astype(jnp.float32) for item in (tokens, norm1_gain, norm1_bias, w_query, b_query, w_key, w_value, b_value, w_out, b_out, norm2_gain, norm2_bias, w_in, b_in, w_back, b_back)))
    result, pullback = jax.vjp(forward, *floats)
    grads = pullback(cotangent.astype(jnp.float32))
    return (result.astype(jnp.bfloat16), grads[0], grads[1], grads[2], grads[3], grads[4], grads[5], grads[6], grads[7], grads[8], grads[9], grads[10], grads[11], grads[12], grads[13], grads[14], grads[15])
```

```python
import functools

import jax
import jax.numpy as jnp
from jax import lax
from jax.experimental import pallas as pl
from jax.experimental.pallas import tpu as pltpu
from jax.sharding import PartitionSpec as P

HEADS = 16
BF = jnp.bfloat16
F32 = jnp.float32
LOG2E = 1.4426950408889634
NEG = -1e30


def dot(left, right):
    return jnp.dot(left, right, preferred_element_type=F32)


def dot_nt(left, right):
    return lax.dot_general(left, right, (((1,), (1,)), ((), ())), preferred_element_type=F32)


def dot_tn(left, right):
    return lax.dot_general(left, right, (((0,), (0,)), ((), ())), preferred_element_type=F32)


def attn_fwd_kernel(len_ref, q_ref, k_ref, v_ref, o_ref, lse_ref, ot_ref, *, blk):
    n, lanes = q_ref.shape
    half = lanes//2
    length = len_ref[0]
    k = k_ref[...].astype(F32)
    lane = lax.broadcasted_iota(jnp.int32,(n,lanes),1)
    row = lax.broadcasted_iota(jnp.int32,(n,lanes),0)
    bias = jnp.where(row<length, 0.0, NEG)
    k_a = jnp.where(lane<half, k, jnp.where(lane==half, bias, 0.0)).astype(BF)
    k_b = jnp.where(lane>=half, k, jnp.where(lane==0, bias, 0.0)).astype(BF)
    qt = q_ref[...].T
    vt = v_ref[...].T
    trow = lax.broadcasted_iota(jnp.int32,(lanes,n),0)
    qt32 = qt.astype(F32)
    qt_a = jnp.where(trow==half, 1.0, qt32).astype(BF)
    qt_b = jnp.where(trow==0, 1.0, qt32).astype(BF)
    tri = lax.broadcasted_iota(jnp.int32,(blk,blk),0) <= lax.broadcasted_iota(jnp.int32,(blk,blk),1)
    ones = jnp.ones((16,n),BF)
    for h,(kk,qq) in enumerate(((k_a,qt_a),(k_b,qt_b))):
        v_ext = jnp.concatenate([vt[h*half:(h+1)*half], ones],0)
        for i in range(n//blk):
            cols = slice(i*blk,(i+1)*blk)
            qb = qq[:,cols]
            diag = jnp.where(tri, dot(kk[cols],qb), NEG)
            if i:
                past = dot(kk[:i*blk],qb)
                top = jnp.maximum(jnp.max(past,0,keepdims=True),jnp.max(diag,0,keepdims=True))
                p = jnp.concatenate([jnp.exp2((past-top)*LOG2E).astype(BF),jnp.exp2((diag-top)*LOG2E).astype(BF)],0)
            else:
                top = jnp.max(diag,0,keepdims=True)
                p = jnp.exp2((diag-top)*LOG2E).astype(BF)
            r = dot(v_ext[:,:(i+1)*blk],p)
            total = r[half:half+1]
            ot_ref[h*half:(h+1)*half,cols] = r[:half]/total
            lse_ref[0,h:h+1,cols] = top + jnp.log(total)
    o_ref[...] = ot_ref[...].T.astype(BF)

def attn_fwd(q,k,v,length,blk=256):
    n,d=q.shape
    pairs=d//128
    spec=pl.BlockSpec((n,128),lambda h:(0,h))
    return pl.pallas_call(functools.partial(attn_fwd_kernel,blk=blk),
        grid=(pairs,),
        in_specs=[pl.BlockSpec(memory_space=pltpu.SMEM),spec,spec,spec],
        out_specs=(spec,pl.BlockSpec((1,2,n),lambda h:(h,0,0))),
        out_shape=(jax.ShapeDtypeStruct((n,d),BF),jax.ShapeDtypeStruct((pairs,2,n),F32)),
        scratch_shapes=[pltpu.VMEM((128,n),F32)],
        compiler_params=pltpu.CompilerParams(vmem_limit_bytes=50<<20),
        cost_estimate=pl.CostEstimate(flops=2*2*n*n*d,bytes_accessed=4*n*d*2,transcendentals=n*n*8),
        name="attn_fwd",
    )(length,q,k,v)

def split3(x):
    a=x.astype(BF).astype(F32); r=x-a
    b=r.astype(BF).astype(F32); c=r-b
    return a,b,c

def attn_bwd_kernel(len_ref, q_ref, k_ref, v_ref, o_ref, do_ref, lse_ref, dq_ref, dk_ref, dv_ref, dqt_ref, dk_acc, dv_acc, *, blk):
    n, lanes = q_ref.shape
    half = lanes//2
    length = len_ref[0]
    lane = lax.broadcasted_iota(jnp.int32,(n,lanes),1)
    row = lax.broadcasted_iota(jnp.int32,(n,lanes),0)
    trow = lax.broadcasted_iota(jnp.int32,(lanes,n),0)
    bias = jnp.where(row<length, 0.0, NEG)
    q = q_ref[...].astype(F32); k = k_ref[...].astype(F32); v=v_ref[...].astype(F32); do=do_ref[...].astype(F32)
    kt = k_ref[...].T
    qt = q_ref[...].T.astype(F32)
    dot_t = do_ref[...].T.astype(F32)
    ot = o_ref[...].T.astype(F32)
    prod = dot_t*ot
    heads=[]
    for h in range(2):
        own = (lane<half) if h==0 else (lane>=half)
        base = half if h==0 else 0
        delta = jnp.sum(prod[h*half:(h+1)*half],0,keepdims=True)
        lse = lse_ref[0,h:h+1,:]
        l1,l2,l3 = split3(-lse)
        d1,d2,d3 = split3(-delta)
        one = jnp.where((lane>=base+1)&(lane<=base+3),1.0,0.0)
        k_x = jnp.where(own,k,jnp.where(lane==base,bias,one)).astype(BF)
        v_x = jnp.where(own,v,one).astype(BF)
        q_x = jnp.where(trow==base,1.0,jnp.where(trow==base+1,l1,jnp.where(trow==base+2,l2,jnp.where(trow==base+3,l3,qt)))).astype(BF)
        d_x = jnp.where(trow==base+1,d1,jnp.where(trow==base+2,d2,jnp.where(trow==base+3,d3,dot_t))).astype(BF)
        q_own = jnp.where(own,q,0.0).astype(BF)
        do_own = jnp.where(own,do,0.0).astype(BF)
        heads.append((k_x,v_x,q_x,d_x,q_own,do_own))
    tri = lax.broadcasted_iota(jnp.int32,(blk,blk),0) <= lax.broadcasted_iota(jnp.int32,(blk,blk),1)
    steps=n//blk
    for i in reversed(range(steps)):
        cols = slice(i*blk,(i+1)*blk)
        ps=[];dss=[]
        for h in range(2):
            k_x,v_x,q_x,d_x,q_own,do_own=heads[h]
            qb=q_x[:,cols]; db=d_x[:,cols]
            p_d = jnp.exp2(jnp.where(tri,dot(k_x[cols],qb),NEG)*LOG2E)
            ds_d = p_d*dot(v_x[cols],db)
            if i:
                p_p = jnp.exp2(dot(k_x[:i*blk],qb)*LOG2E)
                ds_p = p_p*dot(v_x[:i*blk],db)
                p=jnp.concatenate([p_p.astype(BF),p_d.astype(BF)],0)
                ds=jnp.concatenate([ds_p.astype(BF),ds_d.astype(BF)],0)
            else:
                p=p_d.astype(BF); ds=ds_d.astype(BF)
            dqt_ref[h*half:(h+1)*half,cols]=dot(kt[h*half:(h+1)*half,:(i+1)*blk],ds)
            ps.append(p);dss.append(ds)
        dv_new = dot(ps[0],heads[0][5][cols])+dot(ps[1],heads[1][5][cols])
        dk_new = dot(dss[0],heads[0][4][cols])+dot(dss[1],heads[1][4][cols])
        if i==steps-1:
            dv_acc[...]=dv_new; dk_acc[...]=dk_new
        else:
            dv_acc[:(i+1)*blk]+=dv_new; dk_acc[:(i+1)*blk]+=dk_new
    scale=half**-0.5
    dq_ref[...]=(dqt_ref[...]*scale).T.astype(BF)
    dk_ref[...]=dk_acc[...].astype(BF)
    dv_ref[...]=dv_acc[...].astype(BF)

def attn_bwd(q,k,v,o,do,lse,length,blk=256):
    n,d=q.shape
    pairs=d//128
    spec=pl.BlockSpec((n,128),lambda h:(0,h))
    return pl.pallas_call(functools.partial(attn_bwd_kernel,blk=blk),
        grid=(pairs,),
        in_specs=[pl.BlockSpec(memory_space=pltpu.SMEM),spec,spec,spec,spec,spec,pl.BlockSpec((1,2,n),lambda h:(h,0,0))],
        out_specs=(spec,spec,spec),
        out_shape=tuple(jax.ShapeDtypeStruct((n,d),BF) for _ in range(3)),
        scratch_shapes=[pltpu.VMEM((128,n),F32),pltpu.VMEM((n,128),F32),pltpu.VMEM((n,128),F32)],
        compiler_params=pltpu.CompilerParams(vmem_limit_bytes=50<<20),
        cost_estimate=pl.CostEstimate(flops=5*2*n*n*d,bytes_accessed=8*n*d*2,transcendentals=n*n*8),
        name="attn_bwd",
    )(length,q,k,v,o,do,lse)


C0=0.7978845608028654; C1=C0*0.044715

def act_both(z):
    z2=z*z
    a=C1*z2+C0
    t=jnp.tanh(z*a)
    h=0.5*t+0.5
    u=z*h
    q=6.0*a-4.0*C0
    return u, h+u*(1.0-h)*q

def expert_kernel(b_ref,gy_ref,w1_ref,b1_ref,w2_ref,u_ref,dz_ref,g1_ref,g2_ref,gb1_ref,bt_ref,gyt_ref,*,rblk):
    rows=b_ref.shape[0]
    @pl.when(pl.program_id(0)==0)
    def _():
        bt_ref[...]=b_ref[...].T
        gyt_ref[...]=gy_ref[...].T
    w1=w1_ref[...]; w2=w2_ref[...]; bias=b1_ref[...]
    total=None
    for s in range(0,rows,rblk):
        rs=slice(s,s+rblk)
        z=dot(b_ref[rs,:],w1)+bias
        du=dot_nt(gy_ref[rs,:],w2)
        u,slope=act_both(z)
        u_ref[rs,:]=u.astype(BF)
        dz=du*slope
        dz_ref[rs,:]=dz.astype(BF)
        part=jnp.sum(dz,0,keepdims=True)
        total=part if total is None else total+part
    gb1_ref[...]=total
    g1_ref[...]=dot(bt_ref[...],dz_ref[...]).astype(BF)
    g2_ref[...]=dot(gyt_ref[...],u_ref[...]).astype(BF).T

def expert_grads(b,gy,w1,b1,w2,tiles,tile,rblk=256):
    rows,d=b.shape
    count,index=tiles
    const=pl.BlockSpec((rows,d),lambda j:(0,0),pipeline_mode=pl.Buffered(1))
    ff=count*tile
    return pl.pallas_call(functools.partial(expert_kernel,rblk=rblk),
        grid=(count,),
        in_specs=[const,const,pl.BlockSpec((d,tile),lambda j:(0,index(j))),pl.BlockSpec((1,tile),lambda j:(0,index(j))),pl.BlockSpec((tile,d),lambda j:(index(j),0))],
        out_specs=(pl.BlockSpec((rows,tile),lambda j:(0,j)),pl.BlockSpec((rows,tile),lambda j:(0,j)),pl.BlockSpec((d,tile),lambda j:(0,j)),pl.BlockSpec((tile,d),lambda j:(j,0)),pl.BlockSpec((1,tile),lambda j:(0,j))),
        out_shape=(jax.ShapeDtypeStruct((rows,ff),BF),jax.ShapeDtypeStruct((rows,ff),BF),jax.ShapeDtypeStruct((d,ff),BF),jax.ShapeDtypeStruct((ff,d),BF),jax.ShapeDtypeStruct((1,ff),F32)),
        scratch_shapes=[pltpu.VMEM((d,rows),BF),pltpu.VMEM((d,rows),BF)],
        compiler_params=pltpu.CompilerParams(vmem_limit_bytes=56<<20),
        cost_estimate=pl.CostEstimate(flops=8*rows*d*ff,bytes_accessed=(4*rows*d+8*d*ff+4*rows*ff),transcendentals=rows*ff),
        name="expert_grads",
    )(b,gy,w1,b1,w2)


def layer_norm(hidden, norm_gain, norm_bias):
    row_mean = jnp.mean(hidden, -1, keepdims=True)
    centred = hidden - row_mean
    inv_std = lax.rsqrt(jnp.mean(centred * centred, -1, keepdims=True) + 1e-05)
    normed = centred * inv_std
    return (normed * norm_gain + norm_bias, normed, inv_std)


def norm_back(upstream, normed, inv_std, norm_gain):
    scaled = upstream * norm_gain
    mean_one = jnp.mean(scaled, -1, keepdims=True)
    mean_two = jnp.mean(scaled * normed, -1, keepdims=True)
    return (
        inv_std * (scaled - mean_one - normed * mean_two),
        jnp.sum(upstream * normed, 0),
        jnp.sum(upstream, 0),
    )


def halve(block, bit, axis_bits):
    axis = axis_bits[bit]
    size = lax.axis_size("ep")
    mine = (lax.axis_index("ep") >> bit) & 1
    keep = lax.dynamic_index_in_dim(block, mine, axis, keepdims=False)
    send = lax.dynamic_index_in_dim(block, 1 - mine, axis, keepdims=False)
    got = lax.ppermute(send, "ep", [(i, i ^ (1 << bit)) for i in range(size)])
    left = {b: (x - 1 if x > axis else x) for b, x in axis_bits.items() if b != bit}
    return (keep.astype(F32) + got.astype(F32)).astype(BF), left


def sum_over_ep(block, bits, order):
    rep, ep, rows, columns = block.shape
    block = block.reshape((rep,) + (2,) * bits + (rows, columns))
    axis_bits = {b: bits - b for b in range(bits)}
    for bit in order:
        block, axis_bits = halve(block, bit, axis_bits)
    return block


def per_device(
    tokens,
    cotangent,
    lengths,
    expert_ids,
    norm1_gain,
    norm1_bias,
    w_query,
    b_query,
    w_key,
    w_value,
    b_value,
    w_out,
    b_out,
    norm2_gain,
    norm2_bias,
    w_in,
    b_in,
    w_back,
    b_back,
):
    row_count, width = tokens.shape
    head_dim = width // HEADS
    ep = lax.axis_size("ep")
    rep = lax.axis_size("rep")
    slots = 5 * row_count // (4 * ep)
    places = ep * slots
    ff = w_in.shape[2]
    w_first = w_in[0]
    w_second = w_back[0]

    chosen = expert_ids[:, 0]
    onehot = (chosen[:, None] == jnp.arange(ep, dtype=jnp.int32)[None, :]).astype(jnp.int32)
    before = jnp.cumsum(onehot, 0, dtype=jnp.int32) - onehot
    target = chosen * slots + jnp.sum(before * onehot, 1, dtype=jnp.int32)
    route = (jnp.arange(places, dtype=jnp.int32)[:, None] == target[None, :]).astype(BF)

    def exchange(rows):
        sent = lax.all_to_all(rows.reshape(ep, slots, width), "ep", 0, 0, tiled=True)
        return sent.reshape(places, width)

    grad_rows = exchange(dot(route, cotangent).astype(BF))

    residual = tokens.astype(F32)
    normed_a, unit_one, inv_one = layer_norm(residual, norm1_gain, norm1_bias)
    act_a = normed_a.astype(BF)
    queries = ((dot(act_a, w_query) + b_query).astype(BF) * head_dim**-0.5).astype(BF)
    keys = dot(act_a, w_key).astype(BF)
    values = (dot(act_a, w_value) + b_value).astype(BF)
    mixed, lse = attn_fwd(queries, keys, values, lengths)
    hidden_one = residual + dot(mixed, w_out) + b_out
    normed_b, unit_two, inv_two = layer_norm(hidden_one, norm2_gain, norm2_bias)
    act_b = normed_b.astype(BF)
    rows_in = exchange(dot(route, act_b).astype(BF))

    per = ff // (rep * 4)
    first = expert_grads(rows_in, grad_rows, w_first, b_in, w_second, (rep, lambda j: j * 4), per)
    rest = expert_grads(
        rows_in, grad_rows, w_first, b_in, w_second, (rep * 3, lambda j: (j // 3) * 4 + 1 + j % 3), per
    )

    def scatter(block, axis):
        return lax.psum_scatter(block, "rep", scatter_dimension=axis, tiled=True)

    g_second_0 = scatter(first[3], 0)
    g_first_0 = scatter(first[2], 0)
    g_second_1 = scatter(rest[3], 0)
    g_first_1 = scatter(rest[2], 0)

    def columns_of(part0, part1):
        lead = part0.shape[0]
        parts = (part0.reshape(lead, rep, 1, per), part1.reshape(lead, rep, 3, per))
        return jnp.concatenate(parts, 2).reshape(lead, ff)

    active = columns_of(first[0], rest[0])
    grad_inner = columns_of(first[1], rest[1])
    g_bias_first = columns_of(first[4], rest[4])
    g_bias_second = jnp.sum(grad_rows.astype(F32), 0)
    grad_home = exchange(dot_nt(grad_inner, w_first).astype(BF))
    returned = exchange((dot(active, w_second) + b_back[0]).astype(BF))

    grad_normed = dot_tn(route, grad_home)
    combined = dot_tn(route, returned)
    block_out = (hidden_one + combined).astype(BF)
    grad_out = cotangent.astype(F32)

    d_hidden_two, g_gain_two, g_bias_two = norm_back(grad_normed, unit_two, inv_two, norm2_gain)
    grad_hidden = grad_out + d_hidden_two
    grad_attn = grad_hidden.astype(BF)
    g_out = dot_tn(mixed, grad_attn)
    g_bias_out = jnp.sum(grad_attn.astype(F32), 0)
    grad_mixed = dot_nt(grad_attn, w_out).astype(BF)
    grad_q, grad_k, grad_v = attn_bwd(queries, keys, values, mixed, grad_mixed, lse, lengths)
    g_query = dot_tn(act_a, grad_q)
    g_key = dot_tn(act_a, grad_k)
    g_value = dot_tn(act_a, grad_v)
    g_bias_query = jnp.sum(grad_q.astype(F32), 0)
    g_bias_value = jnp.sum(grad_v.astype(F32), 0)
    grad_a = dot_nt(grad_q, w_query) + dot_nt(grad_k, w_key) + dot_nt(grad_v, w_value)
    d_resid, g_gain_one, g_bias_one = norm_back(grad_a, unit_one, inv_one, norm1_gain)
    grad_tokens = grad_hidden + d_resid

    own = width // (rep * ep)
    matrices = [g.reshape(rep, ep, own, width).astype(BF) for g in (g_query, g_key, g_value, g_out)]
    vectors = jnp.stack(
        [g_gain_one, g_bias_one, g_bias_query, g_bias_value, g_bias_out, g_gain_two, g_bias_two]
    )
    count = vectors.shape[0]
    vectors = vectors.reshape(count, rep, ep, own).transpose(1, 2, 0, 3).reshape(rep, ep, 1, count * own)
    vectors = jnp.pad(vectors.astype(BF), ((0, 0), (0, 0), (0, 15), (0, width - count * own)))
    packed = jnp.concatenate(matrices + [vectors], 2)
    bits = ep.bit_length() - 1
    order_one = list(range(bits))
    order_two = [0] + list(range(bits - 1, 0, -1))
    half = width // 2
    summed = jnp.concatenate(
        [
            sum_over_ep(packed[..., :half], bits, order_one),
            sum_over_ep(packed[..., half:], bits, order_two),
        ],
        -1,
    )
    own_ff, own_width = ff // rep, width // rep
    bias_rows = jnp.concatenate(
        [
            g_bias_first.reshape(rep, own_ff // width, width),
            jnp.pad(g_bias_second.reshape(rep, 1, own_width), ((0, 0), (0, 0), (0, width - own_width))),
        ],
        1,
    ).astype(BF)
    bias_rows = jnp.pad(bias_rows, ((0, 0), (0, 16 - bias_rows.shape[1]), (0, 0)))
    summed = jnp.concatenate([summed, bias_rows], 1)
    total = scatter(summed.reshape(-1, width), 0).astype(F32)

    dense = [total[i * own : (i + 1) * own] for i in range(4)]
    small = total[4 * own, : count * own].reshape(count, own)
    grad_bias = total[4 * own + 16 :]
    rows_bias = own_ff // width
    out_bias_first = grad_bias[:rows_bias].reshape(1, own_ff)
    out_bias_second = grad_bias[rows_bias : rows_bias + 1, :own_width]
    out_first = columns_of(g_first_0, g_first_1).astype(F32)[None]
    out_second = jnp.concatenate([g_second_0, g_second_1], 0).astype(F32)[None]
    return (
        block_out,
        grad_tokens,
        small[0],
        small[1],
        dense[0],
        small[2],
        dense[1],
        dense[2],
        small[3],
        dense[3],
        small[4],
        small[5],
        small[6],
        out_first,
        out_bias_first,
        out_second,
        out_bias_second,
    )


def solution(mesh):
    return jax.shard_map(
        per_device,
        mesh=mesh,
        in_specs=(
            P(("rep", "ep"), None),
            P(("rep", "ep"), None),
            P(("rep", "ep")),
            P(("rep", "ep"), None),
            P(),
            P(),
            P(),
            P(),
            P(),
            P(),
            P(),
            P(),
            P(),
            P(),
            P(),
            P("ep", None, None),
            P("ep", None),
            P("ep", None, None),
            P("ep", None),
        ),
        out_specs=(
            P(("rep", "ep"), None),
            P(("rep", "ep"), None),
            P(("rep", "ep")),
            P(("rep", "ep")),
            P(("rep", "ep"), None),
            P(("rep", "ep")),
            P(("rep", "ep"), None),
            P(("rep", "ep"), None),
            P(("rep", "ep")),
            P(("rep", "ep"), None),
            P(("rep", "ep")),
            P(("rep", "ep")),
            P(("rep", "ep")),
            P("ep", "rep", None),
            P("ep", "rep"),
            P("ep", "rep", None),
            P("ep", "rep"),
        ),
        check_vma=False,
    )
```

```python
import functools

import jax
import jax.numpy as jnp
from jax import lax
from jax.experimental import pallas as pl
from jax.experimental.pallas import tpu as pltpu
from jax.sharding import PartitionSpec as P

HEADS = 16
BF = jnp.bfloat16
F32 = jnp.float32
LOG2E = 1.4426950408889634
NEG = -1e30


def dot(left, right):
    return jnp.dot(left, right, preferred_element_type=F32)


def dot_nt(left, right):
    return lax.dot_general(left, right, (((1,), (1,)), ((), ())), preferred_element_type=F32)


def dot_tn(left, right):
    return lax.dot_general(left, right, (((0,), (0,)), ((), ())), preferred_element_type=F32)


def attn_fwd_kernel(len_ref, q_ref, k_ref, v_ref, o_ref, lse_ref, ot_ref, *, blk):
    n, lanes = q_ref.shape
    half = lanes//2
    length = len_ref[0]
    k = k_ref[...].astype(F32)
    lane = lax.broadcasted_iota(jnp.int32,(n,lanes),1)
    row = lax.broadcasted_iota(jnp.int32,(n,lanes),0)
    bias = jnp.where(row<length, 0.0, NEG)
    k_a = jnp.where(lane<half, k, jnp.where(lane==half, bias, 0.0)).astype(BF)
    k_b = jnp.where(lane>=half, k, jnp.where(lane==0, bias, 0.0)).astype(BF)
    qt = q_ref[...].T
    vt = v_ref[...].T
    trow = lax.broadcasted_iota(jnp.int32,(lanes,n),0)
    qt32 = qt.astype(F32)
    qt_a = jnp.where(trow==half, 1.0, qt32).astype(BF)
    qt_b = jnp.where(trow==0, 1.0, qt32).astype(BF)
    tri = lax.broadcasted_iota(jnp.int32,(blk,blk),0) <= lax.broadcasted_iota(jnp.int32,(blk,blk),1)
    ones = jnp.ones((16,n),BF)
    for h,(kk,qq) in enumerate(((k_a,qt_a),(k_b,qt_b))):
        v_ext = jnp.concatenate([vt[h*half:(h+1)*half], ones],0)
        for i in range(n//blk):
            cols = slice(i*blk,(i+1)*blk)
            qb = qq[:,cols]
            diag = jnp.where(tri, dot(kk[cols],qb), NEG)
            if i:
                past = dot(kk[:i*blk],qb)
                top = jnp.maximum(jnp.max(past,0,keepdims=True),jnp.max(diag,0,keepdims=True))
                p = jnp.concatenate([jnp.exp2((past-top)*LOG2E).astype(BF),jnp.exp2((diag-top)*LOG2E).astype(BF)],0)
            else:
                top = jnp.max(diag,0,keepdims=True)
                p = jnp.exp2((diag-top)*LOG2E).astype(BF)
            r = dot(v_ext[:,:(i+1)*blk],p)
            total = r[half:half+1]
            ot_ref[h*half:(h+1)*half,cols] = r[:half]/total
            lse_ref[0,h:h+1,cols] = top + jnp.log(total)
    o_ref[...] = ot_ref[...].T.astype(BF)

def attn_fwd(q,k,v,length,blk=256):
    n,d=q.shape
    pairs=d//128
    spec=pl.BlockSpec((n,128),lambda h:(0,h))
    return pl.pallas_call(functools.partial(attn_fwd_kernel,blk=blk),
        grid=(pairs,),
        in_specs=[pl.BlockSpec(memory_space=pltpu.SMEM),spec,spec,spec],
        out_specs=(spec,pl.BlockSpec((1,2,n),lambda h:(h,0,0))),
        out_shape=(jax.ShapeDtypeStruct((n,d),BF),jax.ShapeDtypeStruct((pairs,2,n),F32)),
        scratch_shapes=[pltpu.VMEM((128,n),F32)],
        compiler_params=pltpu.CompilerParams(vmem_limit_bytes=50<<20),
        cost_estimate=pl.CostEstimate(flops=8 * n * n * d, bytes_accessed=8 * n * d, transcendentals=8 * n * n),
        name="attn_fwd",
    )(length,q,k,v)

def split3(x):
    a=x.astype(BF).astype(F32); r=x-a
    b=r.astype(BF).astype(F32); c=r-b
    return a,b,c

def attn_bwd_kernel(len_ref, q_ref, k_ref, v_ref, o_ref, do_ref, lse_ref, dq_ref, dk_ref, dv_ref, dqt_ref, dk_acc, dv_acc, *, blk):
    n, lanes = q_ref.shape
    half = lanes//2
    length = len_ref[0]
    lane = lax.broadcasted_iota(jnp.int32,(n,lanes),1)
    row = lax.broadcasted_iota(jnp.int32,(n,lanes),0)
    trow = lax.broadcasted_iota(jnp.int32,(lanes,n),0)
    bias = jnp.where(row<length, 0.0, NEG)
    q = q_ref[...].astype(F32); k = k_ref[...].astype(F32); v=v_ref[...].astype(F32); do=do_ref[...].astype(F32)
    kt = k_ref[...].T
    qt = q_ref[...].T.astype(F32)
    dot_t = do_ref[...].T.astype(F32)
    ot = o_ref[...].T.astype(F32)
    prod = dot_t*ot
    heads=[]
    for h in range(2):
        own = (lane<half) if h==0 else (lane>=half)
        base = half if h==0 else 0
        delta = jnp.sum(prod[h*half:(h+1)*half],0,keepdims=True)
        lse = lse_ref[0,h:h+1,:]
        l1,l2,l3 = split3(-lse)
        d1,d2,d3 = split3(-delta)
        one = jnp.where((lane>=base+1)&(lane<=base+3),1.0,0.0)
        k_x = jnp.where(own,k,jnp.where(lane==base,bias,one)).astype(BF)
        v_x = jnp.where(own,v,one).astype(BF)
        q_x = jnp.where(trow==base,1.0,jnp.where(trow==base+1,l1,jnp.where(trow==base+2,l2,jnp.where(trow==base+3,l3,qt)))).astype(BF)
        d_x = jnp.where(trow==base+1,d1,jnp.where(trow==base+2,d2,jnp.where(trow==base+3,d3,dot_t))).astype(BF)
        q_own = jnp.where(own,q,0.0).astype(BF)
        do_own = jnp.where(own,do,0.0).astype(BF)
        heads.append((k_x,v_x,q_x,d_x,q_own,do_own))
    tri = lax.broadcasted_iota(jnp.int32,(blk,blk),0) <= lax.broadcasted_iota(jnp.int32,(blk,blk),1)
    steps=n//blk
    for i in reversed(range(steps)):
        cols = slice(i*blk,(i+1)*blk)
        ps=[];dss=[]
        for h in range(2):
            k_x,v_x,q_x,d_x,q_own,do_own=heads[h]
            qb=q_x[:,cols]; db=d_x[:,cols]
            p_d = jnp.exp2(jnp.where(tri,dot(k_x[cols],qb),NEG)*LOG2E)
            ds_d = p_d*dot(v_x[cols],db)
            if i:
                p_p = jnp.exp2(dot(k_x[:i*blk],qb)*LOG2E)
                ds_p = p_p*dot(v_x[:i*blk],db)
                p=jnp.concatenate([p_p.astype(BF),p_d.astype(BF)],0)
                ds=jnp.concatenate([ds_p.astype(BF),ds_d.astype(BF)],0)
            else:
                p=p_d.astype(BF); ds=ds_d.astype(BF)
            dqt_ref[h*half:(h+1)*half,cols]=dot(kt[h*half:(h+1)*half,:(i+1)*blk],ds)
            ps.append(p);dss.append(ds)
        dv_new = dot(ps[0],heads[0][5][cols])+dot(ps[1],heads[1][5][cols])
        dk_new = dot(dss[0],heads[0][4][cols])+dot(dss[1],heads[1][4][cols])
        if i==steps-1:
            dv_acc[...]=dv_new; dk_acc[...]=dk_new
        else:
            dv_acc[:(i+1)*blk]+=dv_new; dk_acc[:(i+1)*blk]+=dk_new
    scale=half**-0.5
    dq_ref[...]=(dqt_ref[...]*scale).T.astype(BF)
    dk_ref[...]=dk_acc[...].astype(BF)
    dv_ref[...]=dv_acc[...].astype(BF)

def attn_bwd(q,k,v,o,do,lse,length,blk=256):
    n,d=q.shape
    pairs=d//128
    spec=pl.BlockSpec((n,128),lambda h:(0,h))
    return pl.pallas_call(functools.partial(attn_bwd_kernel,blk=blk),
        grid=(pairs,),
        in_specs=[pl.BlockSpec(memory_space=pltpu.SMEM),spec,spec,spec,spec,spec,pl.BlockSpec((1,2,n),lambda h:(h,0,0))],
        out_specs=(spec,spec,spec),
        out_shape=tuple(jax.ShapeDtypeStruct((n,d),BF) for _ in range(3)),
        scratch_shapes=[pltpu.VMEM((128,n),F32),pltpu.VMEM((n,128),F32),pltpu.VMEM((n,128),F32)],
        compiler_params=pltpu.CompilerParams(vmem_limit_bytes=50<<20),
        cost_estimate=pl.CostEstimate(flops=1, bytes_accessed=1, transcendentals=0),
        name="attn_bwd",
    )(length,q,k,v,o,do,lse)


C0=0.7978845608028654; C1=C0*0.044715

def act_both(z):
    z2=z*z
    a=C1*z2+C0
    t=jnp.tanh(z*a)
    h=0.5*t+0.5
    u=z*h
    q=6.0*a-4.0*C0
    return u, h+u*(1.0-h)*q

def expert_tile(b_ref, gy_ref, w1s, bias, w2s, bt_ref, gyt_ref, u_ref, dz_ref, out_ref, rblk):
    w1 = jnp.concatenate([w[...] for w in w1s], 1)
    w2 = jnp.concatenate([w[...] for w in w2s], 0)
    total = None
    for s in range(0, b_ref.shape[0], rblk):
        rs = slice(s, s + rblk)
        u, slope = act_both(dot(b_ref[rs, :], w1) + bias)
        u_ref[rs, :] = u.astype(BF)
        dz = dot_nt(gy_ref[rs, :], w2) * slope
        dz_ref[rs, :] = dz.astype(BF)
        part = jnp.sum(dz, 0, keepdims=True)
        total = part if total is None else total + part
    rep, _two, own = out_ref.shape[:3]
    g1 = dot(bt_ref[...], dz_ref[...]).astype(BF)
    for r in range(rep):
        out_ref[r, 0] = g1[r * own : (r + 1) * own]
    g2 = dot(gyt_ref[...], u_ref[...]).astype(BF).T
    for r in range(rep):
        out_ref[r, 1] = g2[r * own : (r + 1) * own]
    return total


def expert_first_kernel(*refs, rep, rblk):
    b_ref, gy_ref = refs[:2]
    w1s, b1_ref, w2s = refs[2 : 2 + rep], refs[2 + rep], refs[3 + rep : 3 + 2 * rep]
    u_ref, dz_ref, out_ref, gb1_ref, bt_ref, gyt_ref = refs[3 + 2 * rep :]
    bt_ref[...] = b_ref[...].T
    gyt_ref[...] = gy_ref[...].T
    gb1_ref[...] = expert_tile(
        b_ref, gy_ref, w1s, b1_ref[...], w2s, bt_ref, gyt_ref, u_ref, dz_ref, out_ref.at[:, 0], rblk
    )


def expert_rest_kernel(*refs, rep, rblk):
    b_ref, gy_ref = refs[:2]
    w1s, b1_ref, w2s = refs[2 : 2 + rep], refs[2 + rep], refs[3 + rep : 3 + 2 * rep]
    dz0_ref, _u_any, u_ref, out_ref, gb1_ref, db_ref, bt_ref, gyt_ref, dz_ref, acc_ref = refs[3 + 2 * rep :]
    step = pl.program_id(0)
    rows = b_ref.shape[0]

    def add_rows(source, first):
        w1 = jnp.concatenate([w[...] for w in w1s], 1)
        for s in range(0, rows, rblk):
            rs = slice(s, s + rblk)
            part = dot_nt(source[rs, :], w1)
            acc_ref[rs, :] = part if first else acc_ref[rs, :] + part

    @pl.when(step == 0)
    def _():
        bt_ref[...] = b_ref[...].T
        gyt_ref[...] = gy_ref[...].T
        add_rows(dz0_ref, True)

    @pl.when(step > 0)
    def _():
        gb1_ref[...] = expert_tile(
            b_ref, gy_ref, w1s, b1_ref[...], w2s, bt_ref, gyt_ref, u_ref, dz_ref, out_ref.at[:, 0], rblk
        )
        add_rows(dz_ref, False)

    @pl.when(step == pl.num_programs(0) - 1)
    def _():
        db_ref[...] = acc_ref[...].astype(BF)


def expert_specs(rows, d, sub, rep, tiles, tile_of):
    once = pl.Buffered(1)
    whole = pl.BlockSpec((rows, d), lambda j: (0, 0), pipeline_mode=once)

    def first(r):
        return pl.BlockSpec((d, sub), lambda j: (0, r * tiles + tile_of(j)))

    def second(r):
        return pl.BlockSpec((sub, d), lambda j: (r * tiles + tile_of(j), 0))

    return (
        [whole, whole]
        + [first(r) for r in range(rep)]
        + [pl.BlockSpec((1, rep * sub), lambda j: (0, tile_of(j)))]
        + [second(r) for r in range(rep)]
    )


def expert_first(b, gy, w1, b1, w2, rep, tiles, rblk=256):
    rows, d = b.shape
    ff = w1.shape[1]
    sub = ff // (rep * tiles)
    tile = rep * sub
    own = d // rep
    specs = expert_specs(rows, d, sub, rep, tiles, lambda j: 0)
    return pl.pallas_call(
        functools.partial(expert_first_kernel, rep=rep, rblk=rblk),
        grid=(1,),
        in_specs=specs,
        out_specs=(
            pl.BlockSpec((rows, tile), lambda j: (0, 0)),
            pl.BlockSpec((rows, tile), lambda j: (0, 0)),
            pl.BlockSpec((rep, 1, 2, own, d), lambda j: (0, 0, 0, 0, 0)),
            pl.BlockSpec((1, tile), lambda j: (0, 0)),
        ),
        out_shape=(
            jax.ShapeDtypeStruct((rows, ff), BF),
            jax.ShapeDtypeStruct((rows, tile), BF),
            jax.ShapeDtypeStruct((rep, 1, 2, own, d), BF),
            jax.ShapeDtypeStruct((1, tile), F32),
        ),
        scratch_shapes=[pltpu.VMEM((d, rows), BF), pltpu.VMEM((d, rows), BF)],
        compiler_params=pltpu.CompilerParams(vmem_limit_bytes=60 << 20),
        cost_estimate=pl.CostEstimate(flops=1, bytes_accessed=1, transcendentals=0),
        name="expert_first",
    )(b, gy, *([w1] * rep), b1, *([w2] * rep))


def expert_rest(b, gy, w1, b1, w2, dz0, u, rep, tiles, rblk=256):
    rows, d = b.shape
    ff = w1.shape[1]
    sub = ff // (rep * tiles)
    tile = rep * sub
    own = d // rep
    specs = expert_specs(rows, d, sub, rep, tiles, lambda j: j)
    later = lambda j: jnp.maximum(j, 1)
    return pl.pallas_call(
        functools.partial(expert_rest_kernel, rep=rep, rblk=rblk),
        grid=(tiles,),
        in_specs=specs
        + [
            pl.BlockSpec((rows, tile), lambda j: (0, 0), pipeline_mode=pl.Buffered(1)),
            pl.BlockSpec(memory_space=pl.ANY),
        ],
        out_specs=(
            pl.BlockSpec((rows, tile), lambda j: (0, later(j))),
            pl.BlockSpec((rep, 1, 2, own, d), lambda j: (0, later(j) - 1, 0, 0, 0)),
            pl.BlockSpec((1, tile), lambda j: (0, later(j) - 1)),
            pl.BlockSpec((rows, d), lambda j: (0, 0), pipeline_mode=pl.Buffered(1)),
        ),
        out_shape=(
            jax.ShapeDtypeStruct((rows, ff), BF),
            jax.ShapeDtypeStruct((rep, tiles - 1, 2, own, d), BF),
            jax.ShapeDtypeStruct((1, ff - tile), F32),
            jax.ShapeDtypeStruct((rows, d), BF),
        ),
        scratch_shapes=[
            pltpu.VMEM((d, rows), BF),
            pltpu.VMEM((d, rows), BF),
            pltpu.VMEM((rows, tile), BF),
            pltpu.VMEM((rows, d), F32),
        ],
        input_output_aliases={4 + 2 * rep: 0},
        compiler_params=pltpu.CompilerParams(vmem_limit_bytes=62 << 20),
        cost_estimate=pl.CostEstimate(flops=1, bytes_accessed=1, transcendentals=0),
        name="expert_rest",
    )(b, gy, *([w1] * rep), b1, *([w2] * rep), dz0, u)


def expert_result_kernel(*refs, rep, rblk):
    u_ref, w2s, b2_ref, y_ref, acc_ref = refs[0], refs[1 : 1 + rep], refs[1 + rep], refs[2 + rep], refs[3 + rep]
    step = pl.program_id(0)
    w2 = jnp.concatenate([w[...] for w in w2s], 0)

    @pl.when(step == 0)
    def _():
        acc_ref[...] = jnp.broadcast_to(b2_ref[...], acc_ref.shape)

    for s in range(0, u_ref.shape[0], rblk):
        rs = slice(s, s + rblk)
        acc_ref[rs, :] += dot(u_ref[rs, :], w2)

    @pl.when(step == pl.num_programs(0) - 1)
    def _():
        y_ref[...] = acc_ref[...].astype(BF)


def expert_result(u, w2, b2, rep, tiles, rblk=256):
    rows, ff = u.shape
    d = w2.shape[1]
    sub = ff // (rep * tiles)

    def second(r):
        return pl.BlockSpec((sub, d), lambda j: (r * tiles + j, 0))

    return pl.pallas_call(
        functools.partial(expert_result_kernel, rep=rep, rblk=rblk),
        grid=(tiles,),
        in_specs=[pl.BlockSpec((rows, rep * sub), lambda j: (0, j))]
        + [second(r) for r in range(rep)]
        + [pl.BlockSpec((1, d), lambda j: (0, 0))],
        out_specs=pl.BlockSpec((rows, d), lambda j: (0, 0)),
        out_shape=jax.ShapeDtypeStruct((rows, d), BF),
        scratch_shapes=[pltpu.VMEM((rows, d), F32)],
        compiler_params=pltpu.CompilerParams(vmem_limit_bytes=50 << 20),
        cost_estimate=pl.CostEstimate(flops=1, bytes_accessed=1, transcendentals=0),
        name="expert_result",
    )(u, *([w2] * rep), b2)


def unpack_kernel(a_ref, b_ref, g1_ref, g2_ref, *, rep, tiles, sub):
    for c in range(tiles):
        src = a_ref.at[0] if c == 0 else b_ref.at[c - 1]
        for r in range(rep):
            start = (r * tiles + c) * sub
            g1_ref[:, start : start + sub] = src[0, :, r * sub : (r + 1) * sub].astype(F32)
        g2_ref[c * sub : (c + 1) * sub] = src[1].astype(F32)


def unpack_grads(a, b, rep, tiles):
    _one, _two, own, d = a.shape
    sub = own
    vmem = pl.BlockSpec(memory_space=pltpu.VMEM)
    return pl.pallas_call(
        functools.partial(unpack_kernel, rep=rep, tiles=tiles, sub=sub),
        in_specs=[vmem, vmem],
        out_specs=(vmem, vmem),
        out_shape=(
            jax.ShapeDtypeStruct((own, rep * tiles * sub), F32),
            jax.ShapeDtypeStruct((tiles * sub, d), F32),
        ),
        compiler_params=pltpu.CompilerParams(vmem_limit_bytes=40 << 20),
        name="unpack_grads",
    )(a, b)


def layer_norm(hidden, norm_gain, norm_bias):
    row_mean = jnp.mean(hidden, -1, keepdims=True)
    centred = hidden - row_mean
    inv_std = lax.rsqrt(jnp.mean(centred * centred, -1, keepdims=True) + 1e-05)
    normed = centred * inv_std
    return (normed * norm_gain + norm_bias, normed, inv_std)


def norm_back(upstream, normed, inv_std, norm_gain):
    scaled = upstream * norm_gain
    mean_one = jnp.mean(scaled, -1, keepdims=True)
    mean_two = jnp.mean(scaled * normed, -1, keepdims=True)
    return (
        inv_std * (scaled - mean_one - normed * mean_two),
        jnp.sum(upstream * normed, 0),
        jnp.sum(upstream, 0),
    )


def after_experts_kernel(
    target_ref, home_ref, cot_ref, hidden_ref, gain_ref, w_out_ref, gh_ref, ga_ref, do_ref, sums_ref
):
    rows, width = cot_ref.shape
    places = home_ref.shape[0]
    pick = (lax.broadcasted_iota(jnp.int32, (rows, places), 1) == target_ref[...]).astype(BF)
    d = dot(pick, home_ref[...])
    hidden = hidden_ref[...]
    centred = hidden - jnp.mean(hidden, -1, keepdims=True)
    inv = lax.rsqrt(jnp.mean(centred * centred, -1, keepdims=True) + 1e-05)
    unit = centred * inv
    scaled = d * gain_ref[...]
    mean_one = jnp.mean(scaled, -1, keepdims=True)
    mean_two = jnp.mean(scaled * unit, -1, keepdims=True)
    grad = cot_ref[...].astype(F32) + inv * (scaled - mean_one - unit * mean_two)
    gh_ref[...] = grad
    low = grad.astype(BF)
    ga_ref[...] = low
    do_ref[...] = dot_nt(low, w_out_ref[...]).astype(BF)
    parts = [jnp.sum(low.astype(F32), 0, keepdims=True), jnp.sum(d * unit, 0, keepdims=True), jnp.sum(d, 0, keepdims=True)]
    parts = jnp.concatenate(parts + [jnp.zeros((8 - len(parts), width), F32)], 0)

    @pl.when(pl.program_id(0) == 0)
    def _():
        sums_ref[...] = parts

    @pl.when(pl.program_id(0) > 0)
    def _():
        sums_ref[...] += parts


def after_experts(target, home, cot, hidden, gain, w_out, block=256):
    n, width = cot.shape
    places = home.shape[0]
    rows = pl.BlockSpec((block, width), lambda i: (i, 0))
    once = pl.Buffered(1)
    return pl.pallas_call(
        after_experts_kernel,
        grid=(n // block,),
        in_specs=[
            pl.BlockSpec((block, 1), lambda i: (i, 0)),
            pl.BlockSpec((places, width), lambda i: (0, 0), pipeline_mode=once),
            rows,
            rows,
            pl.BlockSpec((1, width), lambda i: (0, 0)),
            pl.BlockSpec((width, width), lambda i: (0, 0), pipeline_mode=once),
        ],
        out_specs=(rows, rows, rows, pl.BlockSpec((8, width), lambda i: (0, 0))),
        out_shape=(
            jax.ShapeDtypeStruct((n, width), F32),
            jax.ShapeDtypeStruct((n, width), BF),
            jax.ShapeDtypeStruct((n, width), BF),
            jax.ShapeDtypeStruct((8, width), F32),
        ),
        compiler_params=pltpu.CompilerParams(vmem_limit_bytes=50 << 20),
        name="after_experts",
    )(target, home, cot, hidden, gain, w_out)


def dense_grads_kernel(
    act_ref, mixed_ref, ga_ref, dq_ref, dk_ref, dv_ref, wq_ref, wk_ref, wv_ref, tok_ref, gh_ref, gain_ref,
    x_ref, gt_ref, bias_ref, norm_ref, at_ref, mt_ref, da_ref, *, rep, ep, own, rblk,
):
    step = pl.program_id(0)
    n = act_ref.shape[0]

    @pl.when(step == 0)
    def _():
        at_ref[...] = act_ref[...].T
        mt_ref[...] = mixed_ref[...].T

    for w, (left, right) in enumerate(((at_ref, dq_ref), (at_ref, dk_ref), (at_ref, dv_ref), (mt_ref, ga_ref))):
        g = dot(left[...], right[...]).astype(BF)
        for r in range(rep):
            for e in range(ep):
                start = (r * ep + e) * own
                x_ref[e, r, w] = g[start : start + own]
    bias_ref[0:1] = jnp.sum(dq_ref[...].astype(F32), 0, keepdims=True)
    bias_ref[1:2] = jnp.sum(dv_ref[...].astype(F32), 0, keepdims=True)
    bias_ref[2:8] = jnp.zeros((6, bias_ref.shape[1]), F32)
    for s in range(0, n, rblk):
        rs = slice(s, s + rblk)
        part = dot_nt(dq_ref[rs], wq_ref[...]) + dot_nt(dk_ref[rs], wk_ref[...]) + dot_nt(dv_ref[rs], wv_ref[...])

        @pl.when(step == 0)
        def _():
            da_ref[rs] = part

        @pl.when(step > 0)
        def _():
            da_ref[rs] += part

    @pl.when(step == pl.num_programs(0) - 1)
    def _():
        total_n = jnp.zeros((1, da_ref.shape[1]), F32)
        total_d = jnp.zeros((1, da_ref.shape[1]), F32)
        for s in range(0, n, rblk):
            rs = slice(s, s + rblk)
            d = da_ref[rs]
            hidden = tok_ref[rs].astype(F32)
            centred = hidden - jnp.mean(hidden, -1, keepdims=True)
            inv = lax.rsqrt(jnp.mean(centred * centred, -1, keepdims=True) + 1e-05)
            unit = centred * inv
            scaled = d * gain_ref[...]
            mean_one = jnp.mean(scaled, -1, keepdims=True)
            mean_two = jnp.mean(scaled * unit, -1, keepdims=True)
            gt_ref[rs] = gh_ref[rs] + inv * (scaled - mean_one - unit * mean_two)
            total_n += jnp.sum(d * unit, 0, keepdims=True)
            total_d += jnp.sum(d, 0, keepdims=True)
        norm_ref[...] = jnp.concatenate([total_n, total_d, jnp.zeros((6, da_ref.shape[1]), F32)], 0)


def dense_grads(act, mixed, ga, dq, dk, dv, wq, wk, wv, tokens, gh, gain, rep, ep, block=256, rblk=256):
    n, width = act.shape
    own = width // (rep * ep)
    once = pl.Buffered(1)
    whole = pl.BlockSpec((n, width), lambda j: (0, 0), pipeline_mode=once)
    cols = pl.BlockSpec((n, block), lambda j: (0, j))
    return pl.pallas_call(
        functools.partial(dense_grads_kernel, rep=rep, ep=ep, own=own, rblk=rblk),
        grid=(width // block,),
        in_specs=[whole, whole, cols, cols, cols, cols, cols, cols, cols, whole, whole, pl.BlockSpec((1, width), lambda j: (0, 0))],
        out_specs=(
            pl.BlockSpec((ep, rep, 4, own, block), lambda j: (0, 0, 0, 0, j)),
            pl.BlockSpec((n, width), lambda j: (0, 0), pipeline_mode=once),
            pl.BlockSpec((8, block), lambda j: (0, j)),
            pl.BlockSpec((8, width), lambda j: (0, 0)),
        ),
        out_shape=(
            jax.ShapeDtypeStruct((ep, rep, 4, own, width), BF),
            jax.ShapeDtypeStruct((n, width), F32),
            jax.ShapeDtypeStruct((8, width), F32),
            jax.ShapeDtypeStruct((8, width), F32),
        ),
        scratch_shapes=[pltpu.VMEM((width, n), BF), pltpu.VMEM((width, n), BF), pltpu.VMEM((n, width), F32)],
        compiler_params=pltpu.CompilerParams(vmem_limit_bytes=58 << 20),
        name="dense_grads",
    )(act, mixed, ga, dq, dk, dv, wq, wk, wv, tokens, gh, gain)


def reduce_kernel(*refs, rep, bits, chunks, half):
    x_ref, vec_ref, bias_ref, out_ref, vec_out, bias_out = refs[:6]
    stages = bits
    sizes = len(chunks)
    at = 6
    got = {}
    for stage in range(stages):
        for c in range(sizes):
            for h in range(1 if stage == 0 else 2):
                got[stage, c, h] = refs[at]
                at += 1
    got_z = refs[at]
    part_z = refs[at + 1]
    vec_got, bias_got, vec_sum = refs[at + 2 : at + 5]
    send, recv, vsend, vrecv, bsend, brecv = refs[at + 5 : at + 11]
    me_z = lax.axis_index("rep")
    me = lax.axis_index("ep")

    def bit(b):
        return lax.rem(me // (1 << b), 2)

    def flip(b):
        return me + (1 - 2 * bit(b)) * (1 << b)

    def zpeer(s):
        low, high = lax.rem(me_z, 2), lax.rem(me_z // 2, 2)
        other = me_z
        if s & 1:
            other = other + 1 - 2 * low
        if s & 2:
            other = other + 2 - 4 * high
        return other

    peers = [(me_z, flip(b)) for b in range(bits)] + [(zpeer(s), me) for s in range(1, rep)]
    barrier = pltpu.get_barrier_semaphore()
    for p in peers:
        pl.semaphore_signal(barrier, inc=1, device_id=p, device_id_type=pl.DeviceIdType.MESH)
    pl.semaphore_wait(barrier, len(peers))

    def order(h):
        rest = list(range(1, bits))
        return [0] + (rest if h == 0 else rest[::-1])

    def copy(src, dst, k, peer, sems=None):
        s, r = sems or (send, recv)
        c = pltpu.make_async_remote_copy(
            src_ref=src, dst_ref=dst, send_sem=s.at[k], recv_sem=r.at[k], device_id=peer, device_id_type=pl.DeviceIdType.MESH
        )
        c.start()
        return c

    width = x_ref.shape[-1]
    columns = [pl.ds(0, half), pl.ds(half, half)]

    def axes_after(h, stage):
        done = order(h)[:stage]
        return [b for b in range(bits - 1, -1, -1) if b not in done]

    def cut(ref, h, stage, value, column=None, w=None):
        left = axes_after(h, stage)
        b = order(h)[stage]
        index = [slice(None)] * len(left)
        index[left.index(b)] = value
        index.append(slice(None))
        index.append(w if w is not None else slice(None))
        index.append(slice(None))
        index.append(column if column is not None else slice(None))
        return tuple(index)

    flying = {}
    k = 0
    for c, w in enumerate(chunks):
        flying[0, c, 0] = copy(x_ref.at[cut(x_ref, 0, 0, 1 - bit(0), w=w)], got[0, c, 0], k, (me_z, flip(0)))
        k += 1
    small = copy(vec_ref, vec_got.at[0], 0, (me_z, flip(0)), (vsend, vrecv))
    bias_copies = [copy(bias_ref, bias_got.at[s - 1], s - 1, (zpeer(s), me), (bsend, brecv)) for s in range(1, rep)]
    vec_sum[0] = vec_ref[...]
    for stage in range(stages):
        for c, w in enumerate(chunks):
            for h in range(1 if stage == 0 else 2):
                flying[stage, c, h].wait()
                ref = got[stage, c, h]
                if stage == 0:
                    ref[...] += x_ref[cut(x_ref, 0, 0, bit(0), w=w)]
                else:
                    prev = got[stage - 1, c, 0 if stage == 1 else h]
                    column = columns[h] if stage == 1 else None
                    ref[...] += prev[cut(prev, h, stage, bit(order(h)[stage]), column)]
            if stage + 1 < stages:
                for h in range(2):
                    b = order(h)[stage + 1]
                    src = got[stage, c, 0 if stage == 0 else h]
                    column = columns[h] if stage == 0 else None
                    flying[stage + 1, c, h] = copy(
                        src.at[cut(src, h, stage + 1, 1 - bit(b), column)], got[stage + 1, c, h], k, (me_z, flip(b))
                    )
                    k += 1
            else:
                for h in range(2):
                    part_z[:, w, :, columns[h]] = got[stage, c, h][...]
                for s in range(1, rep):
                    flying["z", c, s] = copy(part_z.at[zpeer(s), w], got_z.at[s - 1, w], k, (zpeer(s), me))
                    k += 1
        small.wait()
        vec_sum[stage + 1] = vec_sum[stage] + vec_got[stage]
        if stage + 1 < stages:
            small = copy(vec_sum.at[stage + 1], vec_got.at[stage + 1], stage + 1, (me_z, flip(stage + 1)), (vsend, vrecv))
    last = [
        copy(vec_sum.at[stages], vec_got.at[stages - 1 + s], stages - 1 + s, (zpeer(s), me), (vsend, vrecv)) for s in range(1, rep)
    ]
    for c, w in enumerate(chunks):
        total = part_z[me_z, w].astype(F32)
        for s in range(1, rep):
            flying["z", c, s].wait()
            total += got_z[s - 1, w].astype(F32)
        out_ref[w] = total
    vec = vec_sum[stages]
    bias = bias_ref[...]
    for s in range(1, rep):
        last[s - 1].wait()
        vec += vec_got[stages - 1 + s]
        bias_copies[s - 1].wait()
        bias += bias_got[s - 1]
    vec_out[...] = vec
    bias_out[...] = bias


def reduce_all(x, vectors, bias, rep, ep):
    _ep, _rep, four, own, width = x.shape
    bits = ep.bit_length() - 1
    half = width // 2
    per = 2
    chunks = [pl.ds(i, per) for i in range(0, four, per)]
    x = x.reshape((2,) * bits + (rep, four, own, width))
    scratch = []
    for stage in range(bits):
        for _c in chunks:
            for _h in range(1 if stage == 0 else 2):
                lead = (2,) * (bits - 1 - stage)
                scratch.append(pltpu.VMEM(lead + (rep, per, own, width if stage == 0 else half), BF))
    copies = len(chunks) * (1 + 2 * (bits - 1) + rep - 1)
    vcount = bits + rep - 1
    scratch += [
        pltpu.VMEM((rep - 1, four, own, width), BF),
        pltpu.VMEM((rep, four, own, width), BF),
        pltpu.VMEM((vcount,) + vectors.shape, F32),
        pltpu.VMEM((rep - 1,) + bias.shape, F32),
        pltpu.VMEM((bits + 1,) + vectors.shape, F32),
        pltpu.SemaphoreType.DMA((copies,)),
        pltpu.SemaphoreType.DMA((copies,)),
        pltpu.SemaphoreType.DMA((vcount,)),
        pltpu.SemaphoreType.DMA((vcount,)),
        pltpu.SemaphoreType.DMA((rep - 1,)),
        pltpu.SemaphoreType.DMA((rep - 1,)),
    ]
    vmem = pl.BlockSpec(memory_space=pltpu.VMEM)
    return pl.pallas_call(
        functools.partial(reduce_kernel, rep=rep, bits=bits, chunks=chunks, half=half),
        in_specs=[vmem] * 3,
        out_specs=(vmem,) * 3,
        out_shape=(
            jax.ShapeDtypeStruct((four, own, width), F32),
            jax.ShapeDtypeStruct(vectors.shape, F32),
            jax.ShapeDtypeStruct(bias.shape, F32),
        ),
        scratch_shapes=scratch,
        compiler_params=pltpu.CompilerParams(vmem_limit_bytes=50 << 20, collective_id=1, has_side_effects=True),
        name="reduce_all",
    )(x, vectors, bias)


def per_device(
    tokens,
    cotangent,
    lengths,
    expert_ids,
    norm1_gain,
    norm1_bias,
    w_query,
    b_query,
    w_key,
    w_value,
    b_value,
    w_out,
    b_out,
    norm2_gain,
    norm2_bias,
    w_in,
    b_in,
    w_back,
    b_back,
):
    row_count, width = tokens.shape
    head_dim = width // HEADS
    ep = lax.axis_size("ep")
    rep = lax.axis_size("rep")
    slots = 5 * row_count // (4 * ep)
    places = ep * slots
    ff = w_in.shape[2]
    w_first = w_in[0]
    w_second = w_back[0]

    chosen = expert_ids[:, 0]
    onehot = (chosen[:, None] == jnp.arange(ep, dtype=jnp.int32)[None, :]).astype(jnp.int32)
    before = jnp.cumsum(onehot, 0, dtype=jnp.int32) - onehot
    target = chosen * slots + jnp.sum(before * onehot, 1, dtype=jnp.int32)
    route = (jnp.arange(places, dtype=jnp.int32)[:, None] == target[None, :]).astype(BF)

    def exchange(rows):
        sent = lax.all_to_all(rows.reshape(ep, slots, width), "ep", 0, 0, tiled=True)
        return sent.reshape(places, width)

    grad_rows = exchange(dot(route, cotangent).astype(BF))

    residual = tokens.astype(F32)
    normed_a, unit_one, inv_one = layer_norm(residual, norm1_gain, norm1_bias)
    act_a = normed_a.astype(BF)
    queries = ((dot(act_a, w_query) + b_query).astype(BF) * head_dim**-0.5).astype(BF)
    keys = dot(act_a, w_key).astype(BF)
    values = (dot(act_a, w_value) + b_value).astype(BF)
    mixed, lse = attn_fwd(queries, keys, values, lengths)
    mixed, grad_rows = lax.optimization_barrier((mixed, grad_rows))
    hidden_one = residual + dot(mixed, w_out) + b_out
    normed_b, unit_two, inv_two = layer_norm(hidden_one, norm2_gain, norm2_bias)
    act_b = normed_b.astype(BF)
    rows_in = exchange(dot(route, act_b).astype(BF))

    at = lax.axis_index("rep")
    tiles = 4
    sub = ff // (rep * tiles)
    bias_in = b_in.reshape(rep, tiles, sub).transpose(1, 0, 2).reshape(1, ff)
    active, grad_inner, part_0, bias_0 = expert_first(rows_in, grad_rows, w_first, bias_in, w_second, rep, tiles)
    active, part_1, bias_1, grad_input = expert_rest(
        rows_in, grad_rows, w_first, bias_in, w_second, grad_inner, active, rep, tiles
    )
    sum_0 = lax.psum_scatter(part_0, "rep", scatter_dimension=0, tiled=True)
    sum_1 = lax.psum_scatter(part_1, "rep", scatter_dimension=0, tiled=True)
    grad_home = exchange(grad_input)
    result = expert_result(active, w_second, b_back, rep, tiles)
    result, grad_home = lax.optimization_barrier((result, grad_home))
    returned = exchange(result)
    g_bias_first = jnp.concatenate([bias_0, bias_1], 1)
    g_bias_first = g_bias_first.reshape(tiles, rep, sub).transpose(1, 0, 2).reshape(1, ff)
    g_bias_second = jnp.sum(grad_rows.astype(F32), 0)

    def remainder(grad_home, g_bias_first, g_bias_second):
        grad_hidden, grad_attn, grad_mixed, sums = after_experts(
            target[:, None], grad_home, cotangent, hidden_one, norm2_gain[None], w_out
        )
        grad_q, grad_k, grad_v = attn_bwd(queries, keys, values, mixed, grad_mixed, lse, lengths)
        x, grad_tokens, bias_sums, norm_sums = dense_grads(
            act_a, mixed, grad_attn, grad_q, grad_k, grad_v, w_query, w_key, w_value, tokens, grad_hidden,
            norm1_gain[None], rep, ep,
        )
        vectors = jnp.concatenate([norm_sums[:2], bias_sums[:2], sums[:3], jnp.zeros((1, width), F32)], 0)
        bias = jnp.concatenate([g_bias_first.reshape(ff // width, width), g_bias_second[None]], 0)
        bias = jnp.pad(bias, ((0, 8 - bias.shape[0]), (0, 0)))
        return (grad_tokens,) + tuple(reduce_all(x, vectors, bias, rep, ep))

    own = width // (rep * ep)
    own_ff, own_width = ff // rep, width // rep
    args = (grad_home, g_bias_first, g_bias_second)
    shapes = jax.eval_shape(remainder, *args)
    grad_tokens, dense, small, grad_bias = lax.cond(
        lengths[0] > 0, remainder, lambda *_: jax.tree.map(lambda x: jnp.zeros(x.shape, x.dtype), shapes), *args
    )
    block_out = (hidden_one + dot_tn(route, returned)).astype(BF)

    place = at * ep + lax.axis_index("ep")
    small = lax.dynamic_slice_in_dim(small, place * own, own, 1)
    rows_bias = own_ff // width
    out_bias_first = lax.dynamic_slice_in_dim(grad_bias, at * rows_bias, rows_bias, 0).reshape(1, own_ff)
    out_bias_second = lax.dynamic_slice(grad_bias, (ff // width, at * own_width), (1, own_width))
    out_first, out_second = unpack_grads(sum_0[0], sum_1[0], rep, tiles)
    out_first, out_second = out_first[None], out_second[None]
    return (
        block_out,
        grad_tokens,
        small[0],
        small[1],
        dense[0],
        small[2],
        dense[1],
        dense[2],
        small[3],
        dense[3],
        small[4],
        small[5],
        small[6],
        out_first,
        out_bias_first,
        out_second,
        out_bias_second,
    )


def solution(mesh):
    return jax.shard_map(
        per_device,
        mesh=mesh,
        in_specs=(
            P(("rep", "ep"), None),
            P(("rep", "ep"), None),
            P(("rep", "ep")),
            P(("rep", "ep"), None),
            P(),
            P(),
            P(),
            P(),
            P(),
            P(),
            P(),
            P(),
            P(),
            P(),
            P(),
            P("ep", None, None),
            P("ep", None),
            P("ep", None, None),
            P("ep", None),
        ),
        out_specs=(
            P(("rep", "ep"), None),
            P(("rep", "ep"), None),
            P(("rep", "ep")),
            P(("rep", "ep")),
            P(("rep", "ep"), None),
            P(("rep", "ep")),
            P(("rep", "ep"), None),
            P(("rep", "ep"), None),
            P(("rep", "ep")),
            P(("rep", "ep"), None),
            P(("rep", "ep")),
            P(("rep", "ep")),
            P(("rep", "ep")),
            P("ep", "rep", None),
            P("ep", "rep"),
            P("ep", "rep", None),
            P("ep", "rep"),
        ),
        check_vma=False,
    )
```

```python
import functools

import jax
import jax.numpy as jnp
from jax import lax
from jax.experimental import pallas as pl
from jax.experimental.pallas import tpu as pltpu
from jax.sharding import PartitionSpec as P

HEADS = 16
BF = jnp.bfloat16
F32 = jnp.float32
LOG2E = 1.4426950408889634
NEG = -1e30


def dot(left, right):
    return jnp.dot(left, right, preferred_element_type=F32)


def dot_nt(left, right):
    return lax.dot_general(left, right, (((1,), (1,)), ((), ())), preferred_element_type=F32)


def dot_tn(left, right):
    return lax.dot_general(left, right, (((0,), (0,)), ((), ())), preferred_element_type=F32)


def attn_fwd_kernel(len_ref, q_ref, k_ref, v_ref, o_ref, lse_ref, ot_ref, *, blk):
    n, lanes = q_ref.shape
    half = lanes//2
    length = len_ref[0]
    k = k_ref[...].astype(F32)
    lane = lax.broadcasted_iota(jnp.int32,(n,lanes),1)
    row = lax.broadcasted_iota(jnp.int32,(n,lanes),0)
    bias = jnp.where(row<length, 0.0, NEG)
    k_a = jnp.where(lane<half, k, jnp.where(lane==half, bias, 0.0)).astype(BF)
    k_b = jnp.where(lane>=half, k, jnp.where(lane==0, bias, 0.0)).astype(BF)
    qt = q_ref[...].T
    vt = v_ref[...].T
    trow = lax.broadcasted_iota(jnp.int32,(lanes,n),0)
    qt32 = qt.astype(F32)
    qt_a = jnp.where(trow==half, 1.0, qt32).astype(BF)
    qt_b = jnp.where(trow==0, 1.0, qt32).astype(BF)
    tri = lax.broadcasted_iota(jnp.int32,(blk,blk),0) <= lax.broadcasted_iota(jnp.int32,(blk,blk),1)
    ones = jnp.ones((16,n),BF)
    for h,(kk,qq) in enumerate(((k_a,qt_a),(k_b,qt_b))):
        v_ext = jnp.concatenate([vt[h*half:(h+1)*half], ones],0)
        for i in range(n//blk):
            cols = slice(i*blk,(i+1)*blk)
            qb = qq[:,cols]
            diag = jnp.where(tri, dot(kk[cols],qb), NEG)
            if i:
                past = dot(kk[:i*blk],qb)
                top = jnp.maximum(jnp.max(past,0,keepdims=True),jnp.max(diag,0,keepdims=True))
                p = jnp.concatenate([jnp.exp2((past-top)*LOG2E).astype(BF),jnp.exp2((diag-top)*LOG2E).astype(BF)],0)
            else:
                top = jnp.max(diag,0,keepdims=True)
                p = jnp.exp2((diag-top)*LOG2E).astype(BF)
            r = dot(v_ext[:,:(i+1)*blk],p)
            total = r[half:half+1]
            ot_ref[h*half:(h+1)*half,cols] = r[:half]/total
            lse_ref[0,h:h+1,cols] = top + jnp.log(total)
    o_ref[...] = ot_ref[...].T.astype(BF)

def attn_fwd(q, k, v, length, blk=512):
    n, d = q.shape
    pairs = d // 128
    spec = pl.BlockSpec((n, 128), lambda h: (0, h))
    return pl.pallas_call(
        functools.partial(attn_fwd_kernel, blk=blk),
        grid=(pairs,),
        in_specs=[pl.BlockSpec(memory_space=pltpu.SMEM), spec, spec, spec],
        out_specs=(spec, pl.BlockSpec((1, 2, n), lambda h: (h, 0, 0))),
        out_shape=(jax.ShapeDtypeStruct((n, d), BF), jax.ShapeDtypeStruct((pairs, 2, n), F32)),
        scratch_shapes=[pltpu.VMEM((128, n), F32)],
        compiler_params=pltpu.CompilerParams(vmem_limit_bytes=50 << 20),
        cost_estimate=pl.CostEstimate(flops=8 * n * n * d, bytes_accessed=8 * n * d, transcendentals=8 * n * n),
        name="attn_fwd",
    )(length, q, k, v)


def split3(x):
    a=x.astype(BF).astype(F32); r=x-a
    b=r.astype(BF).astype(F32); c=r-b
    return a,b,c

def attn_bwd_kernel(len_ref, q_ref, k_ref, v_ref, o_ref, do_ref, lse_ref, dq_ref, dk_ref, dv_ref, dqt_ref, dk_acc, dv_acc, *, blk):
    n, lanes = q_ref.shape
    half = lanes//2
    length = len_ref[0]
    lane = lax.broadcasted_iota(jnp.int32,(n,lanes),1)
    row = lax.broadcasted_iota(jnp.int32,(n,lanes),0)
    trow = lax.broadcasted_iota(jnp.int32,(lanes,n),0)
    bias = jnp.where(row<length, 0.0, NEG)
    q = q_ref[...].astype(F32); k = k_ref[...].astype(F32); v=v_ref[...].astype(F32); do=do_ref[...].astype(F32)
    kt = k_ref[...].T
    qt = q_ref[...].T.astype(F32)
    dot_t = do_ref[...].T.astype(F32)
    ot = o_ref[...].T.astype(F32)
    prod = dot_t*ot
    heads=[]
    for h in range(2):
        own = (lane<half) if h==0 else (lane>=half)
        base = half if h==0 else 0
        delta = jnp.sum(prod[h*half:(h+1)*half],0,keepdims=True)
        lse = lse_ref[0,h:h+1,:]
        l1,l2,l3 = split3(-lse)
        d1,d2,d3 = split3(-delta)
        one = jnp.where((lane>=base+1)&(lane<=base+3),1.0,0.0)
        k_x = jnp.where(own,k,jnp.where(lane==base,bias,one)).astype(BF)
        v_x = jnp.where(own,v,one).astype(BF)
        q_x = jnp.where(trow==base,1.0,jnp.where(trow==base+1,l1,jnp.where(trow==base+2,l2,jnp.where(trow==base+3,l3,qt)))).astype(BF)
        d_x = jnp.where(trow==base+1,d1,jnp.where(trow==base+2,d2,jnp.where(trow==base+3,d3,dot_t))).astype(BF)
        q_own = jnp.where(own,q,0.0).astype(BF)
        do_own = jnp.where(own,do,0.0).astype(BF)
        heads.append((k_x,v_x,q_x,d_x,q_own,do_own))
    tri = lax.broadcasted_iota(jnp.int32,(blk,blk),0) <= lax.broadcasted_iota(jnp.int32,(blk,blk),1)
    steps=n//blk
    for i in reversed(range(steps)):
        cols = slice(i*blk,(i+1)*blk)
        ps=[];dss=[]
        for h in range(2):
            k_x,v_x,q_x,d_x,q_own,do_own=heads[h]
            qb=q_x[:,cols]; db=d_x[:,cols]
            p_d = jnp.exp2(jnp.where(tri,dot(k_x[cols],qb),NEG)*LOG2E)
            ds_d = p_d*dot(v_x[cols],db)
            if i:
                p_p = jnp.exp2(dot(k_x[:i*blk],qb)*LOG2E)
                ds_p = p_p*dot(v_x[:i*blk],db)
                p=jnp.concatenate([p_p.astype(BF),p_d.astype(BF)],0)
                ds=jnp.concatenate([ds_p.astype(BF),ds_d.astype(BF)],0)
            else:
                p=p_d.astype(BF); ds=ds_d.astype(BF)
            dqt_ref[h*half:(h+1)*half,cols]=dot(kt[h*half:(h+1)*half,:(i+1)*blk],ds)
            ps.append(p);dss.append(ds)
        dv_new = dot(ps[0],heads[0][5][cols])+dot(ps[1],heads[1][5][cols])
        dk_new = dot(dss[0],heads[0][4][cols])+dot(dss[1],heads[1][4][cols])
        if i==steps-1:
            dv_acc[...]=dv_new; dk_acc[...]=dk_new
        else:
            dv_acc[:(i+1)*blk]+=dv_new; dk_acc[:(i+1)*blk]+=dk_new
    scale=half**-0.5
    dq_ref[...]=(dqt_ref[...]*scale).T.astype(BF)
    dk_ref[...]=dk_acc[...].astype(BF)
    dv_ref[...]=dv_acc[...].astype(BF)

def attn_bwd(q,k,v,o,do,lse,length,blk=256):
    n,d=q.shape
    pairs=d//128
    spec=pl.BlockSpec((n,128),lambda h:(0,h))
    return pl.pallas_call(functools.partial(attn_bwd_kernel,blk=blk),
        grid=(pairs,),
        in_specs=[pl.BlockSpec(memory_space=pltpu.SMEM),spec,spec,spec,spec,spec,pl.BlockSpec((1,2,n),lambda h:(h,0,0))],
        out_specs=(spec,spec,spec),
        out_shape=tuple(jax.ShapeDtypeStruct((n,d),BF) for _ in range(3)),
        scratch_shapes=[pltpu.VMEM((128,n),F32),pltpu.VMEM((n,128),F32),pltpu.VMEM((n,128),F32)],
        compiler_params=pltpu.CompilerParams(vmem_limit_bytes=50<<20),
        cost_estimate=pl.CostEstimate(flops=1, bytes_accessed=1, transcendentals=0),
        name="attn_bwd",
    )(length,q,k,v,o,do,lse)


C0=0.7978845608028654; C1=C0*0.044715

def act_both(z):
    z2=z*z
    a=C1*z2+C0
    t=jnp.tanh(z*a)
    h=0.5*t+0.5
    u=z*h
    q=6.0*a-4.0*C0
    return u, h+u*(1.0-h)*q

def expert_own_kernel(
    b_ref, gy_ref, w1_ref, b1_ref, w2_ref, u_ref, dz_ref, gb1_ref, db_ref, acc_ref, *, rblk
):
    step = pl.program_id(0)
    rows = b_ref.shape[0]
    w1 = w1_ref[...]
    w2 = w2_ref[...]
    bias = b1_ref[...]
    total = None
    for s in range(0, rows, rblk):
        rs = slice(s, s + rblk)
        u, slope = act_both(dot(b_ref[rs, :], w1) + bias)
        u_ref[rs, :] = u.astype(BF)
        dz = dot_nt(gy_ref[rs, :], w2) * slope
        dz_ref[rs, :] = dz.astype(BF)
        part = jnp.sum(dz, 0, keepdims=True)
        total = part if total is None else total + part
    gb1_ref[...] = total

    @pl.when(step == 0)
    def _():
        for s in range(0, rows, rblk):
            rs = slice(s, s + rblk)
            acc_ref[rs, :] = dot_nt(dz_ref[rs, :], w1)

    @pl.when(step > 0)
    def _():
        for s in range(0, rows, rblk):
            rs = slice(s, s + rblk)
            acc_ref[rs, :] += dot_nt(dz_ref[rs, :], w1)

    @pl.when(step == pl.num_programs(0) - 1)
    def _():
        db_ref[...] = acc_ref[...].astype(BF)


def expert_own(b, gy, w1, b1, w2, tile, rblk=256):
    rows, d = b.shape
    ff = w1.shape[1]
    whole = pl.BlockSpec((rows, d), lambda j: (0, 0), pipeline_mode=pl.Buffered(1))
    return pl.pallas_call(
        functools.partial(expert_own_kernel, rblk=rblk),
        grid=(ff // tile,),
        in_specs=[
            whole,
            whole,
            pl.BlockSpec((d, tile), lambda j: (0, j)),
            pl.BlockSpec((1, tile), lambda j: (0, j)),
            pl.BlockSpec((tile, d), lambda j: (j, 0)),
        ],
        out_specs=(
            pl.BlockSpec((rows, tile), lambda j: (0, j)),
            pl.BlockSpec((rows, tile), lambda j: (0, j)),
            pl.BlockSpec((1, tile), lambda j: (0, j)),
            pl.BlockSpec((rows, d), lambda j: (0, 0)),
        ),
        out_shape=(
            jax.ShapeDtypeStruct((rows, ff), BF),
            jax.ShapeDtypeStruct((rows, ff), BF),
            jax.ShapeDtypeStruct((1, ff), F32),
            jax.ShapeDtypeStruct((rows, d), BF),
        ),
        scratch_shapes=[pltpu.VMEM((rows, d), F32)],
        compiler_params=pltpu.CompilerParams(vmem_limit_bytes=60 << 20),
        cost_estimate=pl.CostEstimate(flops=8 * rows * d * ff, bytes_accessed=4 * d * ff, transcendentals=rows * ff),
        name="expert_own",
    )(b, gy, w1, b1, w2)


def turn_kernel(half_ref, bo0_ref, bo1_ref, gyo_ref, gyp_ref, bto_ref, gto_ref, gtp_ref):
    @pl.when(pl.program_id(0) == 0)
    def _():
        bto_ref[...] = bo0_ref[...].T

    @pl.when(pl.program_id(0) == 1)
    def _():
        bto_ref[...] = bo1_ref[...].T

    gto_ref[...] = gyo_ref[...].T
    gtp_ref[...] = gyp_ref[...].T


def turn(half, b, gy, gy_pair, rep):
    rows, d = b.shape
    own = d // rep
    block = d // rep
    cols = pl.BlockSpec((rows, block), lambda j, h: (0, j))
    turned = pl.BlockSpec((block, rows), lambda j, h: (j, 0))
    return pl.pallas_call(
        turn_kernel,
        grid_spec=pltpu.PrefetchScalarGridSpec(
            num_scalar_prefetch=1,
            grid=(rep,),
            in_specs=[
                pl.BlockSpec((rows, own), lambda j, h: (0, h[0])),
                pl.BlockSpec((rows, own), lambda j, h: (0, h[0] + 2)),
                cols,
                cols,
            ],
            out_specs=(pl.BlockSpec((own, rows), lambda j, h: (jnp.minimum(j, 1), 0)), turned, turned),
        ),
        out_shape=(
            jax.ShapeDtypeStruct((2 * own, rows), BF),
            jax.ShapeDtypeStruct((d, rows), BF),
            jax.ShapeDtypeStruct((d, rows), BF),
        ),
        compiler_params=pltpu.CompilerParams(vmem_limit_bytes=40 << 20),
        cost_estimate=pl.CostEstimate(flops=1, bytes_accessed=10 * rows * d, transcendentals=0),
        name="turn",
    )(half, b, b, gy, gy_pair)


def pair_kernel(
    half_ref, bto_ref, bp_ref, gto_ref, gtp_ref, gyp_ref, w1_ref, b1_ref, w2_ref, u_ref, dz_ref,
    out_ref, btp_ref, up_ref, dzp_ref, *, seconds, rblk,
):
    step = pl.program_id(0)
    rows = bp_ref.shape[0]
    own = bto_ref.shape[0] // 2
    tile = w1_ref.shape[1]

    @pl.when(step == 0)
    def _():
        for k in range(2):
            start = pl.multiple_of((half_ref[0] + 2 * k) * own, own)
            btp_ref[k * own : (k + 1) * own] = bp_ref[:, pl.ds(start, own)].T

    w1 = w1_ref[...]
    w2 = w2_ref[...]
    bias = b1_ref[...]
    for s in range(0, rows, rblk):
        rs = slice(s, s + rblk)
        u, slope = act_both(dot(bp_ref[rs, :], w1) + bias)
        up_ref[rs, :] = u.astype(BF)
        dzp_ref[rs, :] = (dot_nt(gyp_ref[rs, :], w2) * slope).astype(BF)
    g1 = (dot(bto_ref[...], dz_ref[...]) + dot(btp_ref[...], dzp_ref[...])).astype(BF)
    per_row = out_ref.shape[2] // tile
    base = 2 * tile // 2
    where = pl.ds(pl.multiple_of(base + own * (step // per_row), own), own)
    column = pl.ds(pl.multiple_of(tile * lax.rem(step, per_row), tile), tile)
    out_ref[0, where, column] = g1[:own]
    out_ref[1, where, column] = g1[own:]

    @pl.when(step < seconds)
    def _():
        g2 = dot(gto_ref[...], u_ref[...]) + dot(gtp_ref[...], up_ref[...])
        out_ref[step, :tile] = g2.astype(BF).T


def expert_pair(half, turned, b_pair, gy_pair, w1, b1, w2, u, dz, tile_of, steps, tile, rep, rblk=256):
    rows, d = b_pair.shape
    own = d // rep
    once = pl.Buffered(1)
    per_row = d // tile
    height = tile + own * (steps // per_row)

    def fixed(shape, index=(0, 0)):
        return pl.BlockSpec(shape, lambda j, h: index, pipeline_mode=once)

    return pl.pallas_call(
        functools.partial(pair_kernel, seconds=2, rblk=rblk),
        grid_spec=pltpu.PrefetchScalarGridSpec(
            num_scalar_prefetch=1,
            grid=(steps,),
            in_specs=[
                fixed((2 * own, rows)),
                fixed((rows, d)),
                fixed((d, rows)),
                fixed((d, rows)),
                fixed((rows, d)),
                pl.BlockSpec((d, tile), lambda j, h: (0, tile_of(j, h[0]))),
                pl.BlockSpec((1, tile), lambda j, h: (0, tile_of(j, h[0]))),
                pl.BlockSpec((tile, d), lambda j, h: (tile_of(j, h[0]), 0)),
                pl.BlockSpec((rows, tile), lambda j, h: (0, tile_of(j, h[0]))),
                pl.BlockSpec((rows, tile), lambda j, h: (0, tile_of(j, h[0]))),
            ],
            out_specs=pl.BlockSpec((2, height, d), lambda j, h: (0, 0, 0), pipeline_mode=once),
            scratch_shapes=[
                pltpu.VMEM((2 * own, rows), BF),
                pltpu.VMEM((rows, tile), BF),
                pltpu.VMEM((rows, tile), BF),
            ],
        ),
        out_shape=jax.ShapeDtypeStruct((2, height, d), BF),
        compiler_params=pltpu.CompilerParams(vmem_limit_bytes=60 << 20),
        cost_estimate=pl.CostEstimate(
            flops=9 * rows * d * tile * steps, bytes_accessed=16 * d * tile * steps, transcendentals=rows * tile * steps
        ),
        name="expert_pair",
    )(half, turned[0], b_pair, turned[1], turned[2], gy_pair, w1, b1, w2, u, dz)


def early_tile(j, h):
    return 2 * h + 4 * j


def late_tile(j, h):
    k = j - 2
    return jnp.where(j < 2, 2 * h + 1 + 4 * j, 2 * (1 - h) + lax.rem(k + 2, 2) + 4 * ((k + 2) // 2 - 1))


def unpack_kernel(half_ref, a_ref, b_ref, g1_ref, g2_ref, *, tile, own):
    per_row = a_ref.shape[1] // tile
    h = half_ref[0]
    g2_ref[:tile] = a_ref[:tile].astype(F32)
    g2_ref[tile:] = b_ref[:tile].astype(F32)
    for src, tile_of, steps in ((a_ref, early_tile, 2), (b_ref, late_tile, 6)):
        for j in range(steps):
            start = pl.multiple_of(tile_of(j, h) * tile, tile)
            rows = slice(tile + own * (j // per_row), tile + own * (j // per_row + 1))
            c = tile * (j % per_row)
            g1_ref[:, pl.ds(start, tile)] = src[rows, c : c + tile].astype(F32)


def unpack_grads(half, a, b, tile, ff):
    d = a.shape[1]
    own = d // 4
    vmem = pl.BlockSpec(memory_space=pltpu.VMEM)
    return pl.pallas_call(
        functools.partial(unpack_kernel, tile=tile, own=own),
        in_specs=[pl.BlockSpec(memory_space=pltpu.SMEM), vmem, vmem],
        out_specs=(vmem, vmem),
        out_shape=(jax.ShapeDtypeStruct((own, ff), F32), jax.ShapeDtypeStruct((2 * tile, d), F32)),
        compiler_params=pltpu.CompilerParams(vmem_limit_bytes=60 << 20),
        name="unpack_grads",
    )(half, a, b)


def dispatch_kernel(ids_ref, rows_ref, col_ref, row_ref, out_ref, early_ref, late_ref, *, slots, block, cut):
    n = ids_ref.shape[0]
    places = out_ref.shape[0]
    step = pl.program_id(0)

    @pl.when(step == 0)
    def _():
        ids = ids_ref[...]
        lanes = lax.broadcasted_iota(jnp.int32, (n, 128), 1)
        onehot = jnp.where(ids == lanes, 1.0, 0.0)
        tri = (lax.broadcasted_iota(jnp.int32, (block, block), 1) < lax.broadcasted_iota(jnp.int32, (block, block), 0)).astype(BF)
        carry = jnp.zeros((1, 128), F32)
        for s in range(0, n, block):
            own = onehot[s : s + block]
            before = dot(tri, own.astype(BF)) + carry
            slot = jnp.sum(before * own, 1, keepdims=True).astype(jnp.int32)
            col_ref[s : s + block] = ids[s : s + block] * slots + slot
            carry += jnp.sum(own, 0, keepdims=True)
        row_ref[...] = jnp.broadcast_to(col_ref[...].astype(F32), (n, 128)).T[:8].astype(jnp.int32)

    out = pick_places(row_ref, places, step, rows_ref)
    out_ref[...] = out

    @pl.when(step < cut)
    def _():
        early_ref[...] = out

    @pl.when(step >= cut)
    def _():
        late_ref[...] = out


def pick_places(row_ref, places, step, rows_ref):
    n = rows_ref.shape[0]
    place = lax.broadcasted_iota(jnp.int32, (places, n), 0) + places * step
    return dot((place == row_ref[0:1, :]).astype(BF), rows_ref[...]).astype(BF)


def dispatch(ids, rows, experts, slots, cut, block=256):
    n, width = rows.shape
    places = experts * slots
    steps = places // block
    return pl.pallas_call(
        functools.partial(dispatch_kernel, slots=slots, block=block, cut=cut),
        grid=(steps,),
        in_specs=[
            pl.BlockSpec((n, 1), lambda j: (0, 0)),
            pl.BlockSpec((n, width), lambda j: (0, 0), pipeline_mode=pl.Buffered(1)),
        ],
        out_specs=(
            pl.BlockSpec((n, 1), lambda j: (0, 0)),
            pl.BlockSpec((8, n), lambda j: (0, 0)),
            pl.BlockSpec((block, width), lambda j: (j, 0)),
            pl.BlockSpec((block, width), lambda j: (jnp.minimum(j, cut - 1), 0)),
            pl.BlockSpec((block, width), lambda j: (jnp.maximum(j - cut, 0), 0)),
        ),
        out_shape=(
            jax.ShapeDtypeStruct((n, 1), jnp.int32),
            jax.ShapeDtypeStruct((8, n), jnp.int32),
            jax.ShapeDtypeStruct((places, width), BF),
            jax.ShapeDtypeStruct((cut * block, width), BF),
            jax.ShapeDtypeStruct((places - cut * block, width), BF),
        ),
        compiler_params=pltpu.CompilerParams(vmem_limit_bytes=40 << 20),
        cost_estimate=pl.CostEstimate(flops=2 * n * places * width, bytes_accessed=2 * (n + places) * width, transcendentals=0),
        name="dispatch",
    )(ids, rows)


def unit_rows(hidden):
    centred = hidden - jnp.mean(hidden, -1, keepdims=True)
    return centred * lax.rsqrt(jnp.mean(centred * centred, -1, keepdims=True) + 1e-05)


def project_kernel(tok_ref, gain_ref, shift_ref, wq_ref, bq_ref, wk_ref, wv_ref, bv_ref, act_ref, q_ref, k_ref, v_ref, *, scale):
    act = (unit_rows(tok_ref[...].astype(F32)) * gain_ref[...] + shift_ref[...]).astype(BF)
    act_ref[...] = act
    q_ref[...] = ((dot(act, wq_ref[...]) + bq_ref[...]).astype(BF).astype(F32) * scale).astype(BF)
    k_ref[...] = dot(act, wk_ref[...]).astype(BF)
    v_ref[...] = (dot(act, wv_ref[...]) + bv_ref[...]).astype(BF)


def project(tokens, gain, shift, wq, bq, wk, wv, bv, scale, block=256):
    n, width = tokens.shape
    rows = pl.BlockSpec((block, width), lambda i: (i, 0))
    line = pl.BlockSpec((1, width), lambda i: (0, 0))
    matrix = pl.BlockSpec((width, width), lambda i: (0, 0), pipeline_mode=pl.Buffered(1))
    return pl.pallas_call(
        functools.partial(project_kernel, scale=scale),
        grid=(n // block,),
        in_specs=[rows, line, line, matrix, line, matrix, matrix, line],
        out_specs=(rows,) * 4,
        out_shape=(jax.ShapeDtypeStruct((n, width), BF),) * 4,
        compiler_params=pltpu.CompilerParams(vmem_limit_bytes=40 << 20),
        cost_estimate=pl.CostEstimate(flops=6 * n * width * width, bytes_accessed=16 * n * width, transcendentals=0),
        name="project",
    )(tokens, gain, shift, wq, bq, wk, wv, bv)


def after_attn_kernel(
    mixed_ref, tok_ref, w_ref, bias_ref, gain_ref, shift_ref, row_ref, hidden_ref, out_ref, act_ref, *, first, block
):
    step = pl.program_id(0)
    places = out_ref.shape[0]
    for i in range(first):

        @pl.when(step == i)
        def _(i=i):
            hidden = tok_ref[...].astype(F32) + dot(mixed_ref[...], w_ref[...]) + bias_ref[...]
            hidden_ref[...] = hidden
            act_ref[i * block : (i + 1) * block] = (unit_rows(hidden) * gain_ref[...] + shift_ref[...]).astype(BF)

    @pl.when(step >= first)
    def _():
        out_ref[...] = pick_places(row_ref, places, step - first, act_ref)


def after_attn(mixed, tokens, w, bias, gain, shift, target, places, block=256):
    n, width = tokens.shape
    first = n // block
    rows = pl.BlockSpec((block, width), lambda i: (jnp.minimum(i, first - 1), 0))
    line = pl.BlockSpec((1, width), lambda i: (0, 0))
    return pl.pallas_call(
        functools.partial(after_attn_kernel, first=first, block=block),
        grid=(first + places // block,),
        in_specs=[
            rows,
            rows,
            pl.BlockSpec((width, width), lambda i: (0, 0), pipeline_mode=pl.Buffered(1)),
            line,
            line,
            line,
            pl.BlockSpec((8, n), lambda i: (0, 0)),
        ],
        out_specs=(rows, pl.BlockSpec((block, width), lambda i: (jnp.maximum(i - first, 0), 0))),
        out_shape=(jax.ShapeDtypeStruct((n, width), F32), jax.ShapeDtypeStruct((places, width), BF)),
        scratch_shapes=[pltpu.VMEM((n, width), BF)],
        compiler_params=pltpu.CompilerParams(vmem_limit_bytes=40 << 20),
        cost_estimate=pl.CostEstimate(flops=4 * n * width * width, bytes_accessed=12 * n * width, transcendentals=0),
        name="after_attn",
    )(mixed, tokens, w, bias, gain, shift, target)


def combine_kernel(target_ref, back_ref, hidden_ref, grad_ref, out_ref, grad_out_ref):
    rows, places = hidden_ref.shape[0], back_ref.shape[0]
    pick = (lax.broadcasted_iota(jnp.int32, (rows, places), 1) == target_ref[...]).astype(BF)
    out_ref[...] = (hidden_ref[...] + dot(pick, back_ref[...])).astype(BF)
    grad_out_ref[...] = grad_ref[...]


def combine(target, back, hidden, grad, block=256):
    n, width = hidden.shape
    rows = pl.BlockSpec((block, width), lambda i: (i, 0))
    return pl.pallas_call(
        combine_kernel,
        grid=(n // block,),
        in_specs=[
            pl.BlockSpec((block, 1), lambda i: (i, 0)),
            pl.BlockSpec(back.shape, lambda i: (0, 0), pipeline_mode=pl.Buffered(1)),
            rows,
            rows,
        ],
        out_specs=(rows, rows),
        out_shape=(jax.ShapeDtypeStruct((n, width), BF), jax.ShapeDtypeStruct((n, width), F32)),
        compiler_params=pltpu.CompilerParams(vmem_limit_bytes=40 << 20),
        name="combine",
    )(target, back, hidden, grad)


def after_experts_kernel(
    target_ref, home_ref, cot_ref, hidden_ref, gain_ref, w_out_ref, gh_ref, ga_ref, do_ref, sums_ref
):
    rows, width = cot_ref.shape
    places = home_ref.shape[0]
    pick = (lax.broadcasted_iota(jnp.int32, (rows, places), 1) == target_ref[...]).astype(BF)
    d = dot(pick, home_ref[...])
    hidden = hidden_ref[...]
    centred = hidden - jnp.mean(hidden, -1, keepdims=True)
    inv = lax.rsqrt(jnp.mean(centred * centred, -1, keepdims=True) + 1e-05)
    unit = centred * inv
    scaled = d * gain_ref[...]
    mean_one = jnp.mean(scaled, -1, keepdims=True)
    mean_two = jnp.mean(scaled * unit, -1, keepdims=True)
    grad = cot_ref[...].astype(F32) + inv * (scaled - mean_one - unit * mean_two)
    gh_ref[...] = grad
    low = grad.astype(BF)
    ga_ref[...] = low
    do_ref[...] = dot_nt(low, w_out_ref[...]).astype(BF)
    parts = [jnp.sum(low.astype(F32), 0, keepdims=True), jnp.sum(d * unit, 0, keepdims=True), jnp.sum(d, 0, keepdims=True)]
    parts = jnp.concatenate(parts + [jnp.zeros((8 - len(parts), width), F32)], 0)

    @pl.when(pl.program_id(0) == 0)
    def _():
        sums_ref[...] = parts

    @pl.when(pl.program_id(0) > 0)
    def _():
        sums_ref[...] += parts


def after_experts(target, home, cot, hidden, gain, w_out, block=256):
    n, width = cot.shape
    places = home.shape[0]
    rows = pl.BlockSpec((block, width), lambda i: (i, 0))
    once = pl.Buffered(1)
    return pl.pallas_call(
        after_experts_kernel,
        grid=(n // block,),
        in_specs=[
            pl.BlockSpec((block, 1), lambda i: (i, 0)),
            pl.BlockSpec((places, width), lambda i: (0, 0), pipeline_mode=once),
            rows,
            rows,
            pl.BlockSpec((1, width), lambda i: (0, 0)),
            pl.BlockSpec((width, width), lambda i: (0, 0), pipeline_mode=once),
        ],
        out_specs=(rows, rows, rows, pl.BlockSpec((8, width), lambda i: (0, 0))),
        out_shape=(
            jax.ShapeDtypeStruct((n, width), F32),
            jax.ShapeDtypeStruct((n, width), BF),
            jax.ShapeDtypeStruct((n, width), BF),
            jax.ShapeDtypeStruct((8, width), F32),
        ),
        compiler_params=pltpu.CompilerParams(vmem_limit_bytes=50 << 20),
        name="after_experts",
    )(target, home, cot, hidden, gain, w_out)


def dense_grads_kernel(*refs, ep_bits, rep_bits, own, rblk, steps):
    (act_ref, mixed_ref, ga_ref, dq_ref, dk_ref, dv_ref, wq_ref, wk_ref, wv_ref, tok_ref, gh_ref, gain_ref, sums_ref) = refs[:13]
    bias_ref = refs[13]
    out_ref, gt_ref, vec_out, bias_out = refs[14:18]
    at_ref, mt_ref, da_ref, x_ref = refs[18:22]
    bits = ep_bits + rep_bits
    got = refs[22 : 22 + bits]
    vec_got, vec_sum, bias_got, bias_sum, send, recv, vsend, vrecv, bsend, brecv = refs[22 + bits :]
    step = pl.program_id(0)
    n = act_ref.shape[0]
    width = act_ref.shape[1]
    block = ga_ref.shape[1]
    ep, rep = 1 << ep_bits, 1 << rep_bits
    me_z = lax.axis_index("rep")
    me = lax.axis_index("ep")

    def bit(b):
        return lax.rem(me // (1 << b), 2) if b < ep_bits else lax.rem(me_z // (1 << (b - ep_bits)), 2)

    def flip(b):
        change = 1 - 2 * bit(b)
        return (me_z, me + change * (1 << b)) if b < ep_bits else (me_z + change * (1 << (b - ep_bits)), me)

    def order(c):
        rest = list(range(1, ep_bits))
        return [0] + (rest if c % 2 == 0 else rest[::-1]) + list(range(ep_bits, bits))

    def copy(src, dst, s, r, peer):
        return pltpu.make_async_remote_copy(
            src_ref=src, dst_ref=dst, send_sem=s, recv_sem=r, device_id=peer, device_id_type=pl.DeviceIdType.MESH
        )

    def cut(c, stage, value):
        done = order(c)[:stage]
        left = [b for b in range(ep_bits - 1, -1, -1) if b not in done]
        left += [b for b in range(bits - 1, ep_bits - 1, -1) if b not in done]
        index = [slice(None)] * len(left)
        index[left.index(order(c)[stage])] = value
        return tuple(index)

    def held(c, stage):
        return x_ref.at[c] if stage == 0 else got[stage - 1].at[c]

    def stage_copy(c, stage):
        b = order(c)[stage]
        return copy(
            held(c, stage).at[cut(c, stage, 1 - bit(b))], got[stage].at[c], send.at[c, stage], recv.at[c, stage], flip(b)
        )

    def advance(c, stage):
        stage_copy(c, stage).wait()
        keep = held(c, stage)[cut(c, stage, bit(order(c)[stage]))]
        if stage + 1 < bits:
            got[stage][c] += keep
            stage_copy(c, stage + 1).start()
        else:
            out_ref[:, :, c * block : (c + 1) * block] = got[stage][c].astype(F32) + keep.astype(F32)

    def small_copy(k, got_ref, sum_ref, first, s, r):
        return copy(sum_ref.at[k - first], got_ref.at[k - first], s.at[k - first], r.at[k - first], flip(k))

    def vec_copy(k):
        return small_copy(k, vec_got, vec_sum, 0, vsend, vrecv)

    def bias_copy(k):
        return small_copy(k, bias_got, bias_sum, ep_bits, bsend, brecv)

    @pl.when(step == 0)
    def _():
        barrier = pltpu.get_barrier_semaphore()
        for b in range(bits):
            pl.semaphore_signal(barrier, inc=1, device_id=flip(b), device_id_type=pl.DeviceIdType.MESH)
        pl.semaphore_wait(barrier, bits)
        bias_sum[0] = bias_ref[...]
        bias_copy(ep_bits).start()
        at_ref[...] = act_ref[...].T
        mt_ref[...] = mixed_ref[...].T

    def product(c, w):
        left, right = ((at_ref, dq_ref), (at_ref, dk_ref), (at_ref, dv_ref), (mt_ref, ga_ref))[w]
        g = dot(left[...], right[...]).astype(BF)
        for r in range(rep):
            for e in range(ep):
                start = (r * ep + e) * own
                where = tuple((e >> b) & 1 for b in range(ep_bits - 1, -1, -1))
                where += tuple((r >> b) & 1 for b in range(rep_bits - 1, -1, -1))
                x_ref[(c,) + where + (w,)] = g[start : start + own]

    def rows_part(c):
        for s in range(0, n, rblk):
            rs = slice(s, s + rblk)
            part = dot_nt(dq_ref[rs], wq_ref[...]) + dot_nt(dk_ref[rs], wk_ref[...]) + dot_nt(dv_ref[rs], wv_ref[...])
            if c == 0:
                da_ref[rs] = part
            else:
                da_ref[rs] += part

    def finish_rows():
        total_n = jnp.zeros((1, width), F32)
        total_d = jnp.zeros((1, width), F32)
        for s in range(0, n, rblk):
            rs = slice(s, s + rblk)
            d = da_ref[rs]
            hidden = tok_ref[rs].astype(F32)
            centred = hidden - jnp.mean(hidden, -1, keepdims=True)
            inv = lax.rsqrt(jnp.mean(centred * centred, -1, keepdims=True) + 1e-05)
            unit = centred * inv
            scaled = d * gain_ref[...]
            mean_one = jnp.mean(scaled, -1, keepdims=True)
            mean_two = jnp.mean(scaled * unit, -1, keepdims=True)
            gt_ref[rs] = gh_ref[rs] + inv * (scaled - mean_one - unit * mean_two)
            total_n += jnp.sum(d * unit, 0, keepdims=True)
            total_d += jnp.sum(d, 0, keepdims=True)
        return total_n, total_d

    def vec_step(k):
        vec_copy(k).wait()
        vec_sum[k + 1] = vec_sum[k] + vec_got[k]
        if k + 1 < bits:
            vec_copy(k + 1).start()

    for c in range(steps):

        @pl.when(step == c)
        def _(c=c):
            cols = slice(c * block, (c + 1) * block)
            vec_sum[0, 2:3, cols] = jnp.sum(dq_ref[...].astype(F32), 0, keepdims=True)
            vec_sum[0, 3:4, cols] = jnp.sum(dv_ref[...].astype(F32), 0, keepdims=True)
            vec_sum[0, 4:8, cols] = sums_ref[0:4, cols]
            product(c, 0)
            product(c, 1)
            if c >= 2:
                advance(c - 2, 1)
            product(c, 2)
            product(c, 3)
            stage_copy(c, 0).start()
            if 1 <= c <= rep_bits:
                k = c - 1
                bias_copy(ep_bits + k).wait()
                bias_sum[k + 1] = bias_sum[k] + bias_got[k]
                if k + 1 < rep_bits:
                    bias_copy(ep_bits + k + 1).start()
            if c >= 3:
                advance(c - 3, 2)
            rows_part(c)
            advance(c, 0)
            if c == steps - 1:
                total_n, total_d = finish_rows()
                vec_sum[0, 0:1] = total_n
                vec_sum[0, 1:2] = total_d
                vec_copy(0).start()
                waves = {}
                for d in range(steps):
                    for stage in range(1, bits):
                        if not ((stage == 1 and d + 2 < steps) or (stage == 2 and d + 3 < steps)):
                            waves.setdefault(d + stage, []).append((d, stage))
                k = 0
                for wave in sorted(waves):
                    for d, stage in waves[wave]:
                        advance(d, stage)
                    if k < bits:
                        vec_step(k)
                        k += 1
                for k in range(k, bits):
                    vec_step(k)
                vec_out[...] = vec_sum[bits]
                bias_out[...] = bias_sum[rep_bits]


def dense_grads(act, mixed, ga, dq, dk, dv, wq, wk, wv, tokens, gh, gain, sums, bias, rep, ep, block=256, rblk=256):
    n, width = act.shape
    own = width // (rep * ep)
    ep_bits, rep_bits = ep.bit_length() - 1, rep.bit_length() - 1
    bits = ep_bits + rep_bits
    steps = width // block
    once = pl.Buffered(1)
    whole = pl.BlockSpec((n, width), lambda j: (0, 0), pipeline_mode=once)
    cols = pl.BlockSpec((n, block), lambda j: (0, j))
    eight = pl.BlockSpec((8, width), lambda j: (0, 0))
    scratch = [
        pltpu.VMEM((width, n), BF),
        pltpu.VMEM((width, n), BF),
        pltpu.VMEM((n, width), F32),
        pltpu.VMEM((steps,) + (2,) * bits + (4, own, block), BF),
    ]
    scratch += [pltpu.VMEM((steps,) + (2,) * (bits - 1 - k) + (4, own, block), BF) for k in range(bits)]
    scratch += [
        pltpu.VMEM((bits, 8, width), F32),
        pltpu.VMEM((bits + 1, 8, width), F32),
        pltpu.VMEM((rep_bits, 8, width), F32),
        pltpu.VMEM((rep_bits + 1, 8, width), F32),
        pltpu.SemaphoreType.DMA((steps, bits)),
        pltpu.SemaphoreType.DMA((steps, bits)),
        pltpu.SemaphoreType.DMA((bits,)),
        pltpu.SemaphoreType.DMA((bits,)),
        pltpu.SemaphoreType.DMA((rep_bits,)),
        pltpu.SemaphoreType.DMA((rep_bits,)),
    ]
    return pl.pallas_call(
        functools.partial(dense_grads_kernel, ep_bits=ep_bits, rep_bits=rep_bits, own=own, rblk=rblk, steps=steps),
        grid=(steps,),
        in_specs=[whole, whole, cols, cols, cols, cols, cols, cols, cols, whole, whole, pl.BlockSpec((1, width), lambda j: (0, 0)), eight, eight],
        out_specs=(
            pl.BlockSpec((4, own, width), lambda j: (0, 0, 0)),
            pl.BlockSpec((n, width), lambda j: (0, 0), pipeline_mode=once),
            eight,
            eight,
        ),
        out_shape=(
            jax.ShapeDtypeStruct((4, own, width), F32),
            jax.ShapeDtypeStruct((n, width), F32),
            jax.ShapeDtypeStruct((8, width), F32),
            jax.ShapeDtypeStruct((8, width), F32),
        ),
        scratch_shapes=scratch,
        compiler_params=pltpu.CompilerParams(vmem_limit_bytes=62 << 20, collective_id=1, has_side_effects=True),
        name="dense_grads",
    )(act, mixed, ga, dq, dk, dv, wq, wk, wv, tokens, gh, gain, sums, bias)


def per_device(
    tokens,
    cotangent,
    lengths,
    expert_ids,
    norm1_gain,
    norm1_bias,
    w_query,
    b_query,
    w_key,
    w_value,
    b_value,
    w_out,
    b_out,
    norm2_gain,
    norm2_bias,
    w_in,
    b_in,
    w_back,
    b_back,
):
    row_count, width = tokens.shape
    head_dim = width // HEADS
    ep = lax.axis_size("ep")
    rep = lax.axis_size("rep")
    slots = 5 * row_count // (4 * ep)
    places = ep * slots
    ff = w_in.shape[2]
    w_first = w_in[0]
    w_second = w_back[0]

    def exchange(rows):
        sent = lax.all_to_all(rows.reshape(ep, slots, width), "ep", 0, 0, tiled=True)
        return sent.reshape(places, width)

    at = lax.axis_index("rep")
    swap = [(i, i ^ 1) for i in range(rep)]
    target, target_row, grad_send, early, tail = dispatch(expert_ids, cotangent, ep, slots, 3)
    grad_rows = exchange(grad_send)
    early = lax.ppermute(early, "rep", swap)
    act_a, queries, keys, values = project(
        tokens, norm1_gain[None], norm1_bias[None], w_query, b_query[None], w_key, w_value, b_value[None], head_dim**-0.5
    )
    mixed, lse = attn_fwd(queries, keys, values, lengths)
    mixed, grad_rows, early, tail = lax.optimization_barrier((mixed, grad_rows, early, tail))
    late = lax.ppermute(tail, "rep", swap)
    hidden_one, rows_out = after_attn(
        mixed, tokens, w_out, b_out[None], norm2_gain[None], norm2_bias[None], target_row, places
    )
    rows_in = exchange(rows_out)
    rows_in, both = lax.optimization_barrier((rows_in, jnp.concatenate([early, late], 0)))
    grad_pair = exchange(both)
    rows_pair = lax.ppermute(rows_in, "rep", swap)
    own_fn = functools.partial(expert_own, tile=ff // 4)
    own_out = jax.eval_shape(own_fn, rows_in, grad_rows, w_first, b_in, w_second)
    own_all = lax.cond(
        lengths[0] > 0,
        own_fn,
        lambda *_: tuple(jnp.zeros(x.shape, x.dtype) for x in own_out),
        rows_in,
        grad_rows,
        w_first,
        b_in,
        w_second,
    )
    active, grad_inner, g_bias_first, grad_input = own_all
    grad_home = exchange(grad_input)
    half = (at & 1).astype(jnp.int32)[None]
    turned = turn(half, rows_in, grad_rows, grad_pair, rep)
    active, grad_inner, g_bias_first, rows_pair, grad_pair, turned = lax.optimization_barrier(
        (active, grad_inner, g_bias_first, rows_pair, grad_pair, turned)
    )

    def pair(tile_of, steps):
        return expert_pair(
            half, turned, rows_pair, grad_pair, w_first, b_in, w_second, active, grad_inner, tile_of, steps, ff // 8, rep
        )

    groups = [[0, 2], [1, 3]]
    part_0 = pair(early_tile, 2)
    rows_pair, grad_home, active, part_0 = lax.optimization_barrier((rows_pair, grad_home, active, part_0))
    sum_0 = lax.psum_scatter(part_0, "rep", scatter_dimension=0, axis_index_groups=groups, tiled=True)
    result = (dot(active, w_second) + b_back[0]).astype(BF)
    part_1 = pair(late_tile, 6)
    sum_1 = lax.psum_scatter(part_1, "rep", scatter_dimension=0, axis_index_groups=groups, tiled=True)
    returned = exchange(result)
    g_bias_second = jnp.sum(grad_rows.astype(F32), 0)

    def remainder(grad_home, g_bias_first, g_bias_second):
        grad_hidden, grad_attn, grad_mixed, sums = after_experts(
            target, grad_home, cotangent, hidden_one, norm2_gain[None], w_out
        )
        grad_q, grad_k, grad_v = attn_bwd(queries, keys, values, mixed, grad_mixed, lse, lengths)
        bias = jnp.concatenate([g_bias_first.reshape(ff // width, width), g_bias_second[None]], 0)
        bias = jnp.pad(bias, ((0, 8 - bias.shape[0]), (0, 0)))
        return dense_grads(
            act_a, mixed, grad_attn, grad_q, grad_k, grad_v, w_query, w_key, w_value, tokens, grad_hidden,
            norm1_gain[None], sums, bias, rep, ep,
        )

    own = width // (rep * ep)
    own_ff, own_width = ff // rep, width // rep
    args = (grad_home, g_bias_first, g_bias_second)
    shapes = jax.eval_shape(remainder, *args)
    dense, grad_tokens, small, grad_bias = lax.cond(
        lengths[0] > 0, remainder, lambda *_: jax.tree.map(lambda x: jnp.zeros(x.shape, x.dtype), shapes), *args
    )
    returned, grad_tokens = lax.optimization_barrier((returned, grad_tokens))
    block_out, grad_tokens = combine(target, returned, hidden_one, grad_tokens)

    place = at * ep + lax.axis_index("ep")
    small = lax.dynamic_slice_in_dim(small, place * own, own, 1)
    rows_bias = own_ff // width
    out_bias_first = lax.dynamic_slice_in_dim(grad_bias, at * rows_bias, rows_bias, 0).reshape(1, own_ff)
    out_bias_second = lax.dynamic_slice(grad_bias, (ff // width, at * own_width), (1, own_width))
    out_first, out_second = unpack_grads(half, sum_0[0], sum_1[0], ff // 8, ff)
    out_first, out_second = out_first[None], out_second[None]
    return (
        block_out,
        grad_tokens,
        small[0],
        small[1],
        dense[0],
        small[2],
        dense[1],
        dense[2],
        small[3],
        dense[3],
        small[4],
        small[5],
        small[6],
        out_first,
        out_bias_first,
        out_second,
        out_bias_second,
    )


def solution(mesh):
    return jax.shard_map(
        per_device,
        mesh=mesh,
        in_specs=(
            P(("rep", "ep"), None),
            P(("rep", "ep"), None),
            P(("rep", "ep")),
            P(("rep", "ep"), None),
            P(),
            P(),
            P(),
            P(),
            P(),
            P(),
            P(),
            P(),
            P(),
            P(),
            P(),
            P("ep", None, None),
            P("ep", None),
            P("ep", None, None),
            P("ep", None),
        ),
        out_specs=(
            P(("rep", "ep"), None),
            P(("rep", "ep"), None),
            P(("rep", "ep")),
            P(("rep", "ep")),
            P(("rep", "ep"), None),
            P(("rep", "ep")),
            P(("rep", "ep"), None),
            P(("rep", "ep"), None),
            P(("rep", "ep")),
            P(("rep", "ep"), None),
            P(("rep", "ep")),
            P(("rep", "ep")),
            P(("rep", "ep")),
            P("ep", "rep", None),
            P("ep", "rep"),
            P("ep", "rep", None),
            P("ep", "rep"),
        ),
        check_vma=False,
    )
```

```python
import functools

import jax
import jax.numpy as jnp
from jax import lax
from jax.experimental import pallas as pl
from jax.experimental.pallas import tpu as pltpu
from jax.sharding import PartitionSpec as P

HEADS = 16
BF = jnp.bfloat16
F32 = jnp.float32
LOG2E = 1.4426950408889634
NEG = -1e30


def dot(left, right):
    return jnp.dot(left, right, preferred_element_type=F32)


def dot_nt(left, right):
    return lax.dot_general(left, right, (((1,), (1,)), ((), ())), preferred_element_type=F32)


def dot_tn(left, right):
    return lax.dot_general(left, right, (((0,), (0,)), ((), ())), preferred_element_type=F32)


def attn_fwd_kernel(len_ref, q_ref, k_ref, v_ref, o_ref, lse_ref, ot_ref, *, blk):
    n, lanes = q_ref.shape
    half = lanes//2
    length = len_ref[0]
    k = k_ref[...].astype(F32)
    lane = lax.broadcasted_iota(jnp.int32,(n,lanes),1)
    row = lax.broadcasted_iota(jnp.int32,(n,lanes),0)
    bias = jnp.where(row<length, 0.0, NEG)
    k_a = jnp.where(lane<half, k, jnp.where(lane==half, bias, 0.0)).astype(BF)
    k_b = jnp.where(lane>=half, k, jnp.where(lane==0, bias, 0.0)).astype(BF)
    qt = q_ref[...].T
    vt = v_ref[...].T
    trow = lax.broadcasted_iota(jnp.int32,(lanes,n),0)
    qt32 = qt.astype(F32)
    qt_a = jnp.where(trow==half, 1.0, qt32).astype(BF)
    qt_b = jnp.where(trow==0, 1.0, qt32).astype(BF)
    tri = lax.broadcasted_iota(jnp.int32,(blk,blk),0) <= lax.broadcasted_iota(jnp.int32,(blk,blk),1)
    ones = jnp.ones((16,n),BF)
    for h,(kk,qq) in enumerate(((k_a,qt_a),(k_b,qt_b))):
        v_ext = jnp.concatenate([vt[h*half:(h+1)*half], ones],0)
        for i in range(n//blk):
            cols = slice(i*blk,(i+1)*blk)
            qb = qq[:,cols]
            diag = jnp.where(tri, dot(kk[cols],qb), NEG)
            if i:
                past = dot(kk[:i*blk],qb)
                top = jnp.maximum(jnp.max(past,0,keepdims=True),jnp.max(diag,0,keepdims=True))
                p = jnp.concatenate([jnp.exp2((past-top)*LOG2E).astype(BF),jnp.exp2((diag-top)*LOG2E).astype(BF)],0)
            else:
                top = jnp.max(diag,0,keepdims=True)
                p = jnp.exp2((diag-top)*LOG2E).astype(BF)
            r = dot(v_ext[:,:(i+1)*blk],p)
            total = r[half:half+1]
            ot_ref[h*half:(h+1)*half,cols] = r[:half]/total
            lse_ref[0,h:h+1,cols] = top + jnp.log(total)
    o_ref[...] = ot_ref[...].T.astype(BF)

def attn_fwd(q, k, v, length, blk=512):
    n, d = q.shape
    pairs = d // 128
    spec = pl.BlockSpec((n, 128), lambda h: (0, h))
    return pl.pallas_call(
        functools.partial(attn_fwd_kernel, blk=blk),
        grid=(pairs,),
        in_specs=[pl.BlockSpec(memory_space=pltpu.SMEM), spec, spec, spec],
        out_specs=(spec, pl.BlockSpec((1, 2, n), lambda h: (h, 0, 0))),
        out_shape=(jax.ShapeDtypeStruct((n, d), BF), jax.ShapeDtypeStruct((pairs, 2, n), F32)),
        scratch_shapes=[pltpu.VMEM((128, n), F32)],
        compiler_params=pltpu.CompilerParams(vmem_limit_bytes=50 << 20),
        cost_estimate=pl.CostEstimate(flops=8 * n * n * d, bytes_accessed=8 * n * d, transcendentals=8 * n * n),
        name="attn_fwd",
    )(length, q, k, v)


def split3(x):
    a=x.astype(BF).astype(F32); r=x-a
    b=r.astype(BF).astype(F32); c=r-b
    return a,b,c

def attn_bwd_kernel(len_ref, q_ref, k_ref, v_ref, o_ref, do_ref, lse_ref, dq_ref, dk_ref, dv_ref, dqt_ref, dk_acc, dv_acc, *, blk):
    n, lanes = q_ref.shape
    half = lanes//2
    length = len_ref[0]
    lane = lax.broadcasted_iota(jnp.int32,(n,lanes),1)
    row = lax.broadcasted_iota(jnp.int32,(n,lanes),0)
    trow = lax.broadcasted_iota(jnp.int32,(lanes,n),0)
    bias = jnp.where(row<length, 0.0, NEG)
    q = q_ref[...].astype(F32); k = k_ref[...].astype(F32); v=v_ref[...].astype(F32); do=do_ref[...].astype(F32)
    kt = k_ref[...].T
    qt = q_ref[...].T.astype(F32)
    dot_t = do_ref[...].T.astype(F32)
    ot = o_ref[...].T.astype(F32)
    prod = dot_t*ot
    heads=[]
    for h in range(2):
        own = (lane<half) if h==0 else (lane>=half)
        base = half if h==0 else 0
        delta = jnp.sum(prod[h*half:(h+1)*half],0,keepdims=True)
        lse = lse_ref[0,h:h+1,:]
        l1,l2,l3 = split3(-lse)
        d1,d2,d3 = split3(-delta)
        one = jnp.where((lane>=base+1)&(lane<=base+3),1.0,0.0)
        k_x = jnp.where(own,k,jnp.where(lane==base,bias,one)).astype(BF)
        v_x = jnp.where(own,v,one).astype(BF)
        q_x = jnp.where(trow==base,1.0,jnp.where(trow==base+1,l1,jnp.where(trow==base+2,l2,jnp.where(trow==base+3,l3,qt)))).astype(BF)
        d_x = jnp.where(trow==base+1,d1,jnp.where(trow==base+2,d2,jnp.where(trow==base+3,d3,dot_t))).astype(BF)
        q_own = jnp.where(own,q,0.0).astype(BF)
        do_own = jnp.where(own,do,0.0).astype(BF)
        heads.append((k_x,v_x,q_x,d_x,q_own,do_own))
    tri = lax.broadcasted_iota(jnp.int32,(blk,blk),0) <= lax.broadcasted_iota(jnp.int32,(blk,blk),1)
    steps=n//blk
    for i in reversed(range(steps)):
        cols = slice(i*blk,(i+1)*blk)
        ps=[];dss=[]
        for h in range(2):
            k_x,v_x,q_x,d_x,q_own,do_own=heads[h]
            qb=q_x[:,cols]; db=d_x[:,cols]
            p_d = jnp.exp2(jnp.where(tri,dot(k_x[cols],qb),NEG)*LOG2E)
            ds_d = p_d*dot(v_x[cols],db)
            if i:
                p_p = jnp.exp2(dot(k_x[:i*blk],qb)*LOG2E)
                ds_p = p_p*dot(v_x[:i*blk],db)
                p=jnp.concatenate([p_p.astype(BF),p_d.astype(BF)],0)
                ds=jnp.concatenate([ds_p.astype(BF),ds_d.astype(BF)],0)
            else:
                p=p_d.astype(BF); ds=ds_d.astype(BF)
            dqt_ref[h*half:(h+1)*half,cols]=dot(kt[h*half:(h+1)*half,:(i+1)*blk],ds)
            ps.append(p);dss.append(ds)
        dv_new = dot(ps[0],heads[0][5][cols])+dot(ps[1],heads[1][5][cols])
        dk_new = dot(dss[0],heads[0][4][cols])+dot(dss[1],heads[1][4][cols])
        if i==steps-1:
            dv_acc[...]=dv_new; dk_acc[...]=dk_new
        else:
            dv_acc[:(i+1)*blk]+=dv_new; dk_acc[:(i+1)*blk]+=dk_new
    scale=half**-0.5
    dq_ref[...]=(dqt_ref[...]*scale).T.astype(BF)
    dk_ref[...]=dk_acc[...].astype(BF)
    dv_ref[...]=dv_acc[...].astype(BF)

C0=0.7978845608028654; C1=C0*0.044715

def act_both(z):
    z2=z*z
    a=C1*z2+C0
    t=jnp.tanh(z*a)
    h=0.5*t+0.5
    u=z*h
    q=6.0*a-4.0*C0
    return u, h+u*(1.0-h)*q

def expert_own_kernel(
    b_ref, gy_ref, w1_ref, b1_ref, w2_ref, u_ref, dz_ref, gb1_ref, db_ref, gb2_ref, acc_ref, *, rblk
):
    step = pl.program_id(0)
    rows = b_ref.shape[0]
    w1 = w1_ref[...]
    w2 = w2_ref[...]
    bias = b1_ref[...]
    total = None
    for s in range(0, rows, rblk):
        rs = slice(s, s + rblk)
        u, slope = act_both(dot(b_ref[rs, :], w1) + bias)
        u_ref[rs, :] = u.astype(BF)
        dz = dot_nt(gy_ref[rs, :], w2) * slope
        dz_ref[rs, :] = dz.astype(BF)
        part = jnp.sum(dz, 0, keepdims=True)
        total = part if total is None else total + part
    gb1_ref[...] = total

    @pl.when(step == 0)
    def _():
        total = jnp.zeros_like(gb2_ref)
        for s in range(0, rows, rblk):
            rs = slice(s, s + rblk)
            acc_ref[rs, :] = dot_nt(dz_ref[rs, :], w1)
            total += jnp.sum(gy_ref[rs, :].astype(F32), 0, keepdims=True)
        gb2_ref[...] = total

    @pl.when(step > 0)
    def _():
        for s in range(0, rows, rblk):
            rs = slice(s, s + rblk)
            acc_ref[rs, :] += dot_nt(dz_ref[rs, :], w1)

    @pl.when(step == pl.num_programs(0) - 1)
    def _():
        db_ref[...] = acc_ref[...].astype(BF)


def expert_own(b, gy, w1, b1, w2, tile, rblk=256):
    rows, d = b.shape
    ff = w1.shape[1]
    whole = pl.BlockSpec((rows, d), lambda j: (0, 0), pipeline_mode=pl.Buffered(1))
    return pl.pallas_call(
        functools.partial(expert_own_kernel, rblk=rblk),
        grid=(ff // tile,),
        in_specs=[
            whole,
            whole,
            pl.BlockSpec((d, tile), lambda j: (0, j)),
            pl.BlockSpec((1, tile), lambda j: (0, j)),
            pl.BlockSpec((tile, d), lambda j: (j, 0)),
        ],
        out_specs=(
            pl.BlockSpec((rows, tile), lambda j: (0, j)),
            pl.BlockSpec((rows, tile), lambda j: (0, j)),
            pl.BlockSpec((1, tile), lambda j: (0, j)),
            pl.BlockSpec((rows, d), lambda j: (0, 0)),
            pl.BlockSpec((1, d), lambda j: (0, 0)),
        ),
        out_shape=(
            jax.ShapeDtypeStruct((rows, ff), BF),
            jax.ShapeDtypeStruct((rows, ff), BF),
            jax.ShapeDtypeStruct((1, ff), F32),
            jax.ShapeDtypeStruct((rows, d), BF),
            jax.ShapeDtypeStruct((1, d), F32),
        ),
        scratch_shapes=[pltpu.VMEM((rows, d), F32)],
        compiler_params=pltpu.CompilerParams(vmem_limit_bytes=60 << 20),
        cost_estimate=pl.CostEstimate(flops=8 * rows * d * ff, bytes_accessed=4 * d * ff, transcendentals=rows * ff),
        name="expert_own",
    )(b, gy, w1, b1, w2)


def turn_kernel(half_ref, bo0_ref, bo1_ref, gyo_ref, gyp_ref, bto_ref, gto_ref, gtp_ref):
    @pl.when(pl.program_id(0) == 0)
    def _():
        bto_ref[...] = bo0_ref[...].T

    @pl.when(pl.program_id(0) == 1)
    def _():
        bto_ref[...] = bo1_ref[...].T

    gto_ref[...] = gyo_ref[...].T
    gtp_ref[...] = gyp_ref[...].T


def turn(half, b, gy, gy_pair, rep):
    rows, d = b.shape
    own = d // rep
    block = d // rep
    cols = pl.BlockSpec((rows, block), lambda j, h: (0, j))
    turned = pl.BlockSpec((block, rows), lambda j, h: (j, 0))
    return pl.pallas_call(
        turn_kernel,
        grid_spec=pltpu.PrefetchScalarGridSpec(
            num_scalar_prefetch=1,
            grid=(rep,),
            in_specs=[
                pl.BlockSpec((rows, own), lambda j, h: (0, h[0])),
                pl.BlockSpec((rows, own), lambda j, h: (0, h[0] + 2)),
                cols,
                cols,
            ],
            out_specs=(pl.BlockSpec((own, rows), lambda j, h: (jnp.minimum(j, 1), 0)), turned, turned),
        ),
        out_shape=(
            jax.ShapeDtypeStruct((2 * own, rows), BF),
            jax.ShapeDtypeStruct((d, rows), BF),
            jax.ShapeDtypeStruct((d, rows), BF),
        ),
        compiler_params=pltpu.CompilerParams(vmem_limit_bytes=40 << 20),
        cost_estimate=pl.CostEstimate(flops=1, bytes_accessed=10 * rows * d, transcendentals=0),
        name="turn",
    )(half, b, b, gy, gy_pair)


def pair_kernel(
    half_ref, bto_ref, bp_ref, gto_ref, gtp_ref, gyp_ref, w1_ref, b1_ref, w2_ref, u_ref, dz_ref,
    out_ref, btp_ref, up_ref, dzp_ref, *, seconds, rblk,
):
    step = pl.program_id(0)
    rows = bp_ref.shape[0]
    own = bto_ref.shape[0] // 2
    tile = w1_ref.shape[1]

    @pl.when(step == 0)
    def _():
        for k in range(2):
            start = pl.multiple_of((half_ref[0] + 2 * k) * own, own)
            btp_ref[k * own : (k + 1) * own] = bp_ref[:, pl.ds(start, own)].T

    w1 = w1_ref[...]
    w2 = w2_ref[...]
    bias = b1_ref[...]
    for s in range(0, rows, rblk):
        rs = slice(s, s + rblk)
        u, slope = act_both(dot(bp_ref[rs, :], w1) + bias)
        up_ref[rs, :] = u.astype(BF)
        dzp_ref[rs, :] = (dot_nt(gyp_ref[rs, :], w2) * slope).astype(BF)
    g1 = (dot(bto_ref[...], dz_ref[...]) + dot(btp_ref[...], dzp_ref[...])).astype(BF)
    per_row = out_ref.shape[2] // tile
    base = 2 * tile // 2
    where = pl.ds(pl.multiple_of(base + own * (step // per_row), own), own)
    column = pl.ds(pl.multiple_of(tile * lax.rem(step, per_row), tile), tile)
    out_ref[0, where, column] = g1[:own]
    out_ref[1, where, column] = g1[own:]

    @pl.when(step < seconds)
    def _():
        g2 = dot(gto_ref[...], u_ref[...]) + dot(gtp_ref[...], up_ref[...])
        out_ref[step, :tile] = g2.astype(BF).T


def expert_pair(half, turned, b_pair, gy_pair, w1, b1, w2, u, dz, tile_of, steps, tile, rep, rblk=256):
    rows, d = b_pair.shape
    own = d // rep
    once = pl.Buffered(1)
    per_row = d // tile
    height = tile + own * (steps // per_row)

    def fixed(shape, index=(0, 0)):
        return pl.BlockSpec(shape, lambda j, h: index, pipeline_mode=once)

    return pl.pallas_call(
        functools.partial(pair_kernel, seconds=2, rblk=rblk),
        grid_spec=pltpu.PrefetchScalarGridSpec(
            num_scalar_prefetch=1,
            grid=(steps,),
            in_specs=[
                fixed((2 * own, rows)),
                fixed((rows, d)),
                fixed((d, rows)),
                fixed((d, rows)),
                fixed((rows, d)),
                pl.BlockSpec((d, tile), lambda j, h: (0, tile_of(j, h[0]))),
                pl.BlockSpec((1, tile), lambda j, h: (0, tile_of(j, h[0]))),
                pl.BlockSpec((tile, d), lambda j, h: (tile_of(j, h[0]), 0)),
                pl.BlockSpec((rows, tile), lambda j, h: (0, tile_of(j, h[0]))),
                pl.BlockSpec((rows, tile), lambda j, h: (0, tile_of(j, h[0]))),
            ],
            out_specs=pl.BlockSpec((2, height, d), lambda j, h: (0, 0, 0), pipeline_mode=once),
            scratch_shapes=[
                pltpu.VMEM((2 * own, rows), BF),
                pltpu.VMEM((rows, tile), BF),
                pltpu.VMEM((rows, tile), BF),
            ],
        ),
        out_shape=jax.ShapeDtypeStruct((2, height, d), BF),
        compiler_params=pltpu.CompilerParams(vmem_limit_bytes=60 << 20),
        cost_estimate=pl.CostEstimate(
            flops=9 * rows * d * tile * steps, bytes_accessed=16 * d * tile * steps, transcendentals=rows * tile * steps
        ),
        name="expert_pair",
    )(half, turned[0], b_pair, turned[1], turned[2], gy_pair, w1, b1, w2, u, dz)


def early_tile(j, h):
    return 2 * h + 4 * j


def late_tile(j, h):
    k = j - 2
    return jnp.where(j < 2, 2 * h + 1 + 4 * j, 2 * (1 - h) + lax.rem(k + 2, 2) + 4 * ((k + 2) // 2 - 1))


def dispatch_kernel(ids_ref, rows_ref, col_ref, row_ref, out_ref, early_ref, late_ref, *, slots, block, cut):
    n = ids_ref.shape[0]
    places = out_ref.shape[0]
    step = pl.program_id(0)

    @pl.when(step == 0)
    def _():
        ids = ids_ref[...]
        lanes = lax.broadcasted_iota(jnp.int32, (n, 128), 1)
        onehot = jnp.where(ids == lanes, 1.0, 0.0)
        tri = (lax.broadcasted_iota(jnp.int32, (block, block), 1) < lax.broadcasted_iota(jnp.int32, (block, block), 0)).astype(BF)
        carry = jnp.zeros((1, 128), F32)
        for s in range(0, n, block):
            own = onehot[s : s + block]
            before = dot(tri, own.astype(BF)) + carry
            slot = jnp.sum(before * own, 1, keepdims=True).astype(jnp.int32)
            col_ref[s : s + block] = ids[s : s + block] * slots + slot
            carry += jnp.sum(own, 0, keepdims=True)
        row_ref[...] = jnp.broadcast_to(col_ref[...].astype(F32), (n, 128)).T[:8].astype(jnp.int32)

    out = pick_places(row_ref, places, step, rows_ref)
    out_ref[...] = out

    @pl.when(step < cut)
    def _():
        early_ref[...] = out

    @pl.when(step >= cut)
    def _():
        late_ref[...] = out


def pick_places(row_ref, places, step, rows_ref):
    n = rows_ref.shape[0]
    place = lax.broadcasted_iota(jnp.int32, (places, n), 0) + places * step
    return dot((place == row_ref[0:1, :]).astype(BF), rows_ref[...]).astype(BF)


def dispatch(ids, rows, experts, slots, cut, block=256):
    n, width = rows.shape
    places = experts * slots
    steps = places // block
    return pl.pallas_call(
        functools.partial(dispatch_kernel, slots=slots, block=block, cut=cut),
        grid=(steps,),
        in_specs=[
            pl.BlockSpec((n, 1), lambda j: (0, 0)),
            pl.BlockSpec((n, width), lambda j: (0, 0), pipeline_mode=pl.Buffered(1)),
        ],
        out_specs=(
            pl.BlockSpec((n, 1), lambda j: (0, 0)),
            pl.BlockSpec((8, n), lambda j: (0, 0)),
            pl.BlockSpec((block, width), lambda j: (j, 0)),
            pl.BlockSpec((block, width), lambda j: (jnp.minimum(j, cut - 1), 0)),
            pl.BlockSpec((block, width), lambda j: (jnp.maximum(j - cut, 0), 0)),
        ),
        out_shape=(
            jax.ShapeDtypeStruct((n, 1), jnp.int32),
            jax.ShapeDtypeStruct((8, n), jnp.int32),
            jax.ShapeDtypeStruct((places, width), BF),
            jax.ShapeDtypeStruct((cut * block, width), BF),
            jax.ShapeDtypeStruct((places - cut * block, width), BF),
        ),
        compiler_params=pltpu.CompilerParams(vmem_limit_bytes=40 << 20),
        cost_estimate=pl.CostEstimate(flops=2 * n * places * width, bytes_accessed=2 * (n + places) * width, transcendentals=0),
        name="dispatch",
    )(ids, rows)


def unit_rows(hidden):
    centred = hidden - jnp.mean(hidden, -1, keepdims=True)
    return centred * lax.rsqrt(jnp.mean(centred * centred, -1, keepdims=True) + 1e-05)


def project_kernel(tok_ref, gain_ref, shift_ref, wq_ref, bq_ref, wk_ref, wv_ref, bv_ref, act_ref, q_ref, k_ref, v_ref, *, scale):
    act = (unit_rows(tok_ref[...].astype(F32)) * gain_ref[...] + shift_ref[...]).astype(BF)
    act_ref[...] = act
    q_ref[...] = ((dot(act, wq_ref[...]) + bq_ref[...]).astype(BF).astype(F32) * scale).astype(BF)
    k_ref[...] = dot(act, wk_ref[...]).astype(BF)
    v_ref[...] = (dot(act, wv_ref[...]) + bv_ref[...]).astype(BF)


def project(tokens, gain, shift, wq, bq, wk, wv, bv, scale, block=256):
    n, width = tokens.shape
    rows = pl.BlockSpec((block, width), lambda i: (i, 0))
    line = pl.BlockSpec((1, width), lambda i: (0, 0))
    matrix = pl.BlockSpec((width, width), lambda i: (0, 0), pipeline_mode=pl.Buffered(1))
    return pl.pallas_call(
        functools.partial(project_kernel, scale=scale),
        grid=(n // block,),
        in_specs=[rows, line, line, matrix, line, matrix, matrix, line],
        out_specs=(rows,) * 4,
        out_shape=(jax.ShapeDtypeStruct((n, width), BF),) * 4,
        compiler_params=pltpu.CompilerParams(vmem_limit_bytes=40 << 20),
        cost_estimate=pl.CostEstimate(flops=6 * n * width * width, bytes_accessed=16 * n * width, transcendentals=0),
        name="project",
    )(tokens, gain, shift, wq, bq, wk, wv, bv)


def after_attn_kernel(
    mixed_ref, tok_ref, w_ref, bias_ref, gain_ref, shift_ref, row_ref, hidden_ref, out_ref, act_ref, *, first, block
):
    step = pl.program_id(0)
    places = out_ref.shape[0]
    for i in range(first):

        @pl.when(step == i)
        def _(i=i):
            hidden = tok_ref[...].astype(F32) + dot(mixed_ref[...], w_ref[...]) + bias_ref[...]
            hidden_ref[...] = hidden
            act_ref[i * block : (i + 1) * block] = (unit_rows(hidden) * gain_ref[...] + shift_ref[...]).astype(BF)

    @pl.when(step >= first)
    def _():
        out_ref[...] = pick_places(row_ref, places, step - first, act_ref)


def after_attn(mixed, tokens, w, bias, gain, shift, target, places, block=256):
    n, width = tokens.shape
    first = n // block
    rows = pl.BlockSpec((block, width), lambda i: (jnp.minimum(i, first - 1), 0))
    line = pl.BlockSpec((1, width), lambda i: (0, 0))
    return pl.pallas_call(
        functools.partial(after_attn_kernel, first=first, block=block),
        grid=(first + places // block,),
        in_specs=[
            rows,
            rows,
            pl.BlockSpec((width, width), lambda i: (0, 0), pipeline_mode=pl.Buffered(1)),
            line,
            line,
            line,
            pl.BlockSpec((8, n), lambda i: (0, 0)),
        ],
        out_specs=(rows, pl.BlockSpec((block, width), lambda i: (jnp.maximum(i - first, 0), 0))),
        out_shape=(jax.ShapeDtypeStruct((n, width), F32), jax.ShapeDtypeStruct((places, width), BF)),
        scratch_shapes=[pltpu.VMEM((n, width), BF)],
        compiler_params=pltpu.CompilerParams(vmem_limit_bytes=40 << 20),
        cost_estimate=pl.CostEstimate(flops=4 * n * width * width, bytes_accessed=12 * n * width, transcendentals=0),
        name="after_attn",
    )(mixed, tokens, w, bias, gain, shift, target)


def after_experts_kernel(
    target_ref, home_ref, cot_ref, hidden_ref, gain_ref, w_out_ref, gh_ref, ga_ref, do_ref, sums_ref
):
    rows, width = cot_ref.shape
    places = home_ref.shape[0]
    pick = (lax.broadcasted_iota(jnp.int32, (rows, places), 1) == target_ref[...]).astype(BF)
    d = dot(pick, home_ref[...])
    hidden = hidden_ref[...]
    centred = hidden - jnp.mean(hidden, -1, keepdims=True)
    inv = lax.rsqrt(jnp.mean(centred * centred, -1, keepdims=True) + 1e-05)
    unit = centred * inv
    scaled = d * gain_ref[...]
    mean_one = jnp.mean(scaled, -1, keepdims=True)
    mean_two = jnp.mean(scaled * unit, -1, keepdims=True)
    grad = cot_ref[...].astype(F32) + inv * (scaled - mean_one - unit * mean_two)
    gh_ref[...] = grad
    low = grad.astype(BF)
    ga_ref[...] = low
    do_ref[...] = dot_nt(low, w_out_ref[...]).astype(BF)
    parts = [jnp.sum(low.astype(F32), 0, keepdims=True), jnp.sum(d * unit, 0, keepdims=True), jnp.sum(d, 0, keepdims=True)]
    parts = jnp.concatenate(parts + [jnp.zeros((8 - len(parts), width), F32)], 0)

    @pl.when(pl.program_id(0) == 0)
    def _():
        sums_ref[...] = parts

    @pl.when(pl.program_id(0) > 0)
    def _():
        sums_ref[...] += parts


def after_experts(target, home, cot, hidden, gain, w_out, block=256):
    n, width = cot.shape
    places = home.shape[0]
    rows = pl.BlockSpec((block, width), lambda i: (i, 0))
    once = pl.Buffered(1)
    return pl.pallas_call(
        after_experts_kernel,
        grid=(n // block,),
        in_specs=[
            pl.BlockSpec((block, 1), lambda i: (i, 0)),
            pl.BlockSpec((places, width), lambda i: (0, 0), pipeline_mode=once),
            rows,
            rows,
            pl.BlockSpec((1, width), lambda i: (0, 0)),
            pl.BlockSpec((width, width), lambda i: (0, 0), pipeline_mode=once),
        ],
        out_specs=(rows, rows, rows, pl.BlockSpec((8, width), lambda i: (0, 0))),
        out_shape=(
            jax.ShapeDtypeStruct((n, width), F32),
            jax.ShapeDtypeStruct((n, width), BF),
            jax.ShapeDtypeStruct((n, width), BF),
            jax.ShapeDtypeStruct((8, width), F32),
        ),
        compiler_params=pltpu.CompilerParams(vmem_limit_bytes=50 << 20),
        name="after_experts",
    )(target, home, cot, hidden, gain, w_out)


def backward_kernel(*refs, ep_bits, rep_bits, own, rblk, chunks, blk):
    len_ref, q_ref, k_ref, v_ref, o_ref, do_ref, lse_ref = refs[:7]
    act_ref, mixed_ref, ga_ref, wq_ref, wk_ref, wv_ref, tok_ref, gain_ref, sums_ref, bias_ref = refs[7:17]
    out_ref, da_ref, vec_out, bias_out = refs[17:21]
    at_ref, mt_ref, dq_ref, dk_ref, dv_ref, dqt_ref, dk_acc, dv_acc, x_ref = refs[21:30]
    bits = ep_bits + rep_bits
    got = refs[30 : 30 + bits]
    vec_got, vec_sum, bias_got, bias_sum, send, recv, vsend, vrecv, bsend, brecv = refs[30 + bits :]
    step = pl.program_id(0)
    n, width = act_ref.shape
    block = ga_ref.shape[1]
    lanes = q_ref.shape[1]
    ep, rep = 1 << ep_bits, 1 << rep_bits
    me_z = lax.axis_index("rep")
    me = lax.axis_index("ep")

    def bit(b):
        return lax.rem(me // (1 << b), 2) if b < ep_bits else lax.rem(me_z // (1 << (b - ep_bits)), 2)

    def flip(b):
        change = 1 - 2 * bit(b)
        return (me_z, me + change * (1 << b)) if b < ep_bits else (me_z + change * (1 << (b - ep_bits)), me)

    def order(c):
        rest = list(range(1, ep_bits))
        return [0] + (rest if c % 2 == 0 else rest[::-1]) + list(range(ep_bits, bits))

    def copy(src, dst, s, r, peer):
        return pltpu.make_async_remote_copy(
            src_ref=src, dst_ref=dst, send_sem=s, recv_sem=r, device_id=peer, device_id_type=pl.DeviceIdType.MESH
        )

    def cut(c, stage, value):
        done = order(c)[:stage]
        left = [b for b in range(ep_bits - 1, -1, -1) if b not in done]
        left += [b for b in range(bits - 1, ep_bits - 1, -1) if b not in done]
        index = [slice(None)] * len(left)
        index[left.index(order(c)[stage])] = value
        return tuple(index)

    def held(c, stage):
        return x_ref.at[c] if stage == 0 else got[stage - 1].at[c]

    def stage_copy(c, stage):
        b = order(c)[stage]
        return copy(
            held(c, stage).at[cut(c, stage, 1 - bit(b))], got[stage].at[c], send.at[c, stage], recv.at[c, stage], flip(b)
        )

    def advance(pair, stage):
        for c in (2 * pair, 2 * pair + 1):
            stage_copy(c, stage).wait()
            keep = held(c, stage)[cut(c, stage, bit(order(c)[stage]))]
            if stage + 1 < bits:
                got[stage][c] += keep
                stage_copy(c, stage + 1).start()
            else:
                out_ref[:, :, c * lanes : (c + 1) * lanes] = got[stage][c].astype(F32) + keep.astype(F32)

    def small_copy(k, got_ref, sum_ref, first, s, r):
        return copy(sum_ref.at[k - first], got_ref.at[k - first], s.at[k - first], r.at[k - first], flip(k))

    def vec_copy(k):
        return small_copy(k, vec_got, vec_sum, 0, vsend, vrecv)

    def bias_copy(k):
        return small_copy(k, bias_got, bias_sum, ep_bits, bsend, brecv)

    def vec_step(k):
        vec_copy(k).wait()
        vec_sum[k + 1] = vec_sum[k] + vec_got[k]
        if k + 1 < bits:
            vec_copy(k + 1).start()

    @pl.when(step == 0)
    def _():
        barrier = pltpu.get_barrier_semaphore()
        for b in range(bits):
            pl.semaphore_signal(barrier, inc=1, device_id=flip(b), device_id_type=pl.DeviceIdType.MESH)
        pl.semaphore_wait(barrier, bits)
        bias_sum[0] = bias_ref[...]
        bias_copy(ep_bits).start()
        at_ref[...] = act_ref[...].T
        mt_ref[...] = mixed_ref[...].T

    slot = lax.rem(step, 2)
    attn_bwd_kernel(
        len_ref, q_ref, k_ref, v_ref, o_ref, do_ref, lse_ref, dq_ref.at[slot], dk_ref.at[slot], dv_ref.at[slot],
        dqt_ref, dk_acc, dv_acc, blk=blk,
    )

    def put(c, w, left, right):
        g = dot(left[...], right).astype(BF)
        for r in range(rep):
            for e in range(ep):
                start = (r * ep + e) * own
                where = tuple((e >> b) & 1 for b in range(ep_bits - 1, -1, -1))
                where += tuple((r >> b) & 1 for b in range(rep_bits - 1, -1, -1))
                for k in range(2):
                    x_ref[(2 * c + k,) + where + (w,)] = g[start : start + own, k * lanes : (k + 1) * lanes]

    def norm_sums():
        total_n = jnp.zeros((1, width), F32)
        total_d = jnp.zeros((1, width), F32)
        for s in range(0, n, rblk):
            rs = slice(s, s + rblk)
            d = da_ref[rs]
            total_n += jnp.sum(d * unit_rows(tok_ref[rs].astype(F32)), 0, keepdims=True)
            total_d += jnp.sum(d, 0, keepdims=True)
        return total_n, total_d

    for c in range(chunks):

        @pl.when(step == 2 * c)
        def _(c=c):
            put(c, 3, mt_ref, ga_ref[...])
            for stage in range(0, bits, 2):
                if c - 1 - stage // 2 >= 0:
                    advance(c - 1 - stage // 2, stage)
            if 1 <= c <= rep_bits:
                k = c - 1
                bias_copy(ep_bits + k).wait()
                bias_sum[k + 1] = bias_sum[k] + bias_got[k]
                if k + 1 < rep_bits:
                    bias_copy(ep_bits + k + 1).start()

        @pl.when(step == 2 * c + 1)
        def _(c=c):
            dq = jnp.concatenate([dq_ref[0], dq_ref[1]], 1)
            dk = jnp.concatenate([dk_ref[0], dk_ref[1]], 1)
            dv = jnp.concatenate([dv_ref[0], dv_ref[1]], 1)
            put(c, 0, at_ref, dq)
            put(c, 1, at_ref, dk)
            put(c, 2, at_ref, dv)
            stage_copy(2 * c, 0).start()
            stage_copy(2 * c + 1, 0).start()
            for stage in range(1, bits, 2):
                if c - 1 - stage // 2 >= 0:
                    advance(c - 1 - stage // 2, stage)
            cols = slice(c * block, (c + 1) * block)
            vec_sum[0, 2:3, cols] = jnp.sum(dq.astype(F32), 0, keepdims=True)
            vec_sum[0, 3:4, cols] = jnp.sum(dv.astype(F32), 0, keepdims=True)
            vec_sum[0, 4:8, cols] = sums_ref[0:4, cols]
            if c == chunks - 1:
                advance(c, 0)
            for s in range(0, n, rblk):
                rs = slice(s, s + rblk)
                part = dot_nt(dq[rs], wq_ref[...]) + dot_nt(dk[rs], wk_ref[...]) + dot_nt(dv[rs], wv_ref[...])
                if c == 0:
                    da_ref[rs] = part
                else:
                    da_ref[rs] += part
            if c == chunks - 1:
                total_n, total_d = norm_sums()
                vec_sum[0, 0:1] = total_n
                vec_sum[0, 1:2] = total_d
                vec_copy(0).start()
                waves = {}
                for d in range(chunks):
                    for stage in range(bits):
                        reached = 2 * (d + 1 + stage // 2) + stage % 2
                        if reached > 2 * c + 1 and (d, stage) != (c, 0):
                            waves.setdefault(d + stage, []).append((d, stage))
                k = 0
                for wave in sorted(waves):
                    for d, stage in reversed(waves[wave]):
                        advance(d, stage)
                    if k < bits:
                        vec_step(k)
                        k += 1
                for k in range(k, bits):
                    vec_step(k)
                vec_out[...] = vec_sum[bits]
                bias_out[...] = bias_sum[rep_bits]


def backward(length, q, k, v, o, do, lse, act, ga, wq, wk, wv, tokens, gain, sums, bias, rep, ep, rblk=256, blk=256):
    n, width = act.shape
    own = width // (rep * ep)
    ep_bits, rep_bits = ep.bit_length() - 1, rep.bit_length() - 1
    bits = ep_bits + rep_bits
    lanes = 128
    block = 2 * lanes
    chunks = width // block
    once = pl.Buffered(1)
    whole = pl.BlockSpec((n, width), lambda j: (0, 0), pipeline_mode=once)
    pair = pl.BlockSpec((n, lanes), lambda j: (0, j))
    cols = pl.BlockSpec((n, block), lambda j: (0, j // 2))
    eight = pl.BlockSpec((8, width), lambda j: (0, 0))
    scratch = [
        pltpu.VMEM((width, n), BF),
        pltpu.VMEM((width, n), BF),
        pltpu.VMEM((2, n, lanes), BF),
        pltpu.VMEM((2, n, lanes), BF),
        pltpu.VMEM((2, n, lanes), BF),
        pltpu.VMEM((lanes, n), F32),
        pltpu.VMEM((n, lanes), F32),
        pltpu.VMEM((n, lanes), F32),
        pltpu.VMEM((2 * chunks,) + (2,) * bits + (4, own, lanes), BF),
    ]
    scratch += [pltpu.VMEM((2 * chunks,) + (2,) * (bits - 1 - k) + (4, own, lanes), BF) for k in range(bits)]
    scratch += [
        pltpu.VMEM((bits, 8, width), F32),
        pltpu.VMEM((bits + 1, 8, width), F32),
        pltpu.VMEM((rep_bits, 8, width), F32),
        pltpu.VMEM((rep_bits + 1, 8, width), F32),
        pltpu.SemaphoreType.DMA((2 * chunks, bits)),
        pltpu.SemaphoreType.DMA((2 * chunks, bits)),
        pltpu.SemaphoreType.DMA((bits,)),
        pltpu.SemaphoreType.DMA((bits,)),
        pltpu.SemaphoreType.DMA((rep_bits,)),
        pltpu.SemaphoreType.DMA((rep_bits,)),
    ]
    return pl.pallas_call(
        functools.partial(
            backward_kernel, ep_bits=ep_bits, rep_bits=rep_bits, own=own, rblk=rblk, chunks=chunks, blk=blk
        ),
        grid=(2 * chunks,),
        in_specs=[pl.BlockSpec(memory_space=pltpu.SMEM)]
        + [pair] * 5
        + [pl.BlockSpec((1, 2, n), lambda j: (j, 0, 0)), whole, whole, cols, cols, cols, cols, whole]
        + [pl.BlockSpec((1, width), lambda j: (0, 0)), eight, eight],
        out_specs=(pl.BlockSpec((4, own, width), lambda j: (0, 0, 0)), whole, eight, eight),
        out_shape=(
            jax.ShapeDtypeStruct((4, own, width), F32),
            jax.ShapeDtypeStruct((n, width), F32),
            jax.ShapeDtypeStruct((8, width), F32),
            jax.ShapeDtypeStruct((8, width), F32),
        ),
        scratch_shapes=scratch,
        compiler_params=pltpu.CompilerParams(vmem_limit_bytes=63 << 20, collective_id=1, has_side_effects=True),
        name="backward",
    )(length, q, k, v, o, do, lse, act, o, ga, wq, wk, wv, tokens, gain, sums, bias)


def combine_kernel(target_ref, back_ref, hidden_ref, out_ref):
    rows, places = hidden_ref.shape[0], back_ref.shape[0]
    pick = (lax.broadcasted_iota(jnp.int32, (rows, places), 1) == target_ref[...]).astype(BF)
    out_ref[...] = (hidden_ref[...] + dot(pick, back_ref[...])).astype(BF)


def combine(target, back, hidden, block=256):
    n, width = hidden.shape
    rows = pl.BlockSpec((block, width), lambda i: (i, 0))
    return pl.pallas_call(
        combine_kernel,
        grid=(n // block,),
        in_specs=[
            pl.BlockSpec((block, 1), lambda i: (i, 0)),
            pl.BlockSpec(back.shape, lambda i: (0, 0), pipeline_mode=pl.Buffered(1)),
            rows,
        ],
        out_specs=rows,
        out_shape=jax.ShapeDtypeStruct((n, width), BF),
        compiler_params=pltpu.CompilerParams(vmem_limit_bytes=40 << 20),
        name="combine",
    )(target, back, hidden)


def finish_kernel(
    where_ref, a1_ref, b1_ref, c1_ref, d1_ref, a2_ref, b2_ref, da_ref, gh_ref, tok_ref, gain_ref, small_ref, bias_ref,
    g1_ref, g2_ref, gt_ref, small_out, bias1_out, bias2_out, *, tile,
):
    per_row = a1_ref.shape[1] // tile
    h, shift, row = where_ref[0], where_ref[1], where_ref[2]
    g2_ref[0] = a2_ref[...].astype(F32)
    g2_ref[1] = b2_ref[...].astype(F32)
    for refs, tile_of in (((a1_ref,), early_tile), ((b1_ref, c1_ref, d1_ref), late_tile)):
        for j in range(len(refs) * per_row):
            start = pl.multiple_of(tile_of(j, h) * tile, tile)
            c = tile * (j % per_row)
            g1_ref[:, pl.ds(start, tile)] = refs[j // per_row][:, c : c + tile].astype(F32)
    hidden = tok_ref[...].astype(F32)
    centred = hidden - jnp.mean(hidden, -1, keepdims=True)
    inv = lax.rsqrt(jnp.mean(centred * centred, -1, keepdims=True) + 1e-05)
    unit = centred * inv
    scaled = da_ref[...] * gain_ref[...]
    mean_one = jnp.mean(scaled, -1, keepdims=True)
    mean_two = jnp.mean(scaled * unit, -1, keepdims=True)
    gt_ref[...] = gh_ref[...] + inv * (scaled - mean_one - unit * mean_two)

    @pl.when(pl.program_id(0) == 0)
    def _():
        small_out[...] = pltpu.roll(small_ref[...], shift, 1)[:, : small_out.shape[1]]
        bias1_out[...] = bias_ref[pl.ds(row, 1), :]
        wide = bias2_out.shape[1]
        bias2_out[...] = bias_ref[4:5, pl.ds(pl.multiple_of(row * wide, wide), wide)]


def finish(where, a, b, da, gh, tokens, gain, small, bias, tile, ff, rep, steps=4):
    n, d = tokens.shape
    own = d // rep
    rows = own // steps
    base = tile // rows

    def line(k):
        return pl.BlockSpec((rows, d), lambda i: (base + k * steps + i, 0))

    second = pl.BlockSpec((tile // steps, d), lambda i: (i, 0))
    block = pl.BlockSpec((n // steps, d), lambda i: (i, 0))

    def fixed(shape):
        return pl.BlockSpec(shape, lambda i: (0, 0))

    out = pl.pallas_call(
        functools.partial(finish_kernel, tile=tile),
        grid=(steps,),
        in_specs=[pl.BlockSpec(memory_space=pltpu.SMEM), line(0), line(0), line(1), line(2), second, second]
        + [block, block, block, fixed((1, d)), fixed((8, d)), fixed((8, d))],
        out_specs=(
            pl.BlockSpec((rows, ff), lambda i: (i, 0)),
            pl.BlockSpec((2, tile // steps, d), lambda i: (0, i, 0)),
            block,
            fixed((8, 128)),
            fixed((1, d)),
            fixed((1, own)),
        ),
        out_shape=(
            jax.ShapeDtypeStruct((own, ff), F32),
            jax.ShapeDtypeStruct((2, tile, d), F32),
            jax.ShapeDtypeStruct((n, d), F32),
            jax.ShapeDtypeStruct((8, 128), F32),
            jax.ShapeDtypeStruct((1, d), F32),
            jax.ShapeDtypeStruct((1, own), F32),
        ),
        compiler_params=pltpu.CompilerParams(vmem_limit_bytes=60 << 20),
        name="finish",
    )(where, a, b, b, b, a, b, da, gh, tokens, gain, small, bias)
    return (out[0], out[1].reshape(2 * tile, d)) + tuple(out[2:])


def per_device(
    tokens,
    cotangent,
    lengths,
    expert_ids,
    norm1_gain,
    norm1_bias,
    w_query,
    b_query,
    w_key,
    w_value,
    b_value,
    w_out,
    b_out,
    norm2_gain,
    norm2_bias,
    w_in,
    b_in,
    w_back,
    b_back,
):
    row_count, width = tokens.shape
    head_dim = width // HEADS
    ep = lax.axis_size("ep")
    rep = lax.axis_size("rep")
    slots = 5 * row_count // (4 * ep)
    places = ep * slots
    ff = w_in.shape[2]
    w_first = w_in[0]
    w_second = w_back[0]

    def exchange(rows):
        sent = lax.all_to_all(rows.reshape(ep, slots, width), "ep", 0, 0, tiled=True)
        return sent.reshape(places, width)

    at = lax.axis_index("rep")
    swap = [(i, i ^ 1) for i in range(rep)]
    target, target_row, grad_send, early, tail = dispatch(expert_ids, cotangent, ep, slots, 3)
    grad_rows = exchange(grad_send)
    early = lax.ppermute(early, "rep", swap)
    act_a, queries, keys, values = project(
        tokens, norm1_gain[None], norm1_bias[None], w_query, b_query[None], w_key, w_value, b_value[None], head_dim**-0.5
    )
    mixed, lse = attn_fwd(queries, keys, values, lengths)
    mixed, grad_rows, early, tail = lax.optimization_barrier((mixed, grad_rows, early, tail))
    late = lax.ppermute(tail, "rep", swap)
    hidden_one, rows_out = after_attn(
        mixed, tokens, w_out, b_out[None], norm2_gain[None], norm2_bias[None], target_row, places
    )
    rows_in = exchange(rows_out)
    rows_in, both = lax.optimization_barrier((rows_in, jnp.concatenate([early, late], 0)))
    grad_pair = exchange(both)
    rows_pair = lax.ppermute(rows_in, "rep", swap)
    own_fn = functools.partial(expert_own, tile=ff // 4)
    own_out = jax.eval_shape(own_fn, rows_in, grad_rows, w_first, b_in, w_second)
    own_all = lax.cond(
        lengths[0] > 0,
        own_fn,
        lambda *_: tuple(jnp.zeros(x.shape, x.dtype) for x in own_out),
        rows_in,
        grad_rows,
        w_first,
        b_in,
        w_second,
    )
    active, grad_inner, g_bias_first, grad_input, g_bias_second = own_all
    grad_home = exchange(grad_input)
    half = (at & 1).astype(jnp.int32)[None]
    turned = turn(half, rows_in, grad_rows, grad_pair, rep)
    active, grad_inner, g_bias_first, rows_pair, grad_pair, turned = lax.optimization_barrier(
        (active, grad_inner, g_bias_first, rows_pair, grad_pair, turned)
    )

    def pair(tile_of, steps):
        return expert_pair(
            half, turned, rows_pair, grad_pair, w_first, b_in, w_second, active, grad_inner, tile_of, steps, ff // 8, rep
        )

    groups = [[0, 2], [1, 3]]
    part_0 = pair(early_tile, 2)
    rows_pair, grad_home, active, part_0 = lax.optimization_barrier((rows_pair, grad_home, active, part_0))
    sum_0 = lax.psum_scatter(part_0, "rep", scatter_dimension=0, axis_index_groups=groups, tiled=True)
    result = (dot(active, w_second) + b_back[0]).astype(BF)
    rows_pair, result = lax.optimization_barrier((rows_pair, result))
    returned = exchange(result)
    part_1 = pair(late_tile, 6)
    returned, part_1 = lax.optimization_barrier((returned, part_1))
    sum_1 = lax.psum_scatter(part_1, "rep", scatter_dimension=0, axis_index_groups=groups, tiled=True)
    block_out = combine(target, returned, hidden_one)
    grad_home, block_out = lax.optimization_barrier((grad_home, block_out))

    def remainder(grad_home, g_bias_first, g_bias_second):
        grad_hidden, grad_attn, grad_mixed, sums = after_experts(
            target, grad_home, cotangent, hidden_one, norm2_gain[None], w_out
        )
        bias = jnp.concatenate([g_bias_first.reshape(ff // width, width), g_bias_second], 0)
        bias = jnp.pad(bias, ((0, 8 - bias.shape[0]), (0, 0)))
        return (grad_hidden,) + tuple(
            backward(
                lengths, queries, keys, values, mixed, grad_mixed, lse, act_a, grad_attn, w_query, w_key, w_value, tokens,
                norm1_gain[None], sums, bias, rep, ep,
            )
        )

    own = width // (rep * ep)
    own_ff, own_width = ff // rep, width // rep
    args = (grad_home, g_bias_first, g_bias_second)
    shapes = jax.eval_shape(remainder, *args)
    grad_hidden, dense, grad_act, small, grad_bias = lax.cond(
        lengths[0] > 0, remainder, lambda *_: jax.tree.map(lambda x: jnp.zeros(x.shape, x.dtype), shapes), *args
    )
    place = at * ep + lax.axis_index("ep")
    where = jnp.stack([at & 1, lax.rem(width - place * own, width), at]).astype(jnp.int32)
    out_first, out_second, grad_tokens, small, out_bias_first, out_bias_second = finish(
        where, sum_0[0], sum_1[0], grad_act, grad_hidden, tokens, norm1_gain[None], small, grad_bias, ff // 8, ff, rep
    )
    small = small[:, :own]
    out_first, out_second = out_first[None], out_second[None]
    return (
        block_out,
        grad_tokens,
        small[0],
        small[1],
        dense[0],
        small[2],
        dense[1],
        dense[2],
        small[3],
        dense[3],
        small[4],
        small[5],
        small[6],
        out_first,
        out_bias_first,
        out_second,
        out_bias_second,
    )


def solution(mesh):
    return jax.shard_map(
        per_device,
        mesh=mesh,
        in_specs=(
            P(("rep", "ep"), None),
            P(("rep", "ep"), None),
            P(("rep", "ep")),
            P(("rep", "ep"), None),
            P(),
            P(),
            P(),
            P(),
            P(),
            P(),
            P(),
            P(),
            P(),
            P(),
            P(),
            P("ep", None, None),
            P("ep", None),
            P("ep", None, None),
            P("ep", None),
        ),
        out_specs=(
            P(("rep", "ep"), None),
            P(("rep", "ep"), None),
            P(("rep", "ep")),
            P(("rep", "ep")),
            P(("rep", "ep"), None),
            P(("rep", "ep")),
            P(("rep", "ep"), None),
            P(("rep", "ep"), None),
            P(("rep", "ep")),
            P(("rep", "ep"), None),
            P(("rep", "ep")),
            P(("rep", "ep")),
            P(("rep", "ep")),
            P("ep", "rep", None),
            P("ep", "rep"),
            P("ep", "rep", None),
            P("ep", "rep"),
        ),
        check_vma=False,
    )
```

```python
import functools

import jax
import jax.numpy as jnp
from jax import lax
from jax.experimental import pallas as pl
from jax.experimental.pallas import tpu as pltpu
from jax.sharding import PartitionSpec as P

HEADS = 16
BF = jnp.bfloat16
F32 = jnp.float32
LOG2E = 1.4426950408889634
NEG = -1e30


def dot(left, right):
    return jnp.dot(left, right, preferred_element_type=F32)


def dot_nt(left, right):
    return lax.dot_general(left, right, (((1,), (1,)), ((), ())), preferred_element_type=F32)


def dot_tn(left, right):
    return lax.dot_general(left, right, (((0,), (0,)), ((), ())), preferred_element_type=F32)


def attn_fwd_kernel(len_ref, q_ref, k_ref, v_ref, o_ref, lse_ref, ot_ref, *, blk):
    n, lanes = q_ref.shape
    half = lanes//2
    length = len_ref[0]
    k = k_ref[...].astype(F32)
    lane = lax.broadcasted_iota(jnp.int32,(n,lanes),1)
    row = lax.broadcasted_iota(jnp.int32,(n,lanes),0)
    bias = jnp.where(row<length, 0.0, NEG)
    k_a = jnp.where(lane<half, k, jnp.where(lane==half, bias, 0.0)).astype(BF)
    k_b = jnp.where(lane>=half, k, jnp.where(lane==0, bias, 0.0)).astype(BF)
    qt = q_ref[...].T
    vt = v_ref[...].T
    trow = lax.broadcasted_iota(jnp.int32,(lanes,n),0)
    qt32 = qt.astype(F32)
    qt_a = jnp.where(trow==half, 1.0, qt32).astype(BF)
    qt_b = jnp.where(trow==0, 1.0, qt32).astype(BF)
    tri = lax.broadcasted_iota(jnp.int32,(blk,blk),0) <= lax.broadcasted_iota(jnp.int32,(blk,blk),1)
    ones = jnp.ones((16,n),BF)
    for h,(kk,qq) in enumerate(((k_a,qt_a),(k_b,qt_b))):
        v_ext = jnp.concatenate([vt[h*half:(h+1)*half], ones],0)
        for i in range(n//blk):
            cols = slice(i*blk,(i+1)*blk)
            qb = qq[:,cols]
            diag = jnp.where(tri, dot(kk[cols],qb), NEG)
            if i:
                past = dot(kk[:i*blk],qb)
                top = jnp.maximum(jnp.max(past,0,keepdims=True),jnp.max(diag,0,keepdims=True))
                p = jnp.concatenate([jnp.exp2((past-top)*LOG2E).astype(BF),jnp.exp2((diag-top)*LOG2E).astype(BF)],0)
            else:
                top = jnp.max(diag,0,keepdims=True)
                p = jnp.exp2((diag-top)*LOG2E).astype(BF)
            r = dot(v_ext[:,:(i+1)*blk],p)
            total = r[half:half+1]
            ot_ref[h*half:(h+1)*half,cols] = r[:half]/total
            lse_ref[0,h:h+1,cols] = top + jnp.log(total)
    o_ref[...] = ot_ref[...].T.astype(BF)

def attn_fwd(q, k, v, length, blk=512):
    n, d = q.shape
    pairs = d // 128
    spec = pl.BlockSpec((n, 128), lambda h: (0, h))
    return pl.pallas_call(
        functools.partial(attn_fwd_kernel, blk=blk),
        grid=(pairs,),
        in_specs=[pl.BlockSpec(memory_space=pltpu.SMEM), spec, spec, spec],
        out_specs=(spec, pl.BlockSpec((1, 2, n), lambda h: (h, 0, 0))),
        out_shape=(jax.ShapeDtypeStruct((n, d), BF), jax.ShapeDtypeStruct((pairs, 2, n), F32)),
        scratch_shapes=[pltpu.VMEM((128, n), F32)],
        compiler_params=pltpu.CompilerParams(vmem_limit_bytes=50 << 20),
        cost_estimate=pl.CostEstimate(flops=8 * n * n * d, bytes_accessed=8 * n * d, transcendentals=8 * n * n),
        name="attn_fwd",
    )(length, q, k, v)


def split3(x):
    a=x.astype(BF).astype(F32); r=x-a
    b=r.astype(BF).astype(F32); c=r-b
    return a,b,c

def attn_bwd_kernel(len_ref, q_ref, k_ref, v_ref, o_ref, do_ref, lse_ref, dq_ref, dk_ref, dv_ref, dqt_ref, dk_acc, dv_acc, *, blk):
    n, lanes = q_ref.shape
    half = lanes//2
    length = len_ref[0]
    lane = lax.broadcasted_iota(jnp.int32,(n,lanes),1)
    row = lax.broadcasted_iota(jnp.int32,(n,lanes),0)
    trow = lax.broadcasted_iota(jnp.int32,(lanes,n),0)
    bias = jnp.where(row<length, 0.0, NEG)
    q = q_ref[...].astype(F32); k = k_ref[...].astype(F32); v=v_ref[...].astype(F32); do=do_ref[...].astype(F32)
    kt = k_ref[...].T
    qt = q_ref[...].T.astype(F32)
    dot_t = do_ref[...].T.astype(F32)
    ot = o_ref[...].T.astype(F32)
    prod = dot_t*ot
    heads=[]
    for h in range(2):
        own = (lane<half) if h==0 else (lane>=half)
        base = half if h==0 else 0
        delta = jnp.sum(prod[h*half:(h+1)*half],0,keepdims=True)
        lse = lse_ref[0,h:h+1,:]
        l1,l2,l3 = split3(-lse)
        d1,d2,d3 = split3(-delta)
        one = jnp.where((lane>=base+1)&(lane<=base+3),1.0,0.0)
        k_x = jnp.where(own,k,jnp.where(lane==base,bias,one)).astype(BF)
        v_x = jnp.where(own,v,one).astype(BF)
        q_x = jnp.where(trow==base,1.0,jnp.where(trow==base+1,l1,jnp.where(trow==base+2,l2,jnp.where(trow==base+3,l3,qt)))).astype(BF)
        d_x = jnp.where(trow==base+1,d1,jnp.where(trow==base+2,d2,jnp.where(trow==base+3,d3,dot_t))).astype(BF)
        q_own = jnp.where(own,q,0.0).astype(BF)
        do_own = jnp.where(own,do,0.0).astype(BF)
        heads.append((k_x,v_x,q_x,d_x,q_own,do_own))
    tri = lax.broadcasted_iota(jnp.int32,(blk,blk),0) <= lax.broadcasted_iota(jnp.int32,(blk,blk),1)
    steps=n//blk
    for i in reversed(range(steps)):
        cols = slice(i*blk,(i+1)*blk)
        ps=[];dss=[]
        for h in range(2):
            k_x,v_x,q_x,d_x,q_own,do_own=heads[h]
            qb=q_x[:,cols]; db=d_x[:,cols]
            p_d = jnp.exp2(jnp.where(tri,dot(k_x[cols],qb),NEG)*LOG2E)
            ds_d = p_d*dot(v_x[cols],db)
            if i:
                p_p = jnp.exp2(dot(k_x[:i*blk],qb)*LOG2E)
                ds_p = p_p*dot(v_x[:i*blk],db)
                p=jnp.concatenate([p_p.astype(BF),p_d.astype(BF)],0)
                ds=jnp.concatenate([ds_p.astype(BF),ds_d.astype(BF)],0)
            else:
                p=p_d.astype(BF); ds=ds_d.astype(BF)
            dqt_ref[h*half:(h+1)*half,cols]=dot(kt[h*half:(h+1)*half,:(i+1)*blk],ds)
            ps.append(p);dss.append(ds)
        dv_new = dot(ps[0],heads[0][5][cols])+dot(ps[1],heads[1][5][cols])
        dk_new = dot(dss[0],heads[0][4][cols])+dot(dss[1],heads[1][4][cols])
        if i==steps-1:
            dv_acc[...]=dv_new; dk_acc[...]=dk_new
        else:
            dv_acc[:(i+1)*blk]+=dv_new; dk_acc[:(i+1)*blk]+=dk_new
    scale=half**-0.5
    dq_ref[...]=(dqt_ref[...]*scale).T.astype(BF)
    dk_ref[...]=dk_acc[...].astype(BF)
    dv_ref[...]=dv_acc[...].astype(BF)

C0=0.7978845608028654; C1=C0*0.044715

def act_both(z):
    z2=z*z
    a=C1*z2+C0
    t=jnp.tanh(z*a)
    h=0.5*t+0.5
    u=z*h
    q=6.0*a-4.0*C0
    return u, h+u*(1.0-h)*q

def expert_own_kernel(
    b_ref, gy_ref, w1_ref, b1_ref, w2_ref, u_ref, dz_ref, gb1_ref, db_ref, gb2_ref, acc_ref, *, rblk
):
    step = pl.program_id(0)
    rows = b_ref.shape[0]
    w1 = w1_ref[...]
    w2 = w2_ref[...]
    bias = b1_ref[...]
    total = None
    for s in range(0, rows, rblk):
        rs = slice(s, s + rblk)
        u, slope = act_both(dot(b_ref[rs, :], w1) + bias)
        u_ref[rs, :] = u.astype(BF)
        dz = dot_nt(gy_ref[rs, :], w2) * slope
        dz_ref[rs, :] = dz.astype(BF)
        part = jnp.sum(dz, 0, keepdims=True)
        total = part if total is None else total + part
    gb1_ref[...] = total

    @pl.when(step == 0)
    def _():
        total = jnp.zeros_like(gb2_ref)
        for s in range(0, rows, rblk):
            rs = slice(s, s + rblk)
            acc_ref[rs, :] = dot_nt(dz_ref[rs, :], w1)
            total += jnp.sum(gy_ref[rs, :].astype(F32), 0, keepdims=True)
        gb2_ref[...] = total

    @pl.when(step > 0)
    def _():
        for s in range(0, rows, rblk):
            rs = slice(s, s + rblk)
            acc_ref[rs, :] += dot_nt(dz_ref[rs, :], w1)

    @pl.when(step == pl.num_programs(0) - 1)
    def _():
        db_ref[...] = acc_ref[...].astype(BF)


def expert_own(b, gy, w1, b1, w2, tile, rblk=256):
    rows, d = b.shape
    ff = w1.shape[1]
    whole = pl.BlockSpec((rows, d), lambda j: (0, 0), pipeline_mode=pl.Buffered(1))
    return pl.pallas_call(
        functools.partial(expert_own_kernel, rblk=rblk),
        grid=(ff // tile,),
        in_specs=[
            whole,
            whole,
            pl.BlockSpec((d, tile), lambda j: (0, j)),
            pl.BlockSpec((1, tile), lambda j: (0, j)),
            pl.BlockSpec((tile, d), lambda j: (j, 0)),
        ],
        out_specs=(
            pl.BlockSpec((rows, tile), lambda j: (0, j)),
            pl.BlockSpec((rows, tile), lambda j: (0, j)),
            pl.BlockSpec((1, tile), lambda j: (0, j)),
            pl.BlockSpec((rows, d), lambda j: (0, 0)),
            pl.BlockSpec((1, d), lambda j: (0, 0)),
        ),
        out_shape=(
            jax.ShapeDtypeStruct((rows, ff), BF),
            jax.ShapeDtypeStruct((rows, ff), BF),
            jax.ShapeDtypeStruct((1, ff), F32),
            jax.ShapeDtypeStruct((rows, d), BF),
            jax.ShapeDtypeStruct((1, d), F32),
        ),
        scratch_shapes=[pltpu.VMEM((rows, d), F32)],
        compiler_params=pltpu.CompilerParams(vmem_limit_bytes=60 << 20),
        cost_estimate=pl.CostEstimate(flops=8 * rows * d * ff, bytes_accessed=4 * d * ff, transcendentals=rows * ff),
        name="expert_own",
    )(b, gy, w1, b1, w2)


def turn_kernel(half_ref, bo0_ref, bo1_ref, gyo_ref, gyp_ref, bto_ref, gto_ref, gtp_ref):
    @pl.when(pl.program_id(0) == 0)
    def _():
        bto_ref[...] = bo0_ref[...].T

    @pl.when(pl.program_id(0) == 1)
    def _():
        bto_ref[...] = bo1_ref[...].T

    gto_ref[...] = gyo_ref[...].T
    gtp_ref[...] = gyp_ref[...].T


def turn(half, b, gy, gy_pair, rep):
    rows, d = b.shape
    own = d // rep
    block = d // rep
    cols = pl.BlockSpec((rows, block), lambda j, h: (0, j))
    turned = pl.BlockSpec((block, rows), lambda j, h: (j, 0))
    return pl.pallas_call(
        turn_kernel,
        grid_spec=pltpu.PrefetchScalarGridSpec(
            num_scalar_prefetch=1,
            grid=(rep,),
            in_specs=[
                pl.BlockSpec((rows, own), lambda j, h: (0, h[0])),
                pl.BlockSpec((rows, own), lambda j, h: (0, h[0] + 2)),
                cols,
                cols,
            ],
            out_specs=(pl.BlockSpec((own, rows), lambda j, h: (jnp.minimum(j, 1), 0)), turned, turned),
        ),
        out_shape=(
            jax.ShapeDtypeStruct((2 * own, rows), BF),
            jax.ShapeDtypeStruct((d, rows), BF),
            jax.ShapeDtypeStruct((d, rows), BF),
        ),
        compiler_params=pltpu.CompilerParams(vmem_limit_bytes=62 << 20),
        cost_estimate=pl.CostEstimate(flops=1, bytes_accessed=10 * rows * d, transcendentals=0),
        name="turn",
    )(half, b, b, gy, gy_pair)


def pair_kernel(
    half_ref, bto_any, bp_ref, gto_any, gtp_any, gyp_ref, w1_ref, b1_ref, w2_ref, u_ref, dz_ref,
    out_ref, btp_ref, up_ref, dzp_ref, bto_ref, gto_ref, gtp_ref, sems, *, seconds, rblk,
):
    step = pl.program_id(0)
    rows = bp_ref.shape[0]
    own = bto_ref.shape[0] // 2
    tile = w1_ref.shape[1]

    fetched = [
        pltpu.make_async_copy(src, dst, sems.at[i])
        for i, (src, dst) in enumerate(((bto_any, bto_ref), (gto_any, gto_ref), (gtp_any, gtp_ref)))
    ]

    @pl.when(step == 0)
    def _():
        for copy in fetched:
            copy.start()
        for k in range(2):
            start = pl.multiple_of((half_ref[0] + 2 * k) * own, own)
            btp_ref[k * own : (k + 1) * own] = bp_ref[:, pl.ds(start, own)].T

    w1 = w1_ref[...]
    w2 = w2_ref[...]
    bias = b1_ref[...]
    for s in range(0, rows, rblk):
        rs = slice(s, s + rblk)
        u, slope = act_both(dot(bp_ref[rs, :], w1) + bias)
        up_ref[rs, :] = u.astype(BF)
        dzp_ref[rs, :] = (dot_nt(gyp_ref[rs, :], w2) * slope).astype(BF)

    @pl.when(step == 0)
    def _():
        for copy in fetched:
            copy.wait()

    g1 = (dot(bto_ref[...], dz_ref[...]) + dot(btp_ref[...], dzp_ref[...])).astype(BF)
    per_row = out_ref.shape[2] // tile
    base = 2 * tile // 2
    where = pl.ds(pl.multiple_of(base + own * (step // per_row), own), own)
    column = pl.ds(pl.multiple_of(tile * lax.rem(step, per_row), tile), tile)
    out_ref[0, where, column] = g1[:own]
    out_ref[1, where, column] = g1[own:]

    @pl.when(step < seconds)
    def _():
        g2 = dot(gto_ref[...], u_ref[...]) + dot(gtp_ref[...], up_ref[...])
        out_ref[step, :tile] = g2.astype(BF).T


def expert_pair(half, turned, b_pair, gy_pair, w1, b1, w2, u, dz, tile_of, steps, tile, rep, rblk=256):
    rows, d = b_pair.shape
    own = d // rep
    once = pl.Buffered(1)
    per_row = d // tile
    height = tile + own * (steps // per_row)

    hbm = pl.BlockSpec(memory_space=pl.ANY)

    def fixed(shape, index=(0, 0)):
        return pl.BlockSpec(shape, lambda j, h: index, pipeline_mode=once)

    return pl.pallas_call(
        functools.partial(pair_kernel, seconds=2, rblk=rblk),
        grid_spec=pltpu.PrefetchScalarGridSpec(
            num_scalar_prefetch=1,
            grid=(steps,),
            in_specs=[
                hbm,
                fixed((rows, d)),
                hbm,
                hbm,
                fixed((rows, d)),
                pl.BlockSpec((d, tile), lambda j, h: (0, tile_of(j, h[0]))),
                pl.BlockSpec((1, tile), lambda j, h: (0, tile_of(j, h[0]))),
                pl.BlockSpec((tile, d), lambda j, h: (tile_of(j, h[0]), 0)),
                pl.BlockSpec((rows, tile), lambda j, h: (0, tile_of(j, h[0]))),
                pl.BlockSpec((rows, tile), lambda j, h: (0, tile_of(j, h[0]))),
            ],
            out_specs=pl.BlockSpec((2, height, d), lambda j, h: (0, 0, 0), pipeline_mode=once),
            scratch_shapes=[
                pltpu.VMEM((2 * own, rows), BF),
                pltpu.VMEM((rows, tile), BF),
                pltpu.VMEM((rows, tile), BF),
                pltpu.VMEM((2 * own, rows), BF),
                pltpu.VMEM((d, rows), BF),
                pltpu.VMEM((d, rows), BF),
                pltpu.SemaphoreType.DMA((3,)),
            ],
        ),
        out_shape=jax.ShapeDtypeStruct((2, height, d), BF),
        compiler_params=pltpu.CompilerParams(vmem_limit_bytes=60 << 20),
        cost_estimate=pl.CostEstimate(
            flops=9 * rows * d * tile * steps, bytes_accessed=16 * d * tile * steps, transcendentals=rows * tile * steps
        ),
        name="expert_pair",
    )(half, turned[0], b_pair, turned[1], turned[2], gy_pair, w1, b1, w2, u, dz)


def early_tile(j, h):
    return 2 * h + 4 * j


def late_tile(j, h):
    k = j - 2
    return jnp.where(j < 2, 2 * h + 1 + 4 * j, 2 * (1 - h) + lax.rem(k + 2, 2) + 4 * ((k + 2) // 2 - 1))


def dispatch_kernel(ids_ref, rows_ref, col_ref, row_ref, out_ref, early_ref, late_ref, *, slots, block, cut):
    n = ids_ref.shape[0]
    places = out_ref.shape[0]
    step = pl.program_id(0)

    @pl.when(step == 0)
    def _():
        ids = ids_ref[...]
        lanes = lax.broadcasted_iota(jnp.int32, (n, 128), 1)
        onehot = jnp.where(ids == lanes, 1.0, 0.0)
        tri = (lax.broadcasted_iota(jnp.int32, (block, block), 1) < lax.broadcasted_iota(jnp.int32, (block, block), 0)).astype(BF)
        carry = jnp.zeros((1, 128), F32)
        for s in range(0, n, block):
            own = onehot[s : s + block]
            before = dot(tri, own.astype(BF)) + carry
            slot = jnp.sum(before * own, 1, keepdims=True).astype(jnp.int32)
            col_ref[s : s + block] = ids[s : s + block] * slots + slot
            carry += jnp.sum(own, 0, keepdims=True)
        row_ref[...] = jnp.broadcast_to(col_ref[...].astype(F32), (n, 128)).T[:8].astype(jnp.int32)

    out = pick_places(row_ref, places, step, rows_ref)
    out_ref[...] = out

    @pl.when(step < cut)
    def _():
        early_ref[...] = out

    @pl.when(step >= cut)
    def _():
        late_ref[...] = out


def pick_places(row_ref, places, step, rows_ref):
    n = rows_ref.shape[0]
    place = lax.broadcasted_iota(jnp.int32, (places, n), 0) + places * step
    return dot((place == row_ref[0:1, :]).astype(BF), rows_ref[...]).astype(BF)


def dispatch(ids, rows, experts, slots, cut, block=256):
    n, width = rows.shape
    places = experts * slots
    steps = places // block
    return pl.pallas_call(
        functools.partial(dispatch_kernel, slots=slots, block=block, cut=cut),
        grid=(steps,),
        in_specs=[
            pl.BlockSpec((n, 1), lambda j: (0, 0)),
            pl.BlockSpec((n, width), lambda j: (0, 0), pipeline_mode=pl.Buffered(1)),
        ],
        out_specs=(
            pl.BlockSpec((n, 1), lambda j: (0, 0)),
            pl.BlockSpec((8, n), lambda j: (0, 0)),
            pl.BlockSpec((block, width), lambda j: (j, 0)),
            pl.BlockSpec((block, width), lambda j: (jnp.minimum(j, cut - 1), 0)),
            pl.BlockSpec((block, width), lambda j: (jnp.maximum(j - cut, 0), 0)),
        ),
        out_shape=(
            jax.ShapeDtypeStruct((n, 1), jnp.int32),
            jax.ShapeDtypeStruct((8, n), jnp.int32),
            jax.ShapeDtypeStruct((places, width), BF),
            jax.ShapeDtypeStruct((cut * block, width), BF),
            jax.ShapeDtypeStruct((places - cut * block, width), BF),
        ),
        compiler_params=pltpu.CompilerParams(vmem_limit_bytes=40 << 20),
        cost_estimate=pl.CostEstimate(flops=2 * n * places * width, bytes_accessed=2 * (n + places) * width, transcendentals=0),
        name="dispatch",
    )(ids, rows)


def unit_rows(hidden):
    centred = hidden - jnp.mean(hidden, -1, keepdims=True)
    return centred * lax.rsqrt(jnp.mean(centred * centred, -1, keepdims=True) + 1e-05)


def project_kernel(tok_ref, gain_ref, shift_ref, wq_ref, bq_ref, wk_ref, wv_ref, bv_ref, act_ref, q_ref, k_ref, v_ref, *, scale):
    act = (unit_rows(tok_ref[...].astype(F32)) * gain_ref[...] + shift_ref[...]).astype(BF)
    act_ref[...] = act
    q_ref[...] = ((dot(act, wq_ref[...]) + bq_ref[...]).astype(BF).astype(F32) * scale).astype(BF)
    k_ref[...] = dot(act, wk_ref[...]).astype(BF)
    v_ref[...] = (dot(act, wv_ref[...]) + bv_ref[...]).astype(BF)


def project(tokens, gain, shift, wq, bq, wk, wv, bv, scale, block=512):
    n, width = tokens.shape
    rows = pl.BlockSpec((block, width), lambda i: (i, 0))
    line = pl.BlockSpec((1, width), lambda i: (0, 0))
    matrix = pl.BlockSpec((width, width), lambda i: (0, 0), pipeline_mode=pl.Buffered(1))
    return pl.pallas_call(
        functools.partial(project_kernel, scale=scale),
        grid=(n // block,),
        in_specs=[rows, line, line, matrix, line, matrix, matrix, line],
        out_specs=(rows,) * 4,
        out_shape=(jax.ShapeDtypeStruct((n, width), BF),) * 4,
        compiler_params=pltpu.CompilerParams(vmem_limit_bytes=40 << 20),
        cost_estimate=pl.CostEstimate(flops=6 * n * width * width, bytes_accessed=16 * n * width, transcendentals=0),
        name="project",
    )(tokens, gain, shift, wq, bq, wk, wv, bv)


def after_attn_kernel(
    mixed_ref, tok_ref, w_ref, bias_ref, gain_ref, shift_ref, row_ref, hidden_ref, out_ref, act_ref, *, first, block
):
    step = pl.program_id(0)
    places = out_ref.shape[0]
    for i in range(first):

        @pl.when(step == i)
        def _(i=i):
            hidden = tok_ref[...].astype(F32) + dot(mixed_ref[...], w_ref[...]) + bias_ref[...]
            hidden_ref[...] = hidden
            act_ref[i * block : (i + 1) * block] = (unit_rows(hidden) * gain_ref[...] + shift_ref[...]).astype(BF)

    @pl.when(step >= first)
    def _():
        out_ref[...] = pick_places(row_ref, places, step - first, act_ref)


def after_attn(mixed, tokens, w, bias, gain, shift, target, places, block=512, place_block=640):
    n, width = tokens.shape
    first = n // block
    rows = pl.BlockSpec((block, width), lambda i: (jnp.minimum(i, first - 1), 0))
    line = pl.BlockSpec((1, width), lambda i: (0, 0))
    return pl.pallas_call(
        functools.partial(after_attn_kernel, first=first, block=block),
        grid=(first + places // place_block,),
        in_specs=[
            rows,
            rows,
            pl.BlockSpec((width, width), lambda i: (0, 0), pipeline_mode=pl.Buffered(1)),
            line,
            line,
            line,
            pl.BlockSpec((8, n), lambda i: (0, 0)),
        ],
        out_specs=(rows, pl.BlockSpec((place_block, width), lambda i: (jnp.maximum(i - first, 0), 0))),
        out_shape=(jax.ShapeDtypeStruct((n, width), F32), jax.ShapeDtypeStruct((places, width), BF)),
        scratch_shapes=[pltpu.VMEM((n, width), BF)],
        compiler_params=pltpu.CompilerParams(vmem_limit_bytes=40 << 20),
        cost_estimate=pl.CostEstimate(flops=4 * n * width * width, bytes_accessed=12 * n * width, transcendentals=0),
        name="after_attn",
    )(mixed, tokens, w, bias, gain, shift, target)


def after_experts_kernel(
    target_ref, home_ref, cot_ref, hidden_ref, gain_ref, w_out_ref, gh_ref, ga_ref, do_ref, sums_ref
):
    rows, width = cot_ref.shape
    places = home_ref.shape[0]
    pick = (lax.broadcasted_iota(jnp.int32, (rows, places), 1) == target_ref[...]).astype(BF)
    d = dot(pick, home_ref[...])
    hidden = hidden_ref[...]
    centred = hidden - jnp.mean(hidden, -1, keepdims=True)
    inv = lax.rsqrt(jnp.mean(centred * centred, -1, keepdims=True) + 1e-05)
    unit = centred * inv
    scaled = d * gain_ref[...]
    mean_one = jnp.mean(scaled, -1, keepdims=True)
    mean_two = jnp.mean(scaled * unit, -1, keepdims=True)
    grad = cot_ref[...].astype(F32) + inv * (scaled - mean_one - unit * mean_two)
    gh_ref[...] = grad
    low = grad.astype(BF)
    ga_ref[...] = low
    do_ref[...] = dot_nt(low, w_out_ref[...]).astype(BF)
    parts = [jnp.sum(low.astype(F32), 0, keepdims=True), jnp.sum(d * unit, 0, keepdims=True), jnp.sum(d, 0, keepdims=True)]
    parts = jnp.concatenate(parts + [jnp.zeros((8 - len(parts), width), F32)], 0)

    @pl.when(pl.program_id(0) == 0)
    def _():
        sums_ref[...] = parts

    @pl.when(pl.program_id(0) > 0)
    def _():
        sums_ref[...] += parts


def after_experts(target, home, cot, hidden, gain, w_out, block=256):
    n, width = cot.shape
    places = home.shape[0]
    rows = pl.BlockSpec((block, width), lambda i: (i, 0))
    once = pl.Buffered(1)
    return pl.pallas_call(
        after_experts_kernel,
        grid=(n // block,),
        in_specs=[
            pl.BlockSpec((block, 1), lambda i: (i, 0)),
            pl.BlockSpec((places, width), lambda i: (0, 0), pipeline_mode=once),
            rows,
            rows,
            pl.BlockSpec((1, width), lambda i: (0, 0)),
            pl.BlockSpec((width, width), lambda i: (0, 0), pipeline_mode=once),
        ],
        out_specs=(rows, rows, rows, pl.BlockSpec((8, width), lambda i: (0, 0))),
        out_shape=(
            jax.ShapeDtypeStruct((n, width), F32),
            jax.ShapeDtypeStruct((n, width), BF),
            jax.ShapeDtypeStruct((n, width), BF),
            jax.ShapeDtypeStruct((8, width), F32),
        ),
        compiler_params=pltpu.CompilerParams(vmem_limit_bytes=50 << 20),
        name="after_experts",
    )(target, home, cot, hidden, gain, w_out)


def backward_kernel(*refs, ep_bits, rep_bits, own, rblk, chunks, blk):
    len_ref, q_ref, k_ref, v_ref, o_ref, do_ref, lse_ref = refs[:7]
    act_ref, mixed_ref, ga_ref, wq_ref, wk_ref, wv_ref, tok_ref, gh_ref, gain_ref, sums_ref, bias_ref = refs[7:18]
    out_ref, da_ref, vec_out, bias_out = refs[18:22]
    at_ref, mt_ref, dq_ref, dk_ref, dv_ref, dqt_ref, dk_acc, dv_acc, x_ref = refs[22:31]
    bits = ep_bits + rep_bits
    got = refs[31 : 31 + bits]
    vec_got, vec_sum, bias_got, bias_sum, send, recv, vsend, vrecv, bsend, brecv = refs[31 + bits :]
    step = pl.program_id(0)
    n, width = act_ref.shape
    block = ga_ref.shape[1]
    lanes = q_ref.shape[1]
    ep, rep = 1 << ep_bits, 1 << rep_bits
    me_z = lax.axis_index("rep")
    me = lax.axis_index("ep")

    def bit(b):
        return lax.rem(me // (1 << b), 2) if b < ep_bits else lax.rem(me_z // (1 << (b - ep_bits)), 2)

    def flip(b):
        change = 1 - 2 * bit(b)
        return (me_z, me + change * (1 << b)) if b < ep_bits else (me_z + change * (1 << (b - ep_bits)), me)

    def order(c):
        rest = list(range(1, ep_bits))
        return [0] + (rest if c % 2 == 0 else rest[::-1]) + list(range(ep_bits, bits))

    def copy(src, dst, s, r, peer):
        return pltpu.make_async_remote_copy(
            src_ref=src, dst_ref=dst, send_sem=s, recv_sem=r, device_id=peer, device_id_type=pl.DeviceIdType.MESH
        )

    def cut(c, stage, value):
        done = order(c)[:stage]
        left = [b for b in range(ep_bits - 1, -1, -1) if b not in done]
        left += [b for b in range(bits - 1, ep_bits - 1, -1) if b not in done]
        index = [slice(None)] * len(left)
        index[left.index(order(c)[stage])] = value
        return tuple(index)

    def held(c, stage):
        return x_ref.at[c] if stage == 0 else got[stage - 1].at[c]

    def stage_copy(c, stage):
        b = order(c)[stage]
        return copy(
            held(c, stage).at[cut(c, stage, 1 - bit(b))], got[stage].at[c], send.at[c, stage], recv.at[c, stage], flip(b)
        )

    def advance(pair, stage):
        for c in (2 * pair, 2 * pair + 1):
            stage_copy(c, stage).wait()
            keep = held(c, stage)[cut(c, stage, bit(order(c)[stage]))]
            if stage + 1 < bits:
                got[stage][c] += keep
                stage_copy(c, stage + 1).start()
            else:
                out_ref[:, :, c * lanes : (c + 1) * lanes] = got[stage][c].astype(F32) + keep.astype(F32)

    def small_copy(k, got_ref, sum_ref, first, s, r):
        return copy(sum_ref.at[k - first], got_ref.at[k - first], s.at[k - first], r.at[k - first], flip(k))

    def vec_copy(k):
        return small_copy(k, vec_got, vec_sum, 0, vsend, vrecv)

    def bias_copy(k):
        return small_copy(k, bias_got, bias_sum, ep_bits, bsend, brecv)

    def vec_step(k):
        vec_copy(k).wait()
        vec_sum[k + 1] = vec_sum[k] + vec_got[k]
        if k + 1 < bits:
            vec_copy(k + 1).start()

    @pl.when(step == 0)
    def _():
        barrier = pltpu.get_barrier_semaphore()
        for b in range(bits):
            pl.semaphore_signal(barrier, inc=1, device_id=flip(b), device_id_type=pl.DeviceIdType.MESH)
        pl.semaphore_wait(barrier, bits)
        bias_sum[0] = bias_ref[...]
        bias_copy(ep_bits).start()
        at_ref[...] = act_ref[...].T
        mt_ref[...] = mixed_ref[...].T

    slot = lax.rem(step, 2)
    attn_bwd_kernel(
        len_ref, q_ref, k_ref, v_ref, o_ref, do_ref, lse_ref, dq_ref.at[slot], dk_ref.at[slot], dv_ref.at[slot],
        dqt_ref, dk_acc, dv_acc, blk=blk,
    )

    def put(c, w, left, right):
        g = dot(left[...], right).astype(BF)
        for r in range(rep):
            for e in range(ep):
                start = (r * ep + e) * own
                where = tuple((e >> b) & 1 for b in range(ep_bits - 1, -1, -1))
                where += tuple((r >> b) & 1 for b in range(rep_bits - 1, -1, -1))
                for k in range(2):
                    x_ref[(2 * c + k,) + where + (w,)] = g[start : start + own, k * lanes : (k + 1) * lanes]

    def norm_back():
        total_n = jnp.zeros((1, width), F32)
        total_d = jnp.zeros((1, width), F32)
        for s in range(0, n, rblk):
            rs = slice(s, s + rblk)
            d = da_ref[rs]
            hidden = tok_ref[rs].astype(F32)
            centred = hidden - jnp.mean(hidden, -1, keepdims=True)
            inv = lax.rsqrt(jnp.mean(centred * centred, -1, keepdims=True) + 1e-05)
            unit = centred * inv
            scaled = d * gain_ref[...]
            mean_one = jnp.mean(scaled, -1, keepdims=True)
            mean_two = jnp.mean(scaled * unit, -1, keepdims=True)
            da_ref[rs] = gh_ref[rs] + inv * (scaled - mean_one - unit * mean_two)
            total_n += jnp.sum(d * unit, 0, keepdims=True)
            total_d += jnp.sum(d, 0, keepdims=True)
        return total_n, total_d

    for c in range(chunks):

        @pl.when(step == 2 * c)
        def _(c=c):
            put(c, 3, mt_ref, ga_ref[...])
            for stage in range(0, bits, 2):
                if c - 1 - stage // 2 >= 0:
                    advance(c - 1 - stage // 2, stage)
            if 1 <= c <= rep_bits:
                k = c - 1
                bias_copy(ep_bits + k).wait()
                bias_sum[k + 1] = bias_sum[k] + bias_got[k]
                if k + 1 < rep_bits:
                    bias_copy(ep_bits + k + 1).start()

        @pl.when(step == 2 * c + 1)
        def _(c=c):
            dq = jnp.concatenate([dq_ref[0], dq_ref[1]], 1)
            dk = jnp.concatenate([dk_ref[0], dk_ref[1]], 1)
            dv = jnp.concatenate([dv_ref[0], dv_ref[1]], 1)
            put(c, 0, at_ref, dq)
            put(c, 1, at_ref, dk)
            put(c, 2, at_ref, dv)
            stage_copy(2 * c, 0).start()
            stage_copy(2 * c + 1, 0).start()
            for stage in range(1, bits, 2):
                if c - 1 - stage // 2 >= 0:
                    advance(c - 1 - stage // 2, stage)
            cols = slice(c * block, (c + 1) * block)
            vec_sum[0, 2:3, cols] = jnp.sum(dq.astype(F32), 0, keepdims=True)
            vec_sum[0, 3:4, cols] = jnp.sum(dv.astype(F32), 0, keepdims=True)
            vec_sum[0, 4:8, cols] = sums_ref[0:4, cols]
            if c == chunks - 1:
                advance(c, 0)
            for s in range(0, n, rblk):
                rs = slice(s, s + rblk)
                part = dot_nt(dq[rs], wq_ref[...]) + dot_nt(dk[rs], wk_ref[...]) + dot_nt(dv[rs], wv_ref[...])
                if c == 0:
                    da_ref[rs] = part
                else:
                    da_ref[rs] += part
            if c == chunks - 1:
                total_n, total_d = norm_back()
                vec_sum[0, 0:1] = total_n
                vec_sum[0, 1:2] = total_d
                vec_copy(0).start()
                waves = {}
                for d in range(chunks):
                    for stage in range(bits):
                        reached = 2 * (d + 1 + stage // 2) + stage % 2
                        if reached > 2 * c + 1 and (d, stage) != (c, 0):
                            waves.setdefault(d + stage, []).append((d, stage))
                k = 0
                for wave in sorted(waves):
                    for d, stage in reversed(waves[wave]):
                        advance(d, stage)
                    if k < bits:
                        vec_step(k)
                        k += 1
                for k in range(k, bits):
                    vec_step(k)
                vec_out[...] = vec_sum[bits]
                bias_out[...] = bias_sum[rep_bits]


def backward(length, q, k, v, o, do, lse, act, ga, wq, wk, wv, tokens, gh, gain, sums, bias, rep, ep, rblk=256, blk=256):
    n, width = act.shape
    own = width // (rep * ep)
    ep_bits, rep_bits = ep.bit_length() - 1, rep.bit_length() - 1
    bits = ep_bits + rep_bits
    lanes = 128
    block = 2 * lanes
    chunks = width // block
    once = pl.Buffered(1)
    whole = pl.BlockSpec((n, width), lambda j: (0, 0), pipeline_mode=once)
    pair = pl.BlockSpec((n, lanes), lambda j: (0, j))
    cols = pl.BlockSpec((n, block), lambda j: (0, j // 2))
    eight = pl.BlockSpec((8, width), lambda j: (0, 0))
    scratch = [
        pltpu.VMEM((width, n), BF),
        pltpu.VMEM((width, n), BF),
        pltpu.VMEM((2, n, lanes), BF),
        pltpu.VMEM((2, n, lanes), BF),
        pltpu.VMEM((2, n, lanes), BF),
        pltpu.VMEM((lanes, n), F32),
        pltpu.VMEM((n, lanes), F32),
        pltpu.VMEM((n, lanes), F32),
        pltpu.VMEM((2 * chunks,) + (2,) * bits + (4, own, lanes), BF),
    ]
    scratch += [pltpu.VMEM((2 * chunks,) + (2,) * (bits - 1 - k) + (4, own, lanes), BF) for k in range(bits)]
    scratch += [
        pltpu.VMEM((bits, 8, width), F32),
        pltpu.VMEM((bits + 1, 8, width), F32),
        pltpu.VMEM((rep_bits, 8, width), F32),
        pltpu.VMEM((rep_bits + 1, 8, width), F32),
        pltpu.SemaphoreType.DMA((2 * chunks, bits)),
        pltpu.SemaphoreType.DMA((2 * chunks, bits)),
        pltpu.SemaphoreType.DMA((bits,)),
        pltpu.SemaphoreType.DMA((bits,)),
        pltpu.SemaphoreType.DMA((rep_bits,)),
        pltpu.SemaphoreType.DMA((rep_bits,)),
    ]
    return pl.pallas_call(
        functools.partial(
            backward_kernel, ep_bits=ep_bits, rep_bits=rep_bits, own=own, rblk=rblk, chunks=chunks, blk=blk
        ),
        grid=(2 * chunks,),
        in_specs=[pl.BlockSpec(memory_space=pltpu.SMEM)]
        + [pair] * 5
        + [pl.BlockSpec((1, 2, n), lambda j: (j, 0, 0)), whole, whole, cols, cols, cols, cols, whole, whole]
        + [pl.BlockSpec((1, width), lambda j: (0, 0)), eight, eight],
        out_specs=(pl.BlockSpec((4, own, width), lambda j: (0, 0, 0)), whole, eight, eight),
        out_shape=(
            jax.ShapeDtypeStruct((4, own, width), F32),
            jax.ShapeDtypeStruct((n, width), F32),
            jax.ShapeDtypeStruct((8, width), F32),
            jax.ShapeDtypeStruct((8, width), F32),
        ),
        scratch_shapes=scratch,
        compiler_params=pltpu.CompilerParams(vmem_limit_bytes=63 << 20, collective_id=1, has_side_effects=True),
        name="backward",
    )(length, q, k, v, o, do, lse, act, o, ga, wq, wk, wv, tokens, gh, gain, sums, bias)


def combine_kernel(target_ref, back_ref, hidden_ref, out_ref):
    rows, places = hidden_ref.shape[0], back_ref.shape[0]
    pick = (lax.broadcasted_iota(jnp.int32, (rows, places), 1) == target_ref[...]).astype(BF)
    out_ref[...] = (hidden_ref[...] + dot(pick, back_ref[...])).astype(BF)


def combine(target, back, hidden, block=256):
    n, width = hidden.shape
    rows = pl.BlockSpec((block, width), lambda i: (i, 0))
    return pl.pallas_call(
        combine_kernel,
        grid=(n // block,),
        in_specs=[
            pl.BlockSpec((block, 1), lambda i: (i, 0)),
            pl.BlockSpec(back.shape, lambda i: (0, 0), pipeline_mode=pl.Buffered(1)),
            rows,
        ],
        out_specs=rows,
        out_shape=jax.ShapeDtypeStruct((n, width), BF),
        compiler_params=pltpu.CompilerParams(vmem_limit_bytes=40 << 20),
        name="combine",
    )(target, back, hidden)


def settle_kernel(where_ref, grad_ref, small_ref, bias_ref, gt_ref, small_out, bias1_out, bias2_out):
    gt_ref[...] = grad_ref[...]

    @pl.when(pl.program_id(0) == 0)
    def _():
        shift, row = where_ref[1], where_ref[2]
        small_out[...] = pltpu.roll(small_ref[...], shift, 1)[:, : small_out.shape[1]]
        bias1_out[...] = bias_ref[pl.ds(row, 1), :]
        wide = bias2_out.shape[1]
        bias2_out[...] = bias_ref[4:5, pl.ds(pl.multiple_of(row * wide, wide), wide)]


def settle(where, grad, small, bias, own, steps=4):
    n, d = grad.shape
    block = pl.BlockSpec((n // steps, d), lambda i: (i, 0))

    def fixed(shape):
        return pl.BlockSpec(shape, lambda i: (0, 0))

    return pl.pallas_call(
        settle_kernel,
        grid=(steps,),
        in_specs=[pl.BlockSpec(memory_space=pltpu.SMEM), block, fixed((8, d)), fixed((8, d))],
        out_specs=(block, fixed((8, 128)), fixed((1, d)), fixed((1, own))),
        out_shape=(
            jax.ShapeDtypeStruct((n, d), F32),
            jax.ShapeDtypeStruct((8, 128), F32),
            jax.ShapeDtypeStruct((1, d), F32),
            jax.ShapeDtypeStruct((1, own), F32),
        ),
        compiler_params=pltpu.CompilerParams(vmem_limit_bytes=40 << 20),
        name="settle",
    )(where, grad, small, bias)


def unpack_kernel(where_ref, a1_ref, b1_ref, c1_ref, d1_ref, a2_ref, b2_ref, g1_ref, g2_ref, *, tile):
    per_row = a1_ref.shape[1] // tile
    h = where_ref[0]
    g2_ref[0] = a2_ref[...].astype(F32)
    g2_ref[1] = b2_ref[...].astype(F32)
    for refs, tile_of in (((a1_ref,), early_tile), ((b1_ref, c1_ref, d1_ref), late_tile)):
        for j in range(len(refs) * per_row):
            start = pl.multiple_of(tile_of(j, h) * tile, tile)
            c = tile * (j % per_row)
            g1_ref[:, pl.ds(start, tile)] = refs[j // per_row][:, c : c + tile].astype(F32)


def unpack_grads(where, a, b, tile, ff, rep, steps=4):
    d = a.shape[1]
    own = d // rep
    rows = own // steps
    base = tile // rows

    def line(k):
        return pl.BlockSpec((rows, d), lambda i: (base + k * steps + i, 0))

    second = pl.BlockSpec((tile // steps, d), lambda i: (i, 0))
    g1, g2 = pl.pallas_call(
        functools.partial(unpack_kernel, tile=tile),
        grid=(steps,),
        in_specs=[pl.BlockSpec(memory_space=pltpu.SMEM), line(0), line(0), line(1), line(2), second, second],
        out_specs=(
            pl.BlockSpec((rows, ff), lambda i: (i, 0)),
            pl.BlockSpec((2, tile // steps, d), lambda i: (0, i, 0)),
        ),
        out_shape=(jax.ShapeDtypeStruct((own, ff), F32), jax.ShapeDtypeStruct((2, tile, d), F32)),
        compiler_params=pltpu.CompilerParams(vmem_limit_bytes=60 << 20),
        name="unpack_grads",
    )(where, a, b, b, b, a, b)
    return g1, g2.reshape(2 * tile, d)


def per_device(
    tokens,
    cotangent,
    lengths,
    expert_ids,
    norm1_gain,
    norm1_bias,
    w_query,
    b_query,
    w_key,
    w_value,
    b_value,
    w_out,
    b_out,
    norm2_gain,
    norm2_bias,
    w_in,
    b_in,
    w_back,
    b_back,
):
    row_count, width = tokens.shape
    head_dim = width // HEADS
    ep = lax.axis_size("ep")
    rep = lax.axis_size("rep")
    slots = 5 * row_count // (4 * ep)
    places = ep * slots
    ff = w_in.shape[2]
    w_first = w_in[0]
    w_second = w_back[0]

    def exchange(rows):
        sent = lax.all_to_all(rows.reshape(ep, slots, width), "ep", 0, 0, tiled=True)
        return sent.reshape(places, width)

    at = lax.axis_index("rep")
    swap = [(i, i ^ 1) for i in range(rep)]
    target, target_row, grad_send, early, tail = dispatch(expert_ids, cotangent, ep, slots, 3)
    grad_rows = exchange(grad_send)
    early = lax.ppermute(early, "rep", swap)
    act_a, queries, keys, values = project(
        tokens, norm1_gain[None], norm1_bias[None], w_query, b_query[None], w_key, w_value, b_value[None], head_dim**-0.5
    )
    mixed, lse = attn_fwd(queries, keys, values, lengths)
    mixed, grad_rows, early, tail = lax.optimization_barrier((mixed, grad_rows, early, tail))
    late = lax.ppermute(tail, "rep", swap)
    hidden_one, rows_out = after_attn(
        mixed, tokens, w_out, b_out[None], norm2_gain[None], norm2_bias[None], target_row, places
    )
    rows_in = exchange(rows_out)
    rows_in, both = lax.optimization_barrier((rows_in, jnp.concatenate([early, late], 0)))
    grad_pair = exchange(both)
    rows_pair = lax.ppermute(rows_in, "rep", swap)
    own_fn = functools.partial(expert_own, tile=ff // 4)
    own_out = jax.eval_shape(own_fn, rows_in, grad_rows, w_first, b_in, w_second)
    own_all = lax.cond(
        lengths[0] > 0,
        own_fn,
        lambda *_: tuple(jnp.zeros(x.shape, x.dtype) for x in own_out),
        rows_in,
        grad_rows,
        w_first,
        b_in,
        w_second,
    )
    active, grad_inner, g_bias_first, grad_input, g_bias_second = own_all
    grad_home = exchange(grad_input)
    half = (at & 1).astype(jnp.int32)[None]
    turned = turn(half, rows_in, grad_rows, grad_pair, rep)
    active, grad_inner, g_bias_first, rows_pair, grad_pair, turned = lax.optimization_barrier(
        (active, grad_inner, g_bias_first, rows_pair, grad_pair, turned)
    )

    def pair(tile_of, steps):
        return expert_pair(
            half, turned, rows_pair, grad_pair, w_first, b_in, w_second, active, grad_inner, tile_of, steps, ff // 8, rep
        )

    groups = [[0, 2], [1, 3]]
    part_0 = pair(early_tile, 2)
    rows_pair, grad_home, active, part_0 = lax.optimization_barrier((rows_pair, grad_home, active, part_0))
    sum_0 = lax.psum_scatter(part_0, "rep", scatter_dimension=0, axis_index_groups=groups, tiled=True)
    result = (dot(active, w_second) + b_back[0]).astype(BF)
    rows_pair, result = lax.optimization_barrier((rows_pair, result))
    returned = exchange(result)
    part_1 = pair(late_tile, 6)
    returned, part_1 = lax.optimization_barrier((returned, part_1))
    sum_1 = lax.psum_scatter(part_1, "rep", scatter_dimension=0, axis_index_groups=groups, tiled=True)
    block_out = combine(target, returned, hidden_one)
    grad_home, block_out = lax.optimization_barrier((grad_home, block_out))

    def remainder(grad_home, g_bias_first, g_bias_second):
        grad_hidden, grad_attn, grad_mixed, sums = after_experts(
            target, grad_home, cotangent, hidden_one, norm2_gain[None], w_out
        )
        bias = jnp.concatenate([g_bias_first.reshape(ff // width, width), g_bias_second], 0)
        bias = jnp.pad(bias, ((0, 8 - bias.shape[0]), (0, 0)))
        return backward(
            lengths, queries, keys, values, mixed, grad_mixed, lse, act_a, grad_attn, w_query, w_key, w_value, tokens,
            grad_hidden, norm1_gain[None], sums, bias, rep, ep,
        )

    own = width // (rep * ep)
    own_ff, own_width = ff // rep, width // rep
    args = (grad_home, g_bias_first, g_bias_second)
    shapes = jax.eval_shape(remainder, *args)
    dense, grad_rows_in, small, grad_bias = lax.cond(
        lengths[0] > 0, remainder, lambda *_: jax.tree.map(lambda x: jnp.zeros(x.shape, x.dtype), shapes), *args
    )
    place = at * ep + lax.axis_index("ep")
    where = jnp.stack([at & 1, lax.rem(width - place * own, width), at]).astype(jnp.int32)
    grad_tokens, small, out_bias_first, out_bias_second = settle(where, grad_rows_in, small, grad_bias, width // rep)
    where, grad_tokens, small = lax.optimization_barrier((where, grad_tokens, small))
    out_first, out_second = unpack_grads(where, sum_0[0], sum_1[0], ff // 8, ff, rep)
    small = small[:, :own]
    out_first, out_second = out_first[None], out_second[None]
    return (
        block_out,
        grad_tokens,
        small[0],
        small[1],
        dense[0],
        small[2],
        dense[1],
        dense[2],
        small[3],
        dense[3],
        small[4],
        small[5],
        small[6],
        out_first,
        out_bias_first,
        out_second,
        out_bias_second,
    )


def solution(mesh):
    return jax.shard_map(
        per_device,
        mesh=mesh,
        in_specs=(
            P(("rep", "ep"), None),
            P(("rep", "ep"), None),
            P(("rep", "ep")),
            P(("rep", "ep"), None),
            P(),
            P(),
            P(),
            P(),
            P(),
            P(),
            P(),
            P(),
            P(),
            P(),
            P(),
            P("ep", None, None),
            P("ep", None),
            P("ep", None, None),
            P("ep", None),
        ),
        out_specs=(
            P(("rep", "ep"), None),
            P(("rep", "ep"), None),
            P(("rep", "ep")),
            P(("rep", "ep")),
            P(("rep", "ep"), None),
            P(("rep", "ep")),
            P(("rep", "ep"), None),
            P(("rep", "ep"), None),
            P(("rep", "ep")),
            P(("rep", "ep"), None),
            P(("rep", "ep")),
            P(("rep", "ep")),
            P(("rep", "ep")),
            P("ep", "rep", None),
            P("ep", "rep"),
            P("ep", "rep", None),
            P("ep", "rep"),
        ),
        check_vma=False,
    )
```

```python
import functools

import jax
import jax.numpy as jnp
from jax import lax
from jax.experimental import pallas as pl
from jax.experimental.pallas import tpu as pltpu
from jax.sharding import PartitionSpec as P

HEADS = 16
BF = jnp.bfloat16
F32 = jnp.float32
LOG2E = 1.4426950408889634
NEG = -1e30


def dot(left, right):
    return jnp.dot(left, right, preferred_element_type=F32)


def dot_nt(left, right):
    return lax.dot_general(left, right, (((1,), (1,)), ((), ())), preferred_element_type=F32)


def dot_tn(left, right):
    return lax.dot_general(left, right, (((0,), (0,)), ((), ())), preferred_element_type=F32)


def attn_fwd_kernel(len_ref, q_ref, k_ref, v_ref, o_ref, lse_ref, ot_ref, *, blk):
    n, lanes = q_ref.shape
    half = lanes//2
    length = len_ref[0]
    k = k_ref[...].astype(F32)
    lane = lax.broadcasted_iota(jnp.int32,(n,lanes),1)
    row = lax.broadcasted_iota(jnp.int32,(n,lanes),0)
    bias = jnp.where(row<length, 0.0, NEG)
    k_a = jnp.where(lane<half, k, jnp.where(lane==half, bias, 0.0)).astype(BF)
    k_b = jnp.where(lane>=half, k, jnp.where(lane==0, bias, 0.0)).astype(BF)
    qt = q_ref[...].T
    vt = v_ref[...].T
    trow = lax.broadcasted_iota(jnp.int32,(lanes,n),0)
    qt32 = qt.astype(F32)
    qt_a = jnp.where(trow==half, 1.0, qt32).astype(BF)
    qt_b = jnp.where(trow==0, 1.0, qt32).astype(BF)
    tri = lax.broadcasted_iota(jnp.int32,(blk,blk),0) <= lax.broadcasted_iota(jnp.int32,(blk,blk),1)
    ones = jnp.ones((16,n),BF)
    for h,(kk,qq) in enumerate(((k_a,qt_a),(k_b,qt_b))):
        v_ext = jnp.concatenate([vt[h*half:(h+1)*half], ones],0)
        for i in range(n//blk):
            cols = slice(i*blk,(i+1)*blk)
            qb = qq[:,cols]
            diag = jnp.where(tri, dot(kk[cols],qb), NEG)
            if i:
                past = dot(kk[:i*blk],qb)
                top = jnp.maximum(jnp.max(past,0,keepdims=True),jnp.max(diag,0,keepdims=True))
                p = jnp.concatenate([jnp.exp2((past-top)*LOG2E).astype(BF),jnp.exp2((diag-top)*LOG2E).astype(BF)],0)
            else:
                top = jnp.max(diag,0,keepdims=True)
                p = jnp.exp2((diag-top)*LOG2E).astype(BF)
            r = dot(v_ext[:,:(i+1)*blk],p)
            total = r[half:half+1]
            ot_ref[h*half:(h+1)*half,cols] = r[:half]/total
            lse_ref[0,h:h+1,cols] = top + jnp.log(total)
    o_ref[...] = ot_ref[...].T.astype(BF)

def attn_fwd(q, k, v, length, blk=512):
    n, d = q.shape
    pairs = d // 128
    spec = pl.BlockSpec((n, 128), lambda h: (0, h))
    return pl.pallas_call(
        functools.partial(attn_fwd_kernel, blk=blk),
        grid=(pairs,),
        in_specs=[pl.BlockSpec(memory_space=pltpu.SMEM), spec, spec, spec],
        out_specs=(spec, pl.BlockSpec((1, 2, n), lambda h: (h, 0, 0))),
        out_shape=(jax.ShapeDtypeStruct((n, d), BF), jax.ShapeDtypeStruct((pairs, 2, n), F32)),
        scratch_shapes=[pltpu.VMEM((128, n), F32)],
        compiler_params=pltpu.CompilerParams(vmem_limit_bytes=50 << 20),
        cost_estimate=pl.CostEstimate(flops=8 * n * n * d, bytes_accessed=8 * n * d, transcendentals=8 * n * n),
        name="attn_fwd",
    )(length, q, k, v)


def split3(x):
    a=x.astype(BF).astype(F32); r=x-a
    b=r.astype(BF).astype(F32); c=r-b
    return a,b,c

def attn_bwd_kernel(len_ref, q_ref, k_ref, v_ref, o_ref, do_ref, lse_ref, dq_ref, dk_ref, dv_ref, dqt_ref, dk_acc, dv_acc, *, blk):
    n, lanes = q_ref.shape
    half = lanes//2
    length = len_ref[0]
    lane = lax.broadcasted_iota(jnp.int32,(n,lanes),1)
    row = lax.broadcasted_iota(jnp.int32,(n,lanes),0)
    trow = lax.broadcasted_iota(jnp.int32,(lanes,n),0)
    bias = jnp.where(row<length, 0.0, NEG)
    q = q_ref[...].astype(F32); k = k_ref[...].astype(F32); v=v_ref[...].astype(F32); do=do_ref[...].astype(F32)
    kt = k_ref[...].T
    qt = q_ref[...].T.astype(F32)
    dot_t = do_ref[...].T.astype(F32)
    ot = o_ref[...].T.astype(F32)
    prod = dot_t*ot
    heads=[]
    for h in range(2):
        own = (lane<half) if h==0 else (lane>=half)
        base = half if h==0 else 0
        delta = jnp.sum(prod[h*half:(h+1)*half],0,keepdims=True)
        lse = lse_ref[0,h:h+1,:]
        l1,l2,l3 = split3(-lse)
        d1,d2,d3 = split3(-delta)
        one = jnp.where((lane>=base+1)&(lane<=base+3),1.0,0.0)
        k_x = jnp.where(own,k,jnp.where(lane==base,bias,one)).astype(BF)
        v_x = jnp.where(own,v,one).astype(BF)
        q_x = jnp.where(trow==base,1.0,jnp.where(trow==base+1,l1,jnp.where(trow==base+2,l2,jnp.where(trow==base+3,l3,qt)))).astype(BF)
        d_x = jnp.where(trow==base+1,d1,jnp.where(trow==base+2,d2,jnp.where(trow==base+3,d3,dot_t))).astype(BF)
        q_own = jnp.where(own,q,0.0).astype(BF)
        do_own = jnp.where(own,do,0.0).astype(BF)
        heads.append((k_x,v_x,q_x,d_x,q_own,do_own))
    tri = lax.broadcasted_iota(jnp.int32,(blk,blk),0) <= lax.broadcasted_iota(jnp.int32,(blk,blk),1)
    steps=n//blk
    for i in reversed(range(steps)):
        cols = slice(i*blk,(i+1)*blk)
        ps=[];dss=[]
        for h in range(2):
            k_x,v_x,q_x,d_x,q_own,do_own=heads[h]
            qb=q_x[:,cols]; db=d_x[:,cols]
            p_d = jnp.exp2(jnp.where(tri,dot(k_x[cols],qb),NEG)*LOG2E)
            ds_d = p_d*dot(v_x[cols],db)
            if i:
                p_p = jnp.exp2(dot(k_x[:i*blk],qb)*LOG2E)
                ds_p = p_p*dot(v_x[:i*blk],db)
                p=jnp.concatenate([p_p.astype(BF),p_d.astype(BF)],0)
                ds=jnp.concatenate([ds_p.astype(BF),ds_d.astype(BF)],0)
            else:
                p=p_d.astype(BF); ds=ds_d.astype(BF)
            dqt_ref[h*half:(h+1)*half,cols]=dot(kt[h*half:(h+1)*half,:(i+1)*blk],ds)
            ps.append(p);dss.append(ds)
        dv_new = dot(ps[0],heads[0][5][cols])+dot(ps[1],heads[1][5][cols])
        dk_new = dot(dss[0],heads[0][4][cols])+dot(dss[1],heads[1][4][cols])
        if i==steps-1:
            dv_acc[...]=dv_new; dk_acc[...]=dk_new
        else:
            dv_acc[:(i+1)*blk]+=dv_new; dk_acc[:(i+1)*blk]+=dk_new
    scale=half**-0.5
    dq_ref[...]=(dqt_ref[...]*scale).T.astype(BF)
    dk_ref[...]=dk_acc[...].astype(BF)
    dv_ref[...]=dv_acc[...].astype(BF)

C0=0.7978845608028654; C1=C0*0.044715

def act_both(z):
    z2=z*z
    a=C1*z2+C0
    t=jnp.tanh(z*a)
    h=0.5*t+0.5
    u=z*h
    q=6.0*a-4.0*C0
    return u, h+u*(1.0-h)*q

def expert_own_kernel(
    b_ref, gy_ref, w1_ref, b1_ref, w2_ref, u_ref, dz_ref, gb1_ref, db_ref, gb2_ref, acc_ref, *, rblk
):
    step = pl.program_id(0)
    rows = b_ref.shape[0]
    w1 = w1_ref[...]
    w2 = w2_ref[...]
    bias = b1_ref[...]
    total = None
    for s in range(0, rows, rblk):
        rs = slice(s, s + rblk)
        u, slope = act_both(dot(b_ref[rs, :], w1) + bias)
        u_ref[rs, :] = u.astype(BF)
        dz = dot_nt(gy_ref[rs, :], w2) * slope
        dz_ref[rs, :] = dz.astype(BF)
        part = jnp.sum(dz, 0, keepdims=True)
        total = part if total is None else total + part
    gb1_ref[...] = total

    @pl.when(step == 0)
    def _():
        total = jnp.zeros_like(gb2_ref)
        for s in range(0, rows, rblk):
            rs = slice(s, s + rblk)
            acc_ref[rs, :] = dot_nt(dz_ref[rs, :], w1)
            total += jnp.sum(gy_ref[rs, :].astype(F32), 0, keepdims=True)
        gb2_ref[...] = total

    @pl.when(step > 0)
    def _():
        for s in range(0, rows, rblk):
            rs = slice(s, s + rblk)
            acc_ref[rs, :] += dot_nt(dz_ref[rs, :], w1)

    @pl.when(step == pl.num_programs(0) - 1)
    def _():
        db_ref[...] = acc_ref[...].astype(BF)


def expert_own(b, gy, w1, b1, w2, tile, rblk=256):
    rows, d = b.shape
    ff = w1.shape[1]
    whole = pl.BlockSpec((rows, d), lambda j: (0, 0), pipeline_mode=pl.Buffered(1))
    return pl.pallas_call(
        functools.partial(expert_own_kernel, rblk=rblk),
        grid=(ff // tile,),
        in_specs=[
            whole,
            whole,
            pl.BlockSpec((d, tile), lambda j: (0, j)),
            pl.BlockSpec((1, tile), lambda j: (0, j)),
            pl.BlockSpec((tile, d), lambda j: (j, 0)),
        ],
        out_specs=(
            pl.BlockSpec((rows, tile), lambda j: (0, j)),
            pl.BlockSpec((rows, tile), lambda j: (0, j)),
            pl.BlockSpec((1, tile), lambda j: (0, j)),
            pl.BlockSpec((rows, d), lambda j: (0, 0)),
            pl.BlockSpec((1, d), lambda j: (0, 0)),
        ),
        out_shape=(
            jax.ShapeDtypeStruct((rows, ff), BF),
            jax.ShapeDtypeStruct((rows, ff), BF),
            jax.ShapeDtypeStruct((1, ff), F32),
            jax.ShapeDtypeStruct((rows, d), BF),
            jax.ShapeDtypeStruct((1, d), F32),
        ),
        scratch_shapes=[pltpu.VMEM((rows, d), F32)],
        compiler_params=pltpu.CompilerParams(vmem_limit_bytes=60 << 20),
        cost_estimate=pl.CostEstimate(flops=8 * rows * d * ff, bytes_accessed=4 * d * ff, transcendentals=rows * ff),
        name="expert_own",
    )(b, gy, w1, b1, w2)


def turn_kernel(half_ref, bo0_ref, bo1_ref, gyo_ref, gyp_ref, bto_ref, gto_ref, gtp_ref):
    @pl.when(pl.program_id(0) == 0)
    def _():
        bto_ref[...] = bo0_ref[...].T

    @pl.when(pl.program_id(0) == 1)
    def _():
        bto_ref[...] = bo1_ref[...].T

    gto_ref[...] = gyo_ref[...].T
    gtp_ref[...] = gyp_ref[...].T


def turn(half, b, gy, gy_pair, rep):
    rows, d = b.shape
    own = d // rep
    block = d // rep
    cols = pl.BlockSpec((rows, block), lambda j, h: (0, j))
    turned = pl.BlockSpec((block, rows), lambda j, h: (j, 0))
    return pl.pallas_call(
        turn_kernel,
        grid_spec=pltpu.PrefetchScalarGridSpec(
            num_scalar_prefetch=1,
            grid=(rep,),
            in_specs=[
                pl.BlockSpec((rows, own), lambda j, h: (0, h[0])),
                pl.BlockSpec((rows, own), lambda j, h: (0, h[0] + 2)),
                cols,
                cols,
            ],
            out_specs=(pl.BlockSpec((own, rows), lambda j, h: (jnp.minimum(j, 1), 0)), turned, turned),
        ),
        out_shape=(
            jax.ShapeDtypeStruct((2 * own, rows), BF),
            jax.ShapeDtypeStruct((d, rows), BF),
            jax.ShapeDtypeStruct((d, rows), BF),
        ),
        compiler_params=pltpu.CompilerParams(vmem_limit_bytes=62 << 20),
        cost_estimate=pl.CostEstimate(flops=1, bytes_accessed=10 * rows * d, transcendentals=0),
        name="turn",
    )(half, b, b, gy, gy_pair)


def pair_kernel(
    half_ref, bto_any, bp_ref, gto_any, gtp_any, gyp_ref, w1_ref, b1_ref, w2_ref, u_ref, dz_ref,
    out_ref, btp_ref, up_ref, dzp_ref, bto_ref, gto_ref, gtp_ref, sems, *, seconds, rblk,
):
    step = pl.program_id(0)
    rows = bp_ref.shape[0]
    own = bto_ref.shape[0] // 2
    tile = w1_ref.shape[1]

    fetched = [
        pltpu.make_async_copy(src, dst, sems.at[i])
        for i, (src, dst) in enumerate(((bto_any, bto_ref), (gto_any, gto_ref), (gtp_any, gtp_ref)))
    ]

    @pl.when(step == 0)
    def _():
        for copy in fetched:
            copy.start()
        for k in range(2):
            start = pl.multiple_of((half_ref[0] + 2 * k) * own, own)
            btp_ref[k * own : (k + 1) * own] = bp_ref[:, pl.ds(start, own)].T

    w1 = w1_ref[...]
    w2 = w2_ref[...]
    bias = b1_ref[...]
    for s in range(0, rows, rblk):
        rs = slice(s, s + rblk)
        u, slope = act_both(dot(bp_ref[rs, :], w1) + bias)
        up_ref[rs, :] = u.astype(BF)
        dzp_ref[rs, :] = (dot_nt(gyp_ref[rs, :], w2) * slope).astype(BF)

    @pl.when(step == 0)
    def _():
        for copy in fetched:
            copy.wait()

    g1 = (dot(bto_ref[...], dz_ref[...]) + dot(btp_ref[...], dzp_ref[...])).astype(BF)
    per_row = out_ref.shape[2] // tile
    base = 2 * tile // 2
    where = pl.ds(pl.multiple_of(base + own * (step // per_row), own), own)
    column = pl.ds(pl.multiple_of(tile * lax.rem(step, per_row), tile), tile)
    out_ref[0, where, column] = g1[:own]
    out_ref[1, where, column] = g1[own:]

    @pl.when(step < seconds)
    def _():
        g2 = dot(gto_ref[...], u_ref[...]) + dot(gtp_ref[...], up_ref[...])
        out_ref[step, :tile] = g2.astype(BF).T


def expert_pair(half, turned, b_pair, gy_pair, w1, b1, w2, u, dz, tile_of, steps, tile, rep, rblk=256):
    rows, d = b_pair.shape
    own = d // rep
    once = pl.Buffered(1)
    per_row = d // tile
    height = tile + own * (steps // per_row)

    hbm = pl.BlockSpec(memory_space=pl.ANY)

    def fixed(shape, index=(0, 0)):
        return pl.BlockSpec(shape, lambda j, h: index, pipeline_mode=once)

    return pl.pallas_call(
        functools.partial(pair_kernel, seconds=2, rblk=rblk),
        grid_spec=pltpu.PrefetchScalarGridSpec(
            num_scalar_prefetch=1,
            grid=(steps,),
            in_specs=[
                hbm,
                fixed((rows, d)),
                hbm,
                hbm,
                fixed((rows, d)),
                pl.BlockSpec((d, tile), lambda j, h: (0, tile_of(j, h[0]))),
                pl.BlockSpec((1, tile), lambda j, h: (0, tile_of(j, h[0]))),
                pl.BlockSpec((tile, d), lambda j, h: (tile_of(j, h[0]), 0)),
                pl.BlockSpec((rows, tile), lambda j, h: (0, tile_of(j, h[0]))),
                pl.BlockSpec((rows, tile), lambda j, h: (0, tile_of(j, h[0]))),
            ],
            out_specs=pl.BlockSpec((2, height, d), lambda j, h: (0, 0, 0), pipeline_mode=once),
            scratch_shapes=[
                pltpu.VMEM((2 * own, rows), BF),
                pltpu.VMEM((rows, tile), BF),
                pltpu.VMEM((rows, tile), BF),
                pltpu.VMEM((2 * own, rows), BF),
                pltpu.VMEM((d, rows), BF),
                pltpu.VMEM((d, rows), BF),
                pltpu.SemaphoreType.DMA((3,)),
            ],
        ),
        out_shape=jax.ShapeDtypeStruct((2, height, d), BF),
        compiler_params=pltpu.CompilerParams(vmem_limit_bytes=60 << 20),
        cost_estimate=pl.CostEstimate(
            flops=9 * rows * d * tile * steps, bytes_accessed=16 * d * tile * steps, transcendentals=rows * tile * steps
        ),
        name="expert_pair",
    )(half, turned[0], b_pair, turned[1], turned[2], gy_pair, w1, b1, w2, u, dz)


def early_tile(j, h):
    return 2 * h + 4 * j


def late_tile(j, h):
    k = j - 2
    return jnp.where(j < 2, 2 * h + 1 + 4 * j, 2 * (1 - h) + lax.rem(k + 2, 2) + 4 * ((k + 2) // 2 - 1))


def dispatch_kernel(ids_ref, rows_ref, col_ref, row_ref, out_ref, early_ref, late_ref, *, slots, block, cut):
    n = ids_ref.shape[0]
    places = out_ref.shape[0]
    step = pl.program_id(0)

    @pl.when(step == 0)
    def _():
        ids = ids_ref[...]
        lanes = lax.broadcasted_iota(jnp.int32, (n, 128), 1)
        onehot = jnp.where(ids == lanes, 1.0, 0.0)
        tri = (lax.broadcasted_iota(jnp.int32, (block, block), 1) < lax.broadcasted_iota(jnp.int32, (block, block), 0)).astype(BF)
        carry = jnp.zeros((1, 128), F32)
        for s in range(0, n, block):
            own = onehot[s : s + block]
            before = dot(tri, own.astype(BF)) + carry
            slot = jnp.sum(before * own, 1, keepdims=True).astype(jnp.int32)
            col_ref[s : s + block] = ids[s : s + block] * slots + slot
            carry += jnp.sum(own, 0, keepdims=True)
        row_ref[...] = jnp.broadcast_to(col_ref[...].astype(F32), (n, 128)).T[:8].astype(jnp.int32)

    out = pick_places(row_ref, places, step, rows_ref)
    out_ref[...] = out

    @pl.when(step < cut)
    def _():
        early_ref[...] = out

    @pl.when(step >= cut)
    def _():
        late_ref[...] = out


def pick_places(row_ref, places, step, rows_ref):
    n = rows_ref.shape[0]
    place = lax.broadcasted_iota(jnp.int32, (places, n), 0) + places * step
    return dot((place == row_ref[0:1, :]).astype(BF), rows_ref[...]).astype(BF)


def dispatch(ids, rows, experts, slots, cut, block=256):
    n, width = rows.shape
    places = experts * slots
    steps = places // block
    return pl.pallas_call(
        functools.partial(dispatch_kernel, slots=slots, block=block, cut=cut),
        grid=(steps,),
        in_specs=[
            pl.BlockSpec((n, 1), lambda j: (0, 0)),
            pl.BlockSpec((n, width), lambda j: (0, 0), pipeline_mode=pl.Buffered(1)),
        ],
        out_specs=(
            pl.BlockSpec((n, 1), lambda j: (0, 0)),
            pl.BlockSpec((8, n), lambda j: (0, 0)),
            pl.BlockSpec((block, width), lambda j: (j, 0)),
            pl.BlockSpec((block, width), lambda j: (jnp.minimum(j, cut - 1), 0)),
            pl.BlockSpec((block, width), lambda j: (jnp.maximum(j - cut, 0), 0)),
        ),
        out_shape=(
            jax.ShapeDtypeStruct((n, 1), jnp.int32),
            jax.ShapeDtypeStruct((8, n), jnp.int32),
            jax.ShapeDtypeStruct((places, width), BF),
            jax.ShapeDtypeStruct((cut * block, width), BF),
            jax.ShapeDtypeStruct((places - cut * block, width), BF),
        ),
        compiler_params=pltpu.CompilerParams(vmem_limit_bytes=40 << 20),
        cost_estimate=pl.CostEstimate(flops=2 * n * places * width, bytes_accessed=2 * (n + places) * width, transcendentals=0),
        name="dispatch",
    )(ids, rows)


def unit_rows(hidden):
    centred = hidden - jnp.mean(hidden, -1, keepdims=True)
    return centred * lax.rsqrt(jnp.mean(centred * centred, -1, keepdims=True) + 1e-05)


def project_kernel(tok_ref, gain_ref, shift_ref, wq_ref, bq_ref, wk_ref, wv_ref, bv_ref, act_ref, q_ref, k_ref, v_ref, *, scale):
    act = (unit_rows(tok_ref[...].astype(F32)) * gain_ref[...] + shift_ref[...]).astype(BF)
    act_ref[...] = act
    q_ref[...] = ((dot(act, wq_ref[...]) + bq_ref[...]).astype(BF).astype(F32) * scale).astype(BF)
    k_ref[...] = dot(act, wk_ref[...]).astype(BF)
    v_ref[...] = (dot(act, wv_ref[...]) + bv_ref[...]).astype(BF)


def project(tokens, gain, shift, wq, bq, wk, wv, bv, scale, block=512):
    n, width = tokens.shape
    rows = pl.BlockSpec((block, width), lambda i: (i, 0))
    line = pl.BlockSpec((1, width), lambda i: (0, 0))
    matrix = pl.BlockSpec((width, width), lambda i: (0, 0), pipeline_mode=pl.Buffered(1))
    return pl.pallas_call(
        functools.partial(project_kernel, scale=scale),
        grid=(n // block,),
        in_specs=[rows, line, line, matrix, line, matrix, matrix, line],
        out_specs=(rows,) * 4,
        out_shape=(jax.ShapeDtypeStruct((n, width), BF),) * 4,
        compiler_params=pltpu.CompilerParams(vmem_limit_bytes=40 << 20),
        cost_estimate=pl.CostEstimate(flops=6 * n * width * width, bytes_accessed=16 * n * width, transcendentals=0),
        name="project",
    )(tokens, gain, shift, wq, bq, wk, wv, bv)


def after_attn_kernel(
    mixed_ref, tok_ref, w_ref, bias_ref, gain_ref, shift_ref, row_ref, hidden_ref, out_ref, act_ref, *, first, block
):
    step = pl.program_id(0)
    places = out_ref.shape[0]
    for i in range(first):

        @pl.when(step == i)
        def _(i=i):
            hidden = tok_ref[...].astype(F32) + dot(mixed_ref[...], w_ref[...]) + bias_ref[...]
            hidden_ref[...] = hidden
            act_ref[i * block : (i + 1) * block] = (unit_rows(hidden) * gain_ref[...] + shift_ref[...]).astype(BF)

    @pl.when(step >= first)
    def _():
        out_ref[...] = pick_places(row_ref, places, step - first, act_ref)


def after_attn(mixed, tokens, w, bias, gain, shift, target, places, block=512, place_block=640):
    n, width = tokens.shape
    first = n // block
    rows = pl.BlockSpec((block, width), lambda i: (jnp.minimum(i, first - 1), 0))
    line = pl.BlockSpec((1, width), lambda i: (0, 0))
    return pl.pallas_call(
        functools.partial(after_attn_kernel, first=first, block=block),
        grid=(first + places // place_block,),
        in_specs=[
            rows,
            rows,
            pl.BlockSpec((width, width), lambda i: (0, 0), pipeline_mode=pl.Buffered(1)),
            line,
            line,
            line,
            pl.BlockSpec((8, n), lambda i: (0, 0)),
        ],
        out_specs=(rows, pl.BlockSpec((place_block, width), lambda i: (jnp.maximum(i - first, 0), 0))),
        out_shape=(jax.ShapeDtypeStruct((n, width), F32), jax.ShapeDtypeStruct((places, width), BF)),
        scratch_shapes=[pltpu.VMEM((n, width), BF)],
        compiler_params=pltpu.CompilerParams(vmem_limit_bytes=40 << 20),
        cost_estimate=pl.CostEstimate(flops=4 * n * width * width, bytes_accessed=12 * n * width, transcendentals=0),
        name="after_attn",
    )(mixed, tokens, w, bias, gain, shift, target)


def after_experts_kernel(
    target_ref, home_ref, cot_ref, hidden_ref, gain_ref, w_out_ref, gh_ref, ga_ref, do_ref, sums_ref
):
    rows, width = cot_ref.shape
    places = home_ref.shape[0]
    pick = (lax.broadcasted_iota(jnp.int32, (rows, places), 1) == target_ref[...]).astype(BF)
    d = dot(pick, home_ref[...])
    hidden = hidden_ref[...]
    centred = hidden - jnp.mean(hidden, -1, keepdims=True)
    inv = lax.rsqrt(jnp.mean(centred * centred, -1, keepdims=True) + 1e-05)
    unit = centred * inv
    scaled = d * gain_ref[...]
    mean_one = jnp.mean(scaled, -1, keepdims=True)
    mean_two = jnp.mean(scaled * unit, -1, keepdims=True)
    grad = cot_ref[...].astype(F32) + inv * (scaled - mean_one - unit * mean_two)
    gh_ref[...] = grad
    low = grad.astype(BF)
    ga_ref[...] = low
    do_ref[...] = dot_nt(low, w_out_ref[...]).astype(BF)
    parts = [jnp.sum(low.astype(F32), 0, keepdims=True), jnp.sum(d * unit, 0, keepdims=True), jnp.sum(d, 0, keepdims=True)]
    parts = jnp.concatenate(parts + [jnp.zeros((8 - len(parts), width), F32)], 0)

    @pl.when(pl.program_id(0) == 0)
    def _():
        sums_ref[...] = parts

    @pl.when(pl.program_id(0) > 0)
    def _():
        sums_ref[...] += parts


def after_experts(target, home, cot, hidden, gain, w_out, block=256):
    n, width = cot.shape
    places = home.shape[0]
    rows = pl.BlockSpec((block, width), lambda i: (i, 0))
    once = pl.Buffered(1)
    return pl.pallas_call(
        after_experts_kernel,
        grid=(n // block,),
        in_specs=[
            pl.BlockSpec((block, 1), lambda i: (i, 0)),
            pl.BlockSpec((places, width), lambda i: (0, 0), pipeline_mode=once),
            rows,
            rows,
            pl.BlockSpec((1, width), lambda i: (0, 0)),
            pl.BlockSpec((width, width), lambda i: (0, 0), pipeline_mode=once),
        ],
        out_specs=(rows, rows, rows, pl.BlockSpec((8, width), lambda i: (0, 0))),
        out_shape=(
            jax.ShapeDtypeStruct((n, width), F32),
            jax.ShapeDtypeStruct((n, width), BF),
            jax.ShapeDtypeStruct((n, width), BF),
            jax.ShapeDtypeStruct((8, width), F32),
        ),
        compiler_params=pltpu.CompilerParams(vmem_limit_bytes=50 << 20),
        name="after_experts",
    )(target, home, cot, hidden, gain, w_out)


def backward_kernel(*refs, ep_bits, rep_bits, own, rblk, chunks, blk):
    len_ref, q_ref, k_ref, v_ref, o_ref, do_ref, lse_ref = refs[:7]
    act_ref, mixed_ref, ga_ref, wq_ref, wk_ref, wv_ref, tok_ref, gh_ref, gain_ref, sums_ref, bias_ref = refs[7:18]
    out_ref, da_ref, vec_out, bias_out = refs[18:22]
    at_ref, mt_ref, dq_ref, dk_ref, dv_ref, dqt_ref, dk_acc, dv_acc, x_ref = refs[22:31]
    bits = ep_bits + rep_bits
    got = refs[31 : 31 + bits]
    vec_got, vec_sum, bias_got, bias_sum, send, recv, vsend, vrecv, bsend, brecv = refs[31 + bits :]
    step = pl.program_id(0)
    n, width = act_ref.shape
    block = ga_ref.shape[1]
    lanes = q_ref.shape[1]
    ep, rep = 1 << ep_bits, 1 << rep_bits
    me_z = lax.axis_index("rep")
    me = lax.axis_index("ep")

    def bit(b):
        return lax.rem(me // (1 << b), 2) if b < ep_bits else lax.rem(me_z // (1 << (b - ep_bits)), 2)

    def flip(b):
        change = 1 - 2 * bit(b)
        return (me_z, me + change * (1 << b)) if b < ep_bits else (me_z + change * (1 << (b - ep_bits)), me)

    def order(c):
        rest = list(range(1, ep_bits))
        return [0] + (rest if c % 2 == 0 else rest[::-1]) + list(range(ep_bits, bits))

    def copy(src, dst, s, r, peer):
        return pltpu.make_async_remote_copy(
            src_ref=src, dst_ref=dst, send_sem=s, recv_sem=r, device_id=peer, device_id_type=pl.DeviceIdType.MESH
        )

    def cut(c, stage, value):
        done = order(c)[:stage]
        left = [b for b in range(ep_bits - 1, -1, -1) if b not in done]
        left += [b for b in range(bits - 1, ep_bits - 1, -1) if b not in done]
        index = [slice(None)] * len(left)
        index[left.index(order(c)[stage])] = value
        return tuple(index)

    def held(c, stage):
        return x_ref.at[c] if stage == 0 else got[stage - 1].at[c]

    def stage_copy(c, stage):
        b = order(c)[stage]
        return copy(
            held(c, stage).at[cut(c, stage, 1 - bit(b))], got[stage].at[c], send.at[c, stage], recv.at[c, stage], flip(b)
        )

    def advance(pair, stage):
        for c in (2 * pair, 2 * pair + 1):
            stage_copy(c, stage).wait()
            keep = held(c, stage)[cut(c, stage, bit(order(c)[stage]))]
            if stage + 1 < bits:
                got[stage][c] += keep
                stage_copy(c, stage + 1).start()
            else:
                out_ref[:, :, c * lanes : (c + 1) * lanes] = got[stage][c].astype(F32) + keep.astype(F32)

    def small_copy(k, got_ref, sum_ref, first, s, r):
        return copy(sum_ref.at[k - first], got_ref.at[k - first], s.at[k - first], r.at[k - first], flip(k))

    def vec_copy(k):
        return small_copy(k, vec_got, vec_sum, 0, vsend, vrecv)

    def bias_copy(k):
        return small_copy(k, bias_got, bias_sum, ep_bits, bsend, brecv)

    def vec_step(k):
        vec_copy(k).wait()
        vec_sum[k + 1] = vec_sum[k] + vec_got[k]
        if k + 1 < bits:
            vec_copy(k + 1).start()

    @pl.when(step == 0)
    def _():
        barrier = pltpu.get_barrier_semaphore()
        for b in range(bits):
            pl.semaphore_signal(barrier, inc=1, device_id=flip(b), device_id_type=pl.DeviceIdType.MESH)
        pl.semaphore_wait(barrier, bits)
        bias_sum[0] = bias_ref[...]
        bias_copy(ep_bits).start()
        at_ref[...] = act_ref[...].T
        mt_ref[...] = mixed_ref[...].T

    slot = lax.rem(step, 2)
    attn_bwd_kernel(
        len_ref, q_ref, k_ref, v_ref, o_ref, do_ref, lse_ref, dq_ref.at[slot], dk_ref.at[slot], dv_ref.at[slot],
        dqt_ref, dk_acc, dv_acc, blk=blk,
    )

    def put(c, w, left, right):
        g = dot(left[...], right).astype(BF)
        for r in range(rep):
            for e in range(ep):
                start = (r * ep + e) * own
                where = tuple((e >> b) & 1 for b in range(ep_bits - 1, -1, -1))
                where += tuple((r >> b) & 1 for b in range(rep_bits - 1, -1, -1))
                for k in range(2):
                    x_ref[(2 * c + k,) + where + (w,)] = g[start : start + own, k * lanes : (k + 1) * lanes]

    def norm_back():
        total_n = jnp.zeros((1, width), F32)
        total_d = jnp.zeros((1, width), F32)
        for s in range(0, n, rblk):
            rs = slice(s, s + rblk)
            d = da_ref[rs]
            hidden = tok_ref[rs].astype(F32)
            centred = hidden - jnp.mean(hidden, -1, keepdims=True)
            inv = lax.rsqrt(jnp.mean(centred * centred, -1, keepdims=True) + 1e-05)
            unit = centred * inv
            scaled = d * gain_ref[...]
            mean_one = jnp.mean(scaled, -1, keepdims=True)
            mean_two = jnp.mean(scaled * unit, -1, keepdims=True)
            da_ref[rs] = gh_ref[rs] + inv * (scaled - mean_one - unit * mean_two)
            total_n += jnp.sum(d * unit, 0, keepdims=True)
            total_d += jnp.sum(d, 0, keepdims=True)
        return total_n, total_d

    for c in range(chunks):

        @pl.when(step == 2 * c)
        def _(c=c):
            put(c, 3, mt_ref, ga_ref[...])
            for stage in range(0, ep_bits, 2):
                if c - 1 - stage // 2 >= 0:
                    advance(c - 1 - stage // 2, stage)

        @pl.when(step == 2 * c + 1)
        def _(c=c):
            dq = jnp.concatenate([dq_ref[0], dq_ref[1]], 1)
            dk = jnp.concatenate([dk_ref[0], dk_ref[1]], 1)
            dv = jnp.concatenate([dv_ref[0], dv_ref[1]], 1)
            put(c, 0, at_ref, dq)
            put(c, 1, at_ref, dk)
            put(c, 2, at_ref, dv)
            stage_copy(2 * c, 0).start()
            stage_copy(2 * c + 1, 0).start()
            for stage in range(1, ep_bits, 2):
                if c - 1 - stage // 2 >= 0:
                    advance(c - 1 - stage // 2, stage)
            cols = slice(c * block, (c + 1) * block)
            vec_sum[0, 2:3, cols] = jnp.sum(dq.astype(F32), 0, keepdims=True)
            vec_sum[0, 3:4, cols] = jnp.sum(dv.astype(F32), 0, keepdims=True)
            vec_sum[0, 4:8, cols] = sums_ref[0:4, cols]
            if c == chunks - 1:
                advance(c, 0)
            for s in range(0, n, rblk):
                rs = slice(s, s + rblk)
                part = dot_nt(dq[rs], wq_ref[...]) + dot_nt(dk[rs], wk_ref[...]) + dot_nt(dv[rs], wv_ref[...])
                if c == 0:
                    da_ref[rs] = part
                else:
                    da_ref[rs] += part
            if c == chunks - 1:
                total_n, total_d = norm_back()
                vec_sum[0, 0:1] = total_n
                vec_sum[0, 1:2] = total_d
                vec_copy(0).start()
                waves = {}
                for d in range(chunks):
                    for stage in range(ep_bits):
                        reached = 2 * (d + 1 + stage // 2) + stage % 2
                        if reached > 2 * c + 1 and (d, stage) != (c, 0):
                            waves.setdefault(d + stage, []).append((d, stage))
                k = 0
                for wave in sorted(waves):
                    for d, stage in reversed(waves[wave]):
                        advance(d, stage)
                    if k < ep_bits:
                        vec_step(k)
                        k += 1
                for k in range(k, ep_bits):
                    vec_step(k)
                for stage in range(ep_bits, bits):
                    k = stage - ep_bits
                    bias_copy(stage).wait()
                    bias_sum[k + 1] = bias_sum[k] + bias_got[k]
                    if k + 1 < rep_bits:
                        bias_copy(stage + 1).start()
                    for d in range(chunks):
                        advance(d, stage)
                    vec_step(stage)
                vec_out[...] = vec_sum[bits]
                bias_out[...] = bias_sum[rep_bits]


def backward(length, q, k, v, o, do, lse, act, ga, wq, wk, wv, tokens, gh, gain, sums, bias, rep, ep, rblk=256, blk=256):
    n, width = act.shape
    own = width // (rep * ep)
    ep_bits, rep_bits = ep.bit_length() - 1, rep.bit_length() - 1
    bits = ep_bits + rep_bits
    lanes = 128
    block = 2 * lanes
    chunks = width // block
    once = pl.Buffered(1)
    whole = pl.BlockSpec((n, width), lambda j: (0, 0), pipeline_mode=once)
    pair = pl.BlockSpec((n, lanes), lambda j: (0, j))
    cols = pl.BlockSpec((n, block), lambda j: (0, j // 2))
    eight = pl.BlockSpec((8, width), lambda j: (0, 0))
    scratch = [
        pltpu.VMEM((width, n), BF),
        pltpu.VMEM((width, n), BF),
        pltpu.VMEM((2, n, lanes), BF),
        pltpu.VMEM((2, n, lanes), BF),
        pltpu.VMEM((2, n, lanes), BF),
        pltpu.VMEM((lanes, n), F32),
        pltpu.VMEM((n, lanes), F32),
        pltpu.VMEM((n, lanes), F32),
        pltpu.VMEM((2 * chunks,) + (2,) * bits + (4, own, lanes), BF),
    ]
    scratch += [pltpu.VMEM((2 * chunks,) + (2,) * (bits - 1 - k) + (4, own, lanes), BF) for k in range(bits)]
    scratch += [
        pltpu.VMEM((bits, 8, width), F32),
        pltpu.VMEM((bits + 1, 8, width), F32),
        pltpu.VMEM((rep_bits, 8, width), F32),
        pltpu.VMEM((rep_bits + 1, 8, width), F32),
        pltpu.SemaphoreType.DMA((2 * chunks, bits)),
        pltpu.SemaphoreType.DMA((2 * chunks, bits)),
        pltpu.SemaphoreType.DMA((bits,)),
        pltpu.SemaphoreType.DMA((bits,)),
        pltpu.SemaphoreType.DMA((rep_bits,)),
        pltpu.SemaphoreType.DMA((rep_bits,)),
    ]
    return pl.pallas_call(
        functools.partial(
            backward_kernel, ep_bits=ep_bits, rep_bits=rep_bits, own=own, rblk=rblk, chunks=chunks, blk=blk
        ),
        grid=(2 * chunks,),
        in_specs=[pl.BlockSpec(memory_space=pltpu.SMEM)]
        + [pair] * 5
        + [pl.BlockSpec((1, 2, n), lambda j: (j, 0, 0)), whole, whole, cols, cols, cols, cols, whole, whole]
        + [pl.BlockSpec((1, width), lambda j: (0, 0)), eight, eight],
        out_specs=(pl.BlockSpec((4, own, width), lambda j: (0, 0, 0)), whole, eight, eight),
        out_shape=(
            jax.ShapeDtypeStruct((4, own, width), F32),
            jax.ShapeDtypeStruct((n, width), F32),
            jax.ShapeDtypeStruct((8, width), F32),
            jax.ShapeDtypeStruct((8, width), F32),
        ),
        scratch_shapes=scratch,
        compiler_params=pltpu.CompilerParams(vmem_limit_bytes=63 << 20, collective_id=1, has_side_effects=True),
        name="backward",
    )(length, q, k, v, o, do, lse, act, o, ga, wq, wk, wv, tokens, gh, gain, sums, bias)


def combine_kernel(target_ref, back_ref, hidden_ref, out_ref):
    rows, places = hidden_ref.shape[0], back_ref.shape[0]
    pick = (lax.broadcasted_iota(jnp.int32, (rows, places), 1) == target_ref[...]).astype(BF)
    out_ref[...] = (hidden_ref[...] + dot(pick, back_ref[...])).astype(BF)


def combine(target, back, hidden, block=256):
    n, width = hidden.shape
    rows = pl.BlockSpec((block, width), lambda i: (i, 0))
    return pl.pallas_call(
        combine_kernel,
        grid=(n // block,),
        in_specs=[
            pl.BlockSpec((block, 1), lambda i: (i, 0)),
            pl.BlockSpec(back.shape, lambda i: (0, 0), pipeline_mode=pl.Buffered(1)),
            rows,
        ],
        out_specs=rows,
        out_shape=jax.ShapeDtypeStruct((n, width), BF),
        compiler_params=pltpu.CompilerParams(vmem_limit_bytes=40 << 20),
        name="combine",
    )(target, back, hidden)


def settle_kernel(where_ref, grad_ref, small_ref, bias_ref, gt_ref, small_out, bias1_out, bias2_out):
    gt_ref[...] = grad_ref[...]

    @pl.when(pl.program_id(0) == 0)
    def _():
        shift, row = where_ref[1], where_ref[2]
        small_out[...] = pltpu.roll(small_ref[...], shift, 1)[:, : small_out.shape[1]]
        bias1_out[...] = bias_ref[pl.ds(row, 1), :]
        wide = bias2_out.shape[1]
        bias2_out[...] = bias_ref[4:5, pl.ds(pl.multiple_of(row * wide, wide), wide)]


def settle(where, grad, small, bias, own, steps=4):
    n, d = grad.shape
    block = pl.BlockSpec((n // steps, d), lambda i: (i, 0))

    def fixed(shape):
        return pl.BlockSpec(shape, lambda i: (0, 0))

    return pl.pallas_call(
        settle_kernel,
        grid=(steps,),
        in_specs=[pl.BlockSpec(memory_space=pltpu.SMEM), block, fixed((8, d)), fixed((8, d))],
        out_specs=(block, fixed((8, 128)), fixed((1, d)), fixed((1, own))),
        out_shape=(
            jax.ShapeDtypeStruct((n, d), F32),
            jax.ShapeDtypeStruct((8, 128), F32),
            jax.ShapeDtypeStruct((1, d), F32),
            jax.ShapeDtypeStruct((1, own), F32),
        ),
        compiler_params=pltpu.CompilerParams(vmem_limit_bytes=40 << 20),
        name="settle",
    )(where, grad, small, bias)


def unpack_kernel(where_ref, a1_ref, b1_ref, c1_ref, d1_ref, a2_ref, b2_ref, g1_ref, g2_ref, *, tile):
    per_row = a1_ref.shape[1] // tile
    h = where_ref[0]
    g2_ref[0] = a2_ref[...].astype(F32)
    g2_ref[1] = b2_ref[...].astype(F32)
    for refs, tile_of in (((a1_ref,), early_tile), ((b1_ref, c1_ref, d1_ref), late_tile)):
        for j in range(len(refs) * per_row):
            start = pl.multiple_of(tile_of(j, h) * tile, tile)
            c = tile * (j % per_row)
            g1_ref[:, pl.ds(start, tile)] = refs[j // per_row][:, c : c + tile].astype(F32)


def unpack_grads(where, a, b, tile, ff, rep, steps=4):
    d = a.shape[1]
    own = d // rep
    rows = own // steps
    base = tile // rows

    def line(k):
        return pl.BlockSpec((rows, d), lambda i: (base + k * steps + i, 0))

    second = pl.BlockSpec((tile // steps, d), lambda i: (i, 0))
    g1, g2 = pl.pallas_call(
        functools.partial(unpack_kernel, tile=tile),
        grid=(steps,),
        in_specs=[pl.BlockSpec(memory_space=pltpu.SMEM), line(0), line(0), line(1), line(2), second, second],
        out_specs=(
            pl.BlockSpec((rows, ff), lambda i: (i, 0)),
            pl.BlockSpec((2, tile // steps, d), lambda i: (0, i, 0)),
        ),
        out_shape=(jax.ShapeDtypeStruct((own, ff), F32), jax.ShapeDtypeStruct((2, tile, d), F32)),
        compiler_params=pltpu.CompilerParams(vmem_limit_bytes=60 << 20),
        name="unpack_grads",
    )(where, a, b, b, b, a, b)
    return g1, g2.reshape(2 * tile, d)


def per_device(
    tokens,
    cotangent,
    lengths,
    expert_ids,
    norm1_gain,
    norm1_bias,
    w_query,
    b_query,
    w_key,
    w_value,
    b_value,
    w_out,
    b_out,
    norm2_gain,
    norm2_bias,
    w_in,
    b_in,
    w_back,
    b_back,
):
    row_count, width = tokens.shape
    head_dim = width // HEADS
    ep = lax.axis_size("ep")
    rep = lax.axis_size("rep")
    slots = 5 * row_count // (4 * ep)
    places = ep * slots
    ff = w_in.shape[2]
    w_first = w_in[0]
    w_second = w_back[0]

    def exchange(rows):
        sent = lax.all_to_all(rows.reshape(ep, slots, width), "ep", 0, 0, tiled=True)
        return sent.reshape(places, width)

    at = lax.axis_index("rep")
    swap = [(i, i ^ 1) for i in range(rep)]
    target, target_row, grad_send, early, tail = dispatch(expert_ids, cotangent, ep, slots, 3)
    grad_rows = exchange(grad_send)
    early = lax.ppermute(early, "rep", swap)
    act_a, queries, keys, values = project(
        tokens, norm1_gain[None], norm1_bias[None], w_query, b_query[None], w_key, w_value, b_value[None], head_dim**-0.5
    )
    mixed, lse = attn_fwd(queries, keys, values, lengths)
    mixed, grad_rows, early, tail = lax.optimization_barrier((mixed, grad_rows, early, tail))
    late = lax.ppermute(tail, "rep", swap)
    hidden_one, rows_out = after_attn(
        mixed, tokens, w_out, b_out[None], norm2_gain[None], norm2_bias[None], target_row, places
    )
    rows_in = exchange(rows_out)
    rows_in, both = lax.optimization_barrier((rows_in, jnp.concatenate([early, late], 0)))
    grad_pair = exchange(both)
    rows_pair = lax.ppermute(rows_in, "rep", swap)
    own_fn = functools.partial(expert_own, tile=ff // 4)
    own_out = jax.eval_shape(own_fn, rows_in, grad_rows, w_first, b_in, w_second)
    own_all = lax.cond(
        lengths[0] > 0,
        own_fn,
        lambda *_: tuple(jnp.zeros(x.shape, x.dtype) for x in own_out),
        rows_in,
        grad_rows,
        w_first,
        b_in,
        w_second,
    )
    active, grad_inner, g_bias_first, grad_input, g_bias_second = own_all
    grad_home = exchange(grad_input)
    half = (at & 1).astype(jnp.int32)[None]
    turned = turn(half, rows_in, grad_rows, grad_pair, rep)
    active, grad_inner, g_bias_first, rows_pair, grad_pair, turned = lax.optimization_barrier(
        (active, grad_inner, g_bias_first, rows_pair, grad_pair, turned)
    )

    def pair(tile_of, steps):
        return expert_pair(
            half, turned, rows_pair, grad_pair, w_first, b_in, w_second, active, grad_inner, tile_of, steps, ff // 8, rep
        )

    groups = [[0, 2], [1, 3]]
    part_0 = pair(early_tile, 2)
    rows_pair, grad_home, active, part_0 = lax.optimization_barrier((rows_pair, grad_home, active, part_0))
    sum_0 = lax.psum_scatter(part_0, "rep", scatter_dimension=0, axis_index_groups=groups, tiled=True)
    result = (dot(active, w_second) + b_back[0]).astype(BF)
    rows_pair, result = lax.optimization_barrier((rows_pair, result))
    returned = exchange(result)
    part_1 = pair(late_tile, 6)
    returned, part_1 = lax.optimization_barrier((returned, part_1))
    sum_1 = lax.psum_scatter(part_1, "rep", scatter_dimension=0, axis_index_groups=groups, tiled=True)
    block_out = combine(target, returned, hidden_one)
    grad_home, block_out = lax.optimization_barrier((grad_home, block_out))

    def remainder(grad_home, g_bias_first, g_bias_second):
        grad_hidden, grad_attn, grad_mixed, sums = after_experts(
            target, grad_home, cotangent, hidden_one, norm2_gain[None], w_out
        )
        bias = jnp.concatenate([g_bias_first.reshape(ff // width, width), g_bias_second], 0)
        bias = jnp.pad(bias, ((0, 8 - bias.shape[0]), (0, 0)))
        return backward(
            lengths, queries, keys, values, mixed, grad_mixed, lse, act_a, grad_attn, w_query, w_key, w_value, tokens,
            grad_hidden, norm1_gain[None], sums, bias, rep, ep,
        )

    own = width // (rep * ep)
    own_ff, own_width = ff // rep, width // rep
    args = (grad_home, g_bias_first, g_bias_second)
    shapes = jax.eval_shape(remainder, *args)
    dense, grad_rows_in, small, grad_bias = lax.cond(
        lengths[0] > 0, remainder, lambda *_: jax.tree.map(lambda x: jnp.zeros(x.shape, x.dtype), shapes), *args
    )
    place = at * ep + lax.axis_index("ep")
    where = jnp.stack([at & 1, lax.rem(width - place * own, width), at]).astype(jnp.int32)
    grad_tokens, small, out_bias_first, out_bias_second = settle(where, grad_rows_in, small, grad_bias, width // rep)
    where, grad_tokens, small = lax.optimization_barrier((where, grad_tokens, small))
    out_first, out_second = unpack_grads(where, sum_0[0], sum_1[0], ff // 8, ff, rep)
    small = small[:, :own]
    out_first, out_second = out_first[None], out_second[None]
    return (
        block_out,
        grad_tokens,
        small[0],
        small[1],
        dense[0],
        small[2],
        dense[1],
        dense[2],
        small[3],
        dense[3],
        small[4],
        small[5],
        small[6],
        out_first,
        out_bias_first,
        out_second,
        out_bias_second,
    )


def solution(mesh):
    return jax.shard_map(
        per_device,
        mesh=mesh,
        in_specs=(
            P(("rep", "ep"), None),
            P(("rep", "ep"), None),
            P(("rep", "ep")),
            P(("rep", "ep"), None),
            P(),
            P(),
            P(),
            P(),
            P(),
            P(),
            P(),
            P(),
            P(),
            P(),
            P(),
            P("ep", None, None),
            P("ep", None),
            P("ep", None, None),
            P("ep", None),
        ),
        out_specs=(
            P(("rep", "ep"), None),
            P(("rep", "ep"), None),
            P(("rep", "ep")),
            P(("rep", "ep")),
            P(("rep", "ep"), None),
            P(("rep", "ep")),
            P(("rep", "ep"), None),
            P(("rep", "ep"), None),
            P(("rep", "ep")),
            P(("rep", "ep"), None),
            P(("rep", "ep")),
            P(("rep", "ep")),
            P(("rep", "ep")),
            P("ep", "rep", None),
            P("ep", "rep"),
            P("ep", "rep", None),
            P("ep", "rep"),
        ),
        check_vma=False,
    )
```
